256 devices in a mesh: dp: 16 (over z, core), fsdp: 16 (over y, x).
Axes of the slice: x: 4, y: 4, z: 8, core: 2. Of those that a mesh axis runs over, the one named last changes fastest.
Arguments:
- tokens: bfloat16 [65536, 8192], P(('dp', 'fsdp')), may hold values from -6 to 6
- cotangent: bfloat16 [65536, 1024], P(('dp', 'fsdp')), may hold values from -6 to 6
- value_weight: bfloat16 [8192, 1024], P('fsdp'), may hold values from -0.1875 to 0.1875
- adapter_down_weight: bfloat16 [64, 8192, 64], P('dp', 'fsdp'), may hold values from -0.0625 to 0.0625
- adapter_up_weight: bfloat16 [64, 64, 1024], P('dp', None, 'fsdp'), may hold values from -0.1875 to 0.1875
- segment_tenant: int32 [16, 8], replicated, may hold values from 0 to 63, as said below
- segment_lengths: int32 [16, 8], replicated, may hold values from 1 to 2048, 4096 in all within a row
- tenant_stored_row: int32 [64], replicated, may hold values from 0 to 63, as said below
Outputs:
- input_gradient: bfloat16 [65536, 8192], P(('dp', 'fsdp'))
- adapter_down_gradient: float32 [64, 8192, 64], P('dp', 'fsdp')
- adapter_up_gradient: float32 [64, 64, 1024], P('dp', None, 'fsdp')
The draws below stay inside these ranges and needn't reach their ends.
Inputs may be any that keep to these rules, and one draw needn't show every extreme that they name: `segment_tenant`: the 8 tenants of one bin are distinct, and the packer places them so that their stored rows tenant_stored_row[t] lie in 8 different blocks of 4 consecutive rows (no bin draws two tenants whose adapters one dp index owns). A permutation of the tenants: tenant t's adapters are row tenant_stored_row[t] of adapter_down_weight and adapter_up_weight.
All inputs are finite; a program needn't handle non-finite values.
Results may differ from the reference program's by a relative error of at most 0.018.
Values may be sent and summed in bfloat16 or wider, within the bound.
No kernel may reach another device: no remote copies, remote signals or barrier semaphores. Data moves between devices by JAX's collectives and lax.ppermute only.
A program may use at most 128 MiB of HBM per device.

```python
import math
import jax
import jax.numpy as jnp
import numpy as np
from jax import lax

MODEL_WIDTH = 8192
VALUE_WIDTH = 1024
ADAPTER_RANK = 64
TENANT_COUNT = 64
SEGMENT_COUNT = 8
TOK_DEV = 256
BIN = 4096
TOKENS = 65536
TEN_DEV = 4
N_DP = 16
N_FSDP = 16


def owner_order(owner_key):
    return jax.random.permutation(owner_key, N_DP)


def tenant_layout(key):
    rows_of = jax.random.permutation(key, TENANT_COUNT).astype(jnp.int32)
    tenant_of = jnp.argsort(rows_of).astype(jnp.int32)
    owner_keys = jax.random.split(jax.random.fold_in(key, 101), N_DP)
    owner_pick = jax.vmap(owner_order)(owner_keys)[:, :SEGMENT_COUNT].astype(jnp.int32)
    local_pick = jax.random.randint(jax.random.fold_in(key, 202), (N_DP, SEGMENT_COUNT), 0, TEN_DEV).astype(jnp.int32)
    return (rows_of, tenant_of[owner_pick * TEN_DEV + local_pick].astype(jnp.int32))


def draw_tenant_stored_row(key, part):
    rows_of, slot_rows = tenant_layout(key)
    return rows_of


def draw_segment_tenant(key, part):
    rows_of, slot_rows = tenant_layout(key)
    return slot_rows


def steps_of(rng, dims, cuts, least, largest):
    def one(axis_at, parts):
        heights = jax.random.uniform(jax.random.fold_in(jax.random.fold_in(rng, 6), axis_at), (parts,), jnp.float32, least / len(cuts), largest / len(cuts))
        return jnp.repeat(jnp.exp(heights), dims[axis_at] // parts).reshape((-1,) + (1,) * (len(dims) - axis_at - 1))

    gain = one(*cuts[0])
    for cut in cuts[1:]:
        gain = gain * one(*cut)
    return gain


def profile(count, total, limit, skew):
    portions = [(1 << 20) // math.isqrt(grade ** skew) + 1 for grade in range(2, count + 1)]
    surplus, counts = total - limit - (count - 1), [1] * (count - 1)
    while surplus > 0:
        candidates = [i for i in range(count - 1) if counts[i] < limit]
        mass, remaining = sum([portions[i] for i in candidates]), surplus
        for i in candidates:
            more = min(limit - counts[i], max(1, remaining * portions[i] // mass), surplus)
            counts[i] = counts[i] + more
            surplus = surplus - more
    return np.array([limit] + counts)


def uneven_parts(stream_key, amount, total, bound, skew):
    if amount == 2:
        one = jax.random.randint(stream_key, (), max(1, total - bound), min(bound, total - 1) + 1)
        return jnp.stack([one, total - one])
    tallies = jnp.asarray(profile(amount, total, bound, skew), jnp.int32)
    couples = (amount - 1) // 2
    giver, sink = tallies[1:1 + 2 * couples:2], tallies[2:2 + 2 * couples:2]
    margin = jnp.minimum(giver - 1, bound - sink)
    moved = jax.random.randint(jax.random.fold_in(stream_key, 1), (couples,), 0, 1 << 20) % (margin + 1)
    tallies = tallies.at[1:1 + 2 * couples:2].set(giver - moved).at[2:2 + 2 * couples:2].set(sink + moved)
    return tallies[jax.random.permutation(jax.random.fold_in(stream_key, 2), amount)]


def normal_values(key, shape, spread, most, cuts=(), kind=jnp.bfloat16):
    entries = spread * jax.random.normal(key, shape, jnp.float32)
    if cuts:
        entries = entries * steps_of(key, shape, cuts, -0.22, 0.18)
    return jnp.clip(entries, -most, most).astype(kind)


def setup_inputs(seed: int = 0) -> dict:
    arg_keys = jax.random.split(jax.random.key(seed), 9)
    tokens = normal_values(arg_keys[0], (TOKENS, MODEL_WIDTH), 1.0, 6.0, ((0, 256),))
    cotangent = normal_values(arg_keys[1], (TOKENS, VALUE_WIDTH), 1.0, 6.0, ((0, 256),))
    value_weight = normal_values(arg_keys[2], (MODEL_WIDTH, VALUE_WIDTH), VALUE_WIDTH ** -0.5, 0.1875, ((0, 16),))
    adapter_down_weight = normal_values(arg_keys[3], (TENANT_COUNT, MODEL_WIDTH, ADAPTER_RANK), MODEL_WIDTH ** -0.5, 0.0625, ((0, 16), (1, 16)))
    adapter_up_weight = normal_values(arg_keys[4], (TENANT_COUNT, ADAPTER_RANK, VALUE_WIDTH), VALUE_WIDTH ** -0.5, 0.1875, ((0, 16), (2, 16)))
    segment_tenant = draw_segment_tenant(jax.random.fold_in(arg_keys[8], 71), 0)
    segment_lengths = jax.vmap(lambda own: uneven_parts(own, SEGMENT_COUNT, BIN, BIN // 2, 2))(jax.random.split(arg_keys[6], N_DP)).reshape((N_DP, SEGMENT_COUNT)).astype(jnp.int32)
    tenant_stored_row = draw_tenant_stored_row(jax.random.fold_in(arg_keys[8], 71), 0)
    return {"tokens": tokens, "cotangent": cotangent, "value_weight": value_weight, "adapter_down_weight": adapter_down_weight, "adapter_up_weight": adapter_up_weight, "segment_tenant": segment_tenant, "segment_lengths": segment_lengths, "tenant_stored_row": tenant_stored_row}


ADAPTER_SCALE = 2.0


def reference(tokens, cotangent, value_weight, adapter_down_weight, adapter_up_weight, segment_tenant, segment_lengths, tenant_stored_row):
    highest_precision = lax.Precision.HIGHEST
    stored = tenant_stored_row[segment_tenant].astype(jnp.int32)
    seg_ends = jnp.cumsum(segment_lengths, axis=1).astype(jnp.int32)
    starts = seg_ends - segment_lengths
    positions = jnp.arange(BIN, dtype=jnp.int32)

    def one_bin(packed):
        bin_tokens, bin_output_grads, bin_token_rows, bin_starts, bin_ends = packed
        inside = (positions[:, None] >= bin_starts[None, :]) & (positions[:, None] < bin_ends[None, :])
        broadcast_row_mask = jnp.repeat(inside, ADAPTER_RANK, axis=1)
        flat_down_weight = jnp.transpose(jnp.take(adapter_down_weight, bin_token_rows, axis=0), (1, 0, 2)).reshape(MODEL_WIDTH, SEGMENT_COUNT * ADAPTER_RANK)
        flat_up_weight = jnp.take(adapter_up_weight, bin_token_rows, axis=0).reshape(SEGMENT_COUNT * ADAPTER_RANK, VALUE_WIDTH)
        zero_constant = jnp.zeros((), jnp.bfloat16)
        low_rank = jnp.where(broadcast_row_mask, jnp.dot(bin_tokens, flat_down_weight, preferred_element_type=jnp.float32).astype(jnp.bfloat16), zero_constant)
        rank_space_gradient = jnp.where(broadcast_row_mask, (ADAPTER_SCALE * jnp.dot(bin_output_grads, flat_up_weight.T, preferred_element_type=jnp.float32)).astype(jnp.bfloat16), zero_constant)
        grad_rows = jnp.dot(bin_output_grads, value_weight.T, preferred_element_type=jnp.float32)
        grad_rows = grad_rows + jnp.dot(rank_space_gradient, flat_down_weight.T, preferred_element_type=jnp.float32)
        token_blocks = bin_tokens.reshape(N_FSDP, TOK_DEV, MODEL_WIDTH).astype(jnp.float32)
        low_blocks = rank_space_gradient.reshape(N_FSDP, TOK_DEV, SEGMENT_COUNT * ADAPTER_RANK).astype(jnp.float32)
        part_down = jnp.einsum("ftd,ftk->fdk", token_blocks, low_blocks, precision=highest_precision).astype(jnp.bfloat16)
        sum_down = jnp.sum(part_down.astype(jnp.float32), axis=0).astype(jnp.bfloat16)
        rank_space_blocks = low_rank.reshape(N_FSDP, TOK_DEV, SEGMENT_COUNT * ADAPTER_RANK).astype(jnp.float32)
        output_grad_blocks = bin_output_grads.reshape(N_FSDP, TOK_DEV, VALUE_WIDTH).astype(jnp.float32)
        partial_up_gradient = (ADAPTER_SCALE * jnp.einsum("dri,drc->dic", rank_space_blocks, output_grad_blocks, precision=highest_precision)).astype(jnp.bfloat16)
        sum_up = jnp.sum(partial_up_gradient.astype(jnp.float32), axis=0).astype(jnp.bfloat16)
        return grad_rows.astype(jnp.bfloat16), sum_down, sum_up

    grad_bins, bin_down, bin_up = lax.map(one_bin, (tokens.reshape(N_DP, BIN, MODEL_WIDTH), cotangent.reshape(N_DP, BIN, VALUE_WIDTH), stored, starts, seg_ends))
    input_gradient = grad_bins.reshape(TOKENS, MODEL_WIDTH)
    segment_down_weight = jnp.transpose(bin_down.reshape(N_DP, MODEL_WIDTH, SEGMENT_COUNT, ADAPTER_RANK), (0, 2, 1, 3)).reshape(N_DP * SEGMENT_COUNT, MODEL_WIDTH * ADAPTER_RANK).astype(jnp.float32)
    segment_up_weight = bin_up.reshape(N_DP * SEGMENT_COUNT, ADAPTER_RANK * VALUE_WIDTH).astype(jnp.float32)
    segment_placement = (stored.reshape(-1)[:, None] == jnp.arange(TENANT_COUNT, dtype=jnp.int32)[None, :]).astype(jnp.float32)
    gradient_norm_value = BIN ** -0.5
    adapter_down_gradient = jnp.dot(segment_placement.T, segment_down_weight, precision=highest_precision).reshape(TENANT_COUNT, MODEL_WIDTH, ADAPTER_RANK) * gradient_norm_value
    adapter_up_gradient = jnp.dot(segment_placement.T, segment_up_weight, precision=highest_precision).reshape(TENANT_COUNT, ADAPTER_RANK, VALUE_WIDTH) * gradient_norm_value
    return input_gradient, adapter_down_gradient, adapter_up_gradient
```

```python
import functools

import jax
import jax.numpy as jnp
from jax import lax
from jax.experimental import pallas as pl
from jax.experimental.pallas import tpu as pltpu
from jax.sharding import PartitionSpec as P

ADAPTER_SCALE = 2.0
BF = jnp.bfloat16
F32 = jnp.float32
VMEM_BYTES = 40 * 1024 * 1024


def params():
    return pltpu.CompilerParams(vmem_limit_bytes=VMEM_BYTES)


def cost(flops, moved):
    return pl.CostEstimate(flops=flops, bytes_accessed=moved, transcendentals=0)


def inside_pair(meta, pair, first, shape, slots, rank):
    row = first + lax.broadcasted_iota(jnp.int32, shape, 0)
    low = lax.broadcasted_iota(jnp.int32, shape, 1) < rank
    begin = jnp.where(low, meta[2 + 2 * pair], meta[3 + 2 * pair])
    end = jnp.where(low, meta[2 + slots + 2 * pair], meta[3 + slots + 2 * pair])
    return (row >= begin) & (row < end)


def pack_kernel(tok, cot_t, out):
    rows = tok.shape[0]
    half = cot_t.shape[0] // 2
    out[0, :rows, :] = tok[...]
    out[0, rows:, :rows] = cot_t[:half, :]
    out[0, rows:, rows:] = cot_t[half:, :]


def pack(tokens, cot_t, n):
    rows, width = tokens.shape
    piece, v = width // n, cot_t.shape[0] // n
    extra = v * rows // piece
    return pl.pallas_call(
        pack_kernel,
        grid=(n,),
        in_specs=[
            pl.BlockSpec((rows, piece), lambda f: (0, f)),
            pl.BlockSpec((v, rows), lambda f: (f, 0)),
        ],
        out_specs=pl.BlockSpec((1, rows + extra, piece), lambda f: (f, 0, 0)),
        out_shape=jax.ShapeDtypeStruct((n, rows + extra, piece), BF),
        compiler_params=params(),
        cost_estimate=cost(0, 4 * rows * width),
        name="pack",
    )(tokens, cot_t)


def offer_kernel(slots, meta, down_t, up, out):
    piece, v = down_t.shape[2], up.shape[2]
    out[...] = jnp.zeros_like(out)
    for b in range(out.shape[0]):
        r = jnp.maximum(meta[2 + 3 * slots + b], 0)
        out[b, :, :piece] = down_t[r]
        out[b, :, piece:piece + v] = up[r]


def offer(meta, down_t, up, bins, slots):
    _, rank, piece = down_t.shape
    return pl.pallas_call(
        functools.partial(offer_kernel, slots),
        grid_spec=pltpu.PrefetchScalarGridSpec(
            num_scalar_prefetch=1,
            grid=(1,),
            in_specs=[
                pl.BlockSpec(down_t.shape, lambda i, m: (0, 0, 0)),
                pl.BlockSpec(up.shape, lambda i, m: (0, 0, 0)),
            ],
            out_specs=pl.BlockSpec((bins, rank, piece + 128), lambda i, m: (0, 0, 0)),
        ),
        out_shape=jax.ShapeDtypeStruct((bins, rank, piece + 128), BF),
        compiler_params=params(),
        cost_estimate=cost(0, 2 * bins * rank * piece),
        name="offer",
    )(meta, down_t, up)


def choose_kernel(slots, meta, got, down, up):
    rank, piece = got.shape[1], down.shape[1]
    for s in range(slots):
        block = got[meta[2 + 2 * slots + s]]
        down[s * rank:(s + 1) * rank, :] = block[:, :piece]
        up[s * rank:(s + 1) * rank, :] = block[:, piece:]


def choose(meta, got, slots):
    owners, rank, wide = got.shape
    piece = wide - 128
    return pl.pallas_call(
        functools.partial(choose_kernel, slots),
        grid_spec=pltpu.PrefetchScalarGridSpec(
            num_scalar_prefetch=1,
            grid=(1,),
            in_specs=[pl.BlockSpec(got.shape, lambda i, m: (0, 0, 0))],
            out_specs=[
                pl.BlockSpec((slots * rank, piece), lambda i, m: (0, 0)),
                pl.BlockSpec((slots * rank, 128), lambda i, m: (0, 0)),
            ],
        ),
        out_shape=[
            jax.ShapeDtypeStruct((slots * rank, piece), BF),
            jax.ShapeDtypeStruct((slots * rank, 128), BF),
        ],
        compiler_params=params(),
        cost_estimate=cost(0, 2 * owners * rank * wide),
        name="choose",
    )(meta, got)


def project_kernel(slots, rank, v, meta, part, down, up, out):
    rows = out.shape[1]
    first = pl.program_id(0) * rows
    tok = part[0, :rows, :]
    cot_t = jnp.concatenate([part[0, rows:, :rows], part[0, rows:, rows:]], axis=0)
    lr = lax.dot_general(tok, down[...], (((1,), (1,)), ((), ())), preferred_element_type=F32)
    lg = lax.dot_general(
        cot_t, up[:, :v], (((0,), (1,)), ((), ())), preferred_element_type=F32
    )
    shape = (rows, 2 * rank)
    lr_sum = jnp.zeros(shape, F32)
    lg_sum = jnp.zeros(shape, F32)
    for p in range(slots // 2):
        keep = inside_pair(meta, p, first, shape, slots, rank)
        cols = slice(2 * rank * p, 2 * rank * (p + 1))
        lr_sum += jnp.where(keep, lr[:, cols], 0.0)
        lg_sum += jnp.where(keep, lg[:, cols], 0.0)
    lr_sum += pltpu.roll(lr_sum, rank, 1)
    lg_sum += pltpu.roll(lg_sum, rank, 1)
    low = lax.broadcasted_iota(jnp.int32, shape, 1) < rank
    out[0] = jnp.where(low, lr_sum, ADAPTER_SCALE * lg_sum).astype(BF)


def project(meta, parts, down, up, rows, slots, rank, v):
    n, tall, piece = parts.shape
    return pl.pallas_call(
        functools.partial(project_kernel, slots, rank, v),
        grid_spec=pltpu.PrefetchScalarGridSpec(
            num_scalar_prefetch=1,
            grid=(n,),
            in_specs=[
                pl.BlockSpec((1, tall, piece), lambda j, m: (j, 0, 0)),
                pl.BlockSpec(down.shape, lambda j, m: (0, 0)),
                pl.BlockSpec(up.shape, lambda j, m: (0, 0)),
            ],
            out_specs=pl.BlockSpec((1, rows, 2 * rank), lambda j, m: (j, 0, 0)),
        ),
        out_shape=jax.ShapeDtypeStruct((n, rows, 2 * rank), BF),
        compiler_params=params(),
        cost_estimate=cost(2 * n * rows * (piece + v) * slots * rank, 2 * n * tall * piece),
        name="project",
    )(meta, parts, down, up)


def total_kernel(parts, out):
    acc = parts[0].astype(F32)
    for f in range(1, parts.shape[0]):
        acc += parts[f].astype(F32)
    acc = acc.astype(BF)
    for f in range(out.shape[0]):
        out[f] = acc


def total(parts):
    return pl.pallas_call(
        total_kernel,
        out_shape=jax.ShapeDtypeStruct(parts.shape, BF),
        compiler_params=params(),
        cost_estimate=cost(0, 4 * parts.size),
        name="total",
    )(parts)


def spread(meta, both, take_high, first, slots, rank):
    both = both.astype(F32)
    other = pltpu.roll(both, rank, 1)
    low = lax.broadcasted_iota(jnp.int32, both.shape, 1) < rank
    half = jnp.where(low != take_high, both, other)
    cols = [
        jnp.where(inside_pair(meta, p, first, both.shape, slots, rank), half, 0.0)
        for p in range(slots // 2)
    ]
    return jnp.concatenate(cols, axis=1).astype(BF)


def gradient_kernel(slots, rank, v, meta, part, low, out, acc_down, acc_up):
    rows = low.shape[1]
    step = pl.program_id(0)
    first = step * rows

    @pl.when(step == 0)
    def _():
        acc_down[...] = jnp.zeros_like(acc_down)
        acc_up[...] = jnp.zeros_like(acc_up)

    both = low[0]
    lr = spread(meta, both, False, first, slots, rank)
    lg = spread(meta, both, True, first, slots, rank)
    tok = part[0, :rows, :]
    cot_t = jnp.concatenate([part[0, rows:, :rows], part[0, rows:, rows:]], axis=0)
    acc_down[...] += lax.dot_general(
        lg, tok, (((0,), (0,)), ((), ())), preferred_element_type=F32
    )
    acc_up[...] += jnp.dot(cot_t, lr, preferred_element_type=F32)

    @pl.when(step == pl.num_programs(0) - 1)
    def _():
        piece = acc_down.shape[1]
        out[...] = jnp.zeros_like(out)
        up = jnp.transpose(ADAPTER_SCALE * acc_up[...]).astype(BF)
        for s in range(slots):
            at = meta[2 + 2 * slots + s]
            out[at, :, :piece] = acc_down[s * rank:(s + 1) * rank, :].astype(BF)
            out[at, :, piece:piece + v] = up[s * rank:(s + 1) * rank, :]


def gradient(meta, parts, low, owners, slots, rank, v):
    n, tall, piece = parts.shape
    rows = low.shape[1]
    return pl.pallas_call(
        functools.partial(gradient_kernel, slots, rank, v),
        grid_spec=pltpu.PrefetchScalarGridSpec(
            num_scalar_prefetch=1,
            grid=(n,),
            in_specs=[
                pl.BlockSpec((1, tall, piece), lambda j, m: (j, 0, 0)),
                pl.BlockSpec((1, rows, 2 * rank), lambda j, m: (j, 0, 0)),
            ],
            out_specs=pl.BlockSpec((owners, rank, piece + 128), lambda j, m: (0, 0, 0)),
            scratch_shapes=[
                pltpu.VMEM((slots * rank, piece), F32),
                pltpu.VMEM((v, slots * rank), F32),
            ],
        ),
        out_shape=jax.ShapeDtypeStruct((owners, rank, piece + 128), BF),
        compiler_params=params(),
        cost_estimate=cost(2 * n * rows * (piece + v) * slots * rank, 2 * n * tall * piece),
        name="gradient",
    )(meta, parts, low)


def collect_kernel(slots, scale, meta, got, down, up):
    piece, v = down.shape[2], up.shape[2]
    down[...] = jnp.zeros_like(down)
    up[...] = jnp.zeros_like(up)
    for b in range(got.shape[0]):
        r = meta[2 + 3 * slots + b]

        @pl.when(r >= 0)
        def _():
            down[r] += got[b, :, :piece].astype(F32)
            up[r] += got[b, :, piece:piece + v].astype(F32)

    down[...] = down[...] * scale
    up[...] = up[...] * scale


def collect(meta, got, rows, v, slots, scale):
    bins, rank, wide = got.shape
    piece = wide - 128
    return pl.pallas_call(
        functools.partial(collect_kernel, slots, scale),
        grid_spec=pltpu.PrefetchScalarGridSpec(
            num_scalar_prefetch=1,
            grid=(1,),
            in_specs=[pl.BlockSpec(got.shape, lambda i, m: (0, 0, 0))],
            out_specs=[
                pl.BlockSpec((rows, rank, piece), lambda i, m: (0, 0, 0)),
                pl.BlockSpec((rows, rank, v), lambda i, m: (0, 0, 0)),
            ],
        ),
        out_shape=[
            jax.ShapeDtypeStruct((rows, rank, piece), F32),
            jax.ShapeDtypeStruct((rows, rank, v), F32),
        ],
        compiler_params=params(),
        cost_estimate=cost(0, 2 * got.size),
        name="collect",
    )(meta, got)


def input_kernel(slots, rank, meta, cot, low, mine, other, down, out, lg):
    @pl.when(pl.program_id(0) == 0)
    def _():
        lg[...] = spread(meta, low[0], True, meta[1], slots, rank)

    nt = (((1,), (1,)), ((), ()))
    term = jnp.dot(lg[...], down[0], preferred_element_type=F32)
    a = lax.dot_general(cot[...], mine[0], nt, preferred_element_type=F32)
    b = lax.dot_general(cot[...], other[0], nt, preferred_element_type=F32)
    half = a.shape[1]
    lower = meta[0] == 0
    out[:, :half] = (jnp.where(lower, a, b) + term[:, :half]).astype(BF)
    out[:, half:] = (jnp.where(lower, b, a) + term[:, half:]).astype(BF)


def input_gradient(meta, cot, low, mine, other, down, slots, rank):
    n, half, width = mine.shape
    rows = cot.shape[0]
    piece = 2 * half
    return pl.pallas_call(
        functools.partial(input_kernel, slots, rank),
        grid_spec=pltpu.PrefetchScalarGridSpec(
            num_scalar_prefetch=1,
            grid=(n,),
            in_specs=[
                pl.BlockSpec(cot.shape, lambda f, m: (0, 0)),
                pl.BlockSpec((1, rows, 2 * rank), lambda f, m: (0, 0, 0)),
                pl.BlockSpec((1, half, width), lambda f, m: (f, 0, 0)),
                pl.BlockSpec((1, half, width), lambda f, m: (f, 0, 0)),
                pl.BlockSpec((1, slots * rank, piece), lambda f, m: (f, 0, 0)),
            ],
            out_specs=pl.BlockSpec((rows, piece), lambda f, m: (0, f)),
            scratch_shapes=[pltpu.VMEM((rows, slots * rank), BF)],
        ),
        out_shape=jax.ShapeDtypeStruct((rows, n * piece), BF),
        compiler_params=params(),
        cost_estimate=cost(
            2 * rows * n * piece * (width + slots * rank),
            2 * n * piece * (width + slots * rank + rows),
        ),
        name="input_gradient",
    )(meta, cot, low, mine, other, down)


def exchange(x, axis):
    return lax.all_to_all(x, axis, 0, 0, tiled=True)


def local(
    tokens,
    cotangent,
    value_weight,
    adapter_down_weight,
    adapter_up_weight,
    segment_tenant,
    segment_lengths,
    tenant_stored_row,
):
    own, piece, rank = adapter_down_weight.shape
    v = adapter_up_weight.shape[2]
    bins, slots = segment_tenant.shape
    rows = tokens.shape[0]
    n = lax.axis_size("fsdp")
    me_bin = lax.axis_index("dp")
    me_piece = lax.axis_index("fsdp")
    core = me_bin % 2
    scale = (n * rows) ** (-0.5)

    half = piece // 2
    half_weight = lax.dynamic_slice_in_dim(value_weight, core * half, half, 0)
    mine = lax.all_gather(half_weight, "fsdp", axis=0)
    other = lax.ppermute(mine, "dp", [(i, i ^ 1) for i in range(bins)])

    tenants = jnp.arange(tenant_stored_row.shape[0], dtype=jnp.int32)
    stored = jnp.sum(
        jnp.where(segment_tenant[:, :, None] == tenants, tenant_stored_row, 0), axis=2
    )
    my_stored = lax.dynamic_index_in_dim(stored, me_bin, 0, keepdims=False)
    lengths = lax.dynamic_index_in_dim(segment_lengths, me_bin, 0, keepdims=False)
    ends = jnp.cumsum(lengths)
    wanted = jnp.max(jnp.where(stored // own == me_bin, stored % own, -1), axis=1)
    meta = jnp.concatenate(
        [
            jnp.stack([core, me_piece * rows]),
            ends - lengths,
            ends,
            my_stored // own,
            wanted,
        ]
    ).astype(jnp.int32)

    got = exchange(
        offer(meta, jnp.swapaxes(adapter_down_weight, 1, 2), adapter_up_weight, bins, slots), "dp"
    )
    down, up = choose(meta, got, slots)
    down_all = lax.all_gather(down, "fsdp", axis=0)

    parts = exchange(pack(tokens, jnp.swapaxes(cotangent, 0, 1), n), "fsdp")
    low_own = total(exchange(project(meta, parts, down, up, rows, slots, rank, v), "fsdp"))
    low_all = exchange(low_own, "fsdp")
    sent = exchange(gradient(meta, parts, low_all, bins, slots, rank, v), "dp")
    down_grad, up_grad = collect(meta, sent, own, v, slots, scale)
    grad = input_gradient(meta, cotangent, low_own, mine, other, down_all, slots, rank)
    return grad, jnp.swapaxes(down_grad, 1, 2), up_grad


def solution(mesh):
    placed = (
        P(("dp", "fsdp"), None),
        P(("dp", "fsdp"), None),
        P("fsdp", None),
        P("dp", "fsdp", None),
        P("dp", None, "fsdp"),
        P(),
        P(),
        P(),
    )
    return jax.shard_map(
        local,
        mesh=mesh,
        in_specs=placed,
        out_specs=(P(("dp", "fsdp"), None), P("dp", "fsdp", None), P("dp", None, "fsdp")),
        check_vma=False,
    )
```

```python
import functools

import jax
import jax.numpy as jnp
from jax import lax
from jax.experimental import pallas as pl
from jax.experimental.pallas import tpu as pltpu
from jax.sharding import PartitionSpec as P

ADAPTER_SCALE = 2.0
BF = jnp.bfloat16
F32 = jnp.float32
VMEM_BYTES = 40 * 1024 * 1024
GROUP = 4
CORE, FIRST, CHIP, LIST = 0, 1, 2, 3


def call(kernel, name, flops=0, moved=0, **kw):
    return pl.pallas_call(
        kernel,
        compiler_params=pltpu.CompilerParams(vmem_limit_bytes=VMEM_BYTES),
        cost_estimate=pl.CostEstimate(flops=flops, bytes_accessed=moved, transcendentals=0),
        name=name,
        **kw,
    )


def whole(shape):
    return pl.BlockSpec(shape, lambda i, m: (0,) * len(shape))


def with_meta(grid, in_specs, out_specs, scratch=()):
    return pltpu.PrefetchScalarGridSpec(
        num_scalar_prefetch=1,
        grid=grid,
        in_specs=in_specs,
        out_specs=out_specs,
        scratch_shapes=list(scratch),
    )


def start_of(meta, s):
    return meta[LIST + s]


def end_of(meta, s, slots):
    return meta[LIST + slots + s]


def owner_of(meta, s, slots):
    return meta[LIST + 2 * slots + s]


def wanted_by(meta, b, slots):
    return meta[LIST + 3 * slots + b]


def segment_at(meta, owner, slots, bins):
    return meta[LIST + 3 * slots + bins + owner]


def inside_pair(meta, pair, first, shape, slots, rank):
    row = first + lax.broadcasted_iota(jnp.int32, shape, 0)
    low = lax.broadcasted_iota(jnp.int32, shape, 1) < rank
    begin = jnp.where(low, start_of(meta, 2 * pair), start_of(meta, 2 * pair + 1))
    end = jnp.where(low, end_of(meta, 2 * pair, slots), end_of(meta, 2 * pair + 1, slots))
    return (row >= begin) & (row < end)


def turn_kernel(meta, w, out):
    out[...] = jnp.transpose(w[...].astype(F32)).astype(BF)


def turn(meta, w):
    piece, width = w.shape
    half = piece // 2
    return call(
        turn_kernel,
        "turn",
        moved=4 * half * width,
        grid_spec=with_meta(
            (1,),
            [pl.BlockSpec((half, width), lambda i, m: (m[CORE], 0))],
            whole((width, half)),
        ),
        out_shape=jax.ShapeDtypeStruct((width, half), BF),
    )(meta, w)


def pack_kernel(tok, cot_t, out):
    rows = tok.shape[0]
    n, _, piece = out.shape
    v = cot_t.shape[0] // n
    for f in range(n):
        out[f, :rows, :] = tok[:, f * piece:(f + 1) * piece]
        out[f, rows:, :rows] = cot_t[f * v:f * v + v // 2, :]
        out[f, rows:, rows:] = cot_t[f * v + v // 2:(f + 1) * v, :]


def pack(tokens, cot_t, n):
    rows, width = tokens.shape
    piece, v = width // n, cot_t.shape[0] // n
    tall = rows + v * rows // piece
    return call(
        pack_kernel,
        "pack",
        moved=4 * rows * width,
        grid=(n // GROUP,),
        in_specs=[
            pl.BlockSpec((rows, GROUP * piece), lambda f: (0, f)),
            pl.BlockSpec((GROUP * v, rows), lambda f: (f, 0)),
        ],
        out_specs=pl.BlockSpec((GROUP, tall, piece), lambda f: (f, 0, 0)),
        out_shape=jax.ShapeDtypeStruct((n, tall, piece), BF),
    )(tokens, cot_t)


def offer_kernel(slots, meta, down_t, up, keep, give):
    piece, v = down_t.shape[2], up.shape[2]
    keep[...] = jnp.zeros_like(keep)
    give[...] = jnp.zeros_like(give)
    for z in range(keep.shape[0]):
        for out, core in ((keep, meta[CORE]), (give, 1 - meta[CORE])):
            r = jnp.maximum(wanted_by(meta, 2 * z + core, slots), 0)
            out[z, :, :piece] = down_t[r]
            out[z, :, piece:piece + v] = up[r]


def offer(meta, down_t, up, chips, slots):
    _, rank, piece = down_t.shape
    shape = (chips, rank, piece + 128)
    return call(
        functools.partial(offer_kernel, slots),
        "offer",
        moved=8 * chips * rank * piece,
        grid_spec=with_meta(
            (1,), [whole(down_t.shape), whole(up.shape)], [whole(shape), whole(shape)]
        ),
        out_shape=[jax.ShapeDtypeStruct(shape, BF)] * 2,
    )(meta, down_t, up)


def merge_kernel(meta, keep, taken, *outs):
    chips = len(outs)
    for k, out in enumerate(outs):
        z = lax.rem(meta[CHIP] + k, chips)
        out[meta[CORE]] = keep[z]
        out[1 - meta[CORE]] = taken[z]


def merge(meta, keep, taken):
    chips, rank, wide = keep.shape
    shape = (2, rank, wide)
    return call(
        merge_kernel,
        "merge",
        moved=4 * keep.size,
        grid_spec=with_meta(
            (1,), [whole(keep.shape), whole(taken.shape)], [whole(shape)] * chips
        ),
        out_shape=[jax.ShapeDtypeStruct(shape, BF)] * chips,
    )(meta, keep, taken)


def choose_kernel(slots, meta, *refs):
    chips = len(refs) - 3
    got, (down, turned, up) = refs[:chips], refs[chips:]
    piece, v, rank = down.shape[2], up.shape[0], down.shape[1]
    for k in range(chips):
        z = lax.rem(meta[CHIP] + chips - k, chips)
        for core in range(2):
            s = segment_at(meta, 2 * z + core, slots, 2 * chips)

            @pl.when(s >= 0)
            def _():
                down[s] = got[k][core]

    for p in range(slots // 2):
        pair = jnp.concatenate([down[2 * p], down[2 * p + 1]], axis=0).astype(F32)
        cols = slice(2 * rank * p, 2 * rank * (p + 1))
        turned[:, cols] = jnp.transpose(pair[:, :turned.shape[0]]).astype(BF)
        up[:, cols] = jnp.transpose(pair[:, turned.shape[0]:])[:v].astype(BF)


def choose(meta, got, slots, v):
    _, rank, wide = got[0].shape
    piece = wide - 128
    shapes = [(slots, rank, wide), (piece, slots * rank), (v, slots * rank)]
    return call(
        functools.partial(choose_kernel, slots),
        "choose",
        moved=4 * slots * rank * wide,
        grid_spec=with_meta((1,), [whole(g.shape) for g in got], [whole(s) for s in shapes]),
        out_shape=[jax.ShapeDtypeStruct(s, BF) for s in shapes],
    )(meta, *got)


def cot_of(part, rows):
    return jnp.concatenate([part[rows:, :rows], part[rows:, rows:]], axis=0)


def project_kernel(slots, rank, meta, part, down_t, up_t, out):
    group, rows, _ = out.shape
    shape = (rows, 2 * rank)
    low = lax.broadcasted_iota(jnp.int32, shape, 1) < rank
    for g in range(group):
        first = (pl.program_id(0) * group + g) * rows
        block = part[g]
        lr = jnp.dot(block[:rows], down_t[...], preferred_element_type=F32)
        lg = lax.dot_general(
            cot_of(block, rows), up_t[...], (((0,), (0,)), ((), ())), preferred_element_type=F32
        )
        lr_sum = jnp.zeros(shape, F32)
        lg_sum = jnp.zeros(shape, F32)
        for p in range(slots // 2):
            keep = inside_pair(meta, p, first, shape, slots, rank)
            cols = slice(2 * rank * p, 2 * rank * (p + 1))
            lr_sum += jnp.where(keep, lr[:, cols], 0.0)
            lg_sum += jnp.where(keep, lg[:, cols], 0.0)
        lr_sum += pltpu.roll(lr_sum, rank, 1)
        lg_sum += pltpu.roll(lg_sum, rank, 1)
        out[g] = jnp.where(low, lr_sum, ADAPTER_SCALE * lg_sum).astype(BF)


def project(meta, parts, down_t, up_t, rows, slots, rank):
    n, tall, piece = parts.shape
    return call(
        functools.partial(project_kernel, slots, rank),
        "project",
        flops=2 * n * rows * piece * slots * rank,
        moved=2 * n * tall * piece,
        grid_spec=with_meta(
            (n // GROUP,),
            [
                pl.BlockSpec((GROUP, tall, piece), lambda j, m: (j, 0, 0)),
                whole(down_t.shape),
                whole(up_t.shape),
            ],
            pl.BlockSpec((GROUP, rows, 2 * rank), lambda j, m: (j, 0, 0)),
        ),
        out_shape=jax.ShapeDtypeStruct((n, rows, 2 * rank), BF),
    )(meta, parts, down_t, up_t)


def total_kernel(parts, out, copies):
    acc = parts[0].astype(F32)
    for f in range(1, parts.shape[0]):
        acc += parts[f].astype(F32)
    out[...] = acc.astype(BF)
    turned = jnp.transpose(acc).astype(BF)
    for f in range(copies.shape[0]):
        copies[f] = turned


def total(parts):
    n, rows, wide = parts.shape
    return call(
        total_kernel,
        "total",
        moved=4 * parts.size,
        out_shape=[
            jax.ShapeDtypeStruct((rows, wide), BF),
            jax.ShapeDtypeStruct((n, wide, rows), BF),
        ],
    )(parts)


def gradient_kernel(slots, rank, v, meta, part, low, out, acc_down, acc_up):
    group, _, rows = low.shape
    step = pl.program_id(0)

    @pl.when(step == 0)
    def _():
        acc_down[...] = jnp.zeros_like(acc_down)
        acc_up[...] = jnp.zeros_like(acc_up)

    for g in range(group):
        first = (step * group + g) * rows
        for s in range(slots):
            start, end = start_of(meta, s), end_of(meta, s, slots)

            @pl.when((start < first + rows) & (end > first))
            def _():
                token = first + lax.broadcasted_iota(jnp.int32, (2 * rank, rows), 1)
                both = low[g].astype(F32)
                both = jnp.where((token >= start) & (token < end), both, 0.0).astype(BF)
                at = slice(s * rank, (s + 1) * rank)
                acc_down[at, :] += jnp.dot(
                    both[rank:], part[g, :rows, :], preferred_element_type=F32
                )
                acc_up[at, :] += lax.dot_general(
                    both[:rank],
                    cot_of(part[g], rows),
                    (((1,), (1,)), ((), ())),
                    preferred_element_type=F32,
                )

    @pl.when(step == pl.num_programs(0) - 1)
    def _():
        piece = acc_down.shape[1]
        out[...] = jnp.zeros_like(out)
        for s in range(slots):
            at = owner_of(meta, s, slots)
            rows_of = slice(s * rank, (s + 1) * rank)
            out[at, :, :piece] = acc_down[rows_of, :].astype(BF)
            out[at, :, piece:piece + v] = (ADAPTER_SCALE * acc_up[rows_of, :]).astype(BF)


def gradient(meta, parts, low, owners, slots, rank, v):
    n, tall, piece = parts.shape
    rows = low.shape[2]
    shape = (owners, rank, piece + 128)
    return call(
        functools.partial(gradient_kernel, slots, rank, v),
        "gradient",
        flops=2 * n * rows * piece * slots * rank,
        moved=2 * n * tall * piece,
        grid_spec=with_meta(
            (n // GROUP,),
            [
                pl.BlockSpec((GROUP, tall, piece), lambda j, m: (j, 0, 0)),
                pl.BlockSpec((GROUP, 2 * rank, rows), lambda j, m: (j, 0, 0)),
            ],
            whole(shape),
            [pltpu.VMEM((slots * rank, piece), F32), pltpu.VMEM((slots * rank, v), F32)],
        ),
        out_shape=jax.ShapeDtypeStruct(shape, BF),
    )(meta, parts, low)


def collect_kernel(slots, scale, meta, got, down, up):
    piece, v = down.shape[2], up.shape[2]
    down[...] = jnp.zeros_like(down)
    up[...] = jnp.zeros_like(up)
    for b in range(got.shape[0]):
        r = wanted_by(meta, b, slots)

        @pl.when(r >= 0)
        def _():
            down[r] += got[b, :, :piece].astype(F32) * scale
            up[r] += got[b, :, piece:piece + v].astype(F32) * scale


def collect(meta, got, rows, v, slots, scale):
    _, rank, wide = got.shape
    shapes = [(rows, rank, wide - 128), (rows, rank, v)]
    return call(
        functools.partial(collect_kernel, slots, scale),
        "collect",
        moved=2 * got.size,
        grid_spec=with_meta((1,), [whole(got.shape)], [whole(s) for s in shapes]),
        out_shape=[jax.ShapeDtypeStruct(s, F32) for s in shapes],
    )(meta, got)


def input_kernel(slots, rank, meta, cot, low, mine, other, down, out, lg):
    @pl.when(pl.program_id(0) == 0)
    def _():
        both = low[...].astype(F32)
        half = jnp.where(
            lax.broadcasted_iota(jnp.int32, both.shape, 1) < rank,
            pltpu.roll(both, rank, 1),
            both,
        )
        for p in range(slots // 2):
            keep = inside_pair(meta, p, meta[FIRST], both.shape, slots, rank)
            lg[:, 2 * rank * p:2 * rank * (p + 1)] = jnp.where(keep, half, 0.0).astype(BF)

    lower = meta[CORE] == 0
    group, _, half = mine.shape
    for g in range(group):
        at = 2 * g * half
        term = jnp.dot(lg[...], down[g], preferred_element_type=F32)
        a = jnp.dot(cot[...], mine[g], preferred_element_type=F32)
        b = jnp.dot(cot[...], other[g], preferred_element_type=F32)
        out[:, at:at + half] = (jnp.where(lower, a, b) + term[:, :half]).astype(BF)
        out[:, at + half:at + 2 * half] = (jnp.where(lower, b, a) + term[:, half:]).astype(BF)


def input_gradient(meta, cot, low, mine, other, down, slots, rank):
    n, width, half = mine.shape
    rows = cot.shape[0]
    piece = 2 * half
    group = 2
    return call(
        functools.partial(input_kernel, slots, rank),
        "input_gradient",
        flops=2 * rows * n * piece * (width + slots * rank),
        moved=2 * n * piece * (width + slots * rank + rows),
        grid_spec=with_meta(
            (n // group,),
            [
                whole(cot.shape),
                whole(low.shape),
                pl.BlockSpec((group, width, half), lambda f, m: (f, 0, 0)),
                pl.BlockSpec((group, width, half), lambda f, m: (f, 0, 0)),
                pl.BlockSpec((group, slots * rank, piece), lambda f, m: (f, 0, 0)),
            ],
            pl.BlockSpec((rows, group * piece), lambda f, m: (0, f)),
            [pltpu.VMEM((rows, slots * rank), BF)],
        ),
        out_shape=jax.ShapeDtypeStruct((rows, n * piece), BF),
    )(meta, cot, low, mine, other, down)


def exchange(x, axis):
    return lax.all_to_all(x, axis, 0, 0, tiled=True)


def swap(x, bins):
    return lax.ppermute(x, "dp", [(i, i ^ 1) for i in range(bins)])


def shift(x, k, bins):
    chips = bins // 2
    return lax.ppermute(
        x, "dp", [(i, (i // 2 + k) % chips * 2 + i % 2) for i in range(bins)]
    )


def scalars(segment_tenant, segment_lengths, tenant_stored_row, own, rows):
    bins, slots = segment_tenant.shape
    me = lax.axis_index("dp")
    tenants = jnp.arange(tenant_stored_row.shape[0], dtype=jnp.int32)
    stored = jnp.sum(
        jnp.where(segment_tenant[:, :, None] == tenants, tenant_stored_row, 0), axis=2
    )
    owners = lax.dynamic_index_in_dim(stored, me, 0, keepdims=False) // own
    lengths = lax.dynamic_index_in_dim(segment_lengths, me, 0, keepdims=False)
    place = jnp.arange(slots, dtype=jnp.int32)
    starts = jnp.sum(jnp.where(place[None, :] < place[:, None], lengths[None, :], 0), axis=1)
    wanted = jnp.max(jnp.where(stored // own == me, stored % own, -1), axis=1)
    every = jnp.arange(bins, dtype=jnp.int32)
    segment = jnp.max(jnp.where(owners[None, :] == every[:, None], place[None, :], -1), axis=1)
    head = jnp.stack([me % 2, lax.axis_index("fsdp") * rows, me // 2])
    return jnp.concatenate([head, starts, starts + lengths, owners, wanted, segment]).astype(
        jnp.int32
    )


def local(
    tokens,
    cotangent,
    value_weight,
    adapter_down_weight,
    adapter_up_weight,
    segment_tenant,
    segment_lengths,
    tenant_stored_row,
):
    own, piece, rank = adapter_down_weight.shape
    v = adapter_up_weight.shape[2]
    bins, slots = segment_tenant.shape
    chips = bins // 2
    rows = tokens.shape[0]
    n = lax.axis_size("fsdp")
    scale = (n * rows) ** (-0.5)
    meta = scalars(segment_tenant, segment_lengths, tenant_stored_row, own, rows)

    parts = exchange(pack(tokens, jnp.swapaxes(cotangent, 0, 1), n), "fsdp")
    mine = lax.all_gather(turn(meta, value_weight), "fsdp", axis=0)

    keep, give = offer(
        meta, jnp.swapaxes(adapter_down_weight, 1, 2), adapter_up_weight, chips, slots
    )
    blocks = merge(meta, keep, swap(give, bins))
    got = [blocks[0]] + [shift(blocks[k], k, bins) for k in range(1, chips)]
    parts, got = lax.optimization_barrier((parts, got))
    down, down_t, up_t = choose(meta, got, slots, v)
    down_all = lax.all_gather(
        down[:, :, :piece].reshape(slots * rank, piece), "fsdp", axis=0
    )

    low, copies = total(
        exchange(project(meta, parts, down_t, up_t, rows, slots, rank), "fsdp")
    )
    mine, copies = lax.optimization_barrier((mine, copies))
    other = swap(mine, bins)
    sent = exchange(
        gradient(meta, parts, exchange(copies, "fsdp"), bins, slots, rank, v), "dp"
    )
    grad = input_gradient(meta, cotangent, low, mine, other, down_all, slots, rank)
    sent, grad = lax.optimization_barrier((sent, grad))
    down_grad, up_grad = collect(meta, sent, own, v, slots, scale)
    return grad, jnp.swapaxes(down_grad, 1, 2), up_grad


def solution(mesh):
    placed = (
        P(("dp", "fsdp"), None),
        P(("dp", "fsdp"), None),
        P("fsdp", None),
        P("dp", "fsdp", None),
        P("dp", None, "fsdp"),
        P(),
        P(),
        P(),
    )
    return jax.shard_map(
        local,
        mesh=mesh,
        in_specs=placed,
        out_specs=(P(("dp", "fsdp"), None), P("dp", "fsdp", None), P("dp", None, "fsdp")),
        check_vma=False,
    )
```

```python
import functools

import jax
import jax.numpy as jnp
from jax import lax
from jax.experimental import pallas as pl
from jax.experimental.pallas import tpu as pltpu
from jax.sharding import PartitionSpec as P

ADAPTER_SCALE = 2.0
BF = jnp.bfloat16
F32 = jnp.float32
VMEM_BYTES = 40 * 1024 * 1024
GROUP = 4
CORE, FIRST, CHIP, LIST = 0, 1, 2, 3


def call(kernel, name, flops=0, moved=0, **kw):
    return pl.pallas_call(
        kernel,
        compiler_params=pltpu.CompilerParams(vmem_limit_bytes=VMEM_BYTES),
        cost_estimate=pl.CostEstimate(flops=flops, bytes_accessed=moved, transcendentals=0),
        name=name,
        **kw,
    )


def whole(shape):
    return pl.BlockSpec(shape, lambda i, m: (0,) * len(shape))


def with_meta(grid, in_specs, out_specs, scratch=()):
    return pltpu.PrefetchScalarGridSpec(
        num_scalar_prefetch=1,
        grid=grid,
        in_specs=in_specs,
        out_specs=out_specs,
        scratch_shapes=list(scratch),
    )


def start_of(meta, s):
    return meta[LIST + s]


def end_of(meta, s, slots):
    return meta[LIST + slots + s]


def owner_of(meta, s, slots):
    return meta[LIST + 2 * slots + s]


def wanted_by(meta, b, slots):
    return meta[LIST + 3 * slots + b]


def segment_at(meta, owner, slots, bins):
    return meta[LIST + 3 * slots + bins + owner]


def inside_pair(meta, pair, first, shape, slots, rank):
    row = first + lax.broadcasted_iota(jnp.int32, shape, 0)
    low = lax.broadcasted_iota(jnp.int32, shape, 1) < rank
    begin = jnp.where(low, start_of(meta, 2 * pair), start_of(meta, 2 * pair + 1))
    end = jnp.where(low, end_of(meta, 2 * pair, slots), end_of(meta, 2 * pair + 1, slots))
    return (row >= begin) & (row < end)


def turn_kernel(at, w, out):
    out[...] = jnp.transpose(w[...].astype(F32)).astype(BF)


def turn(at, w):
    piece, width = w.shape
    part = piece // 4
    return call(
        turn_kernel,
        "turn",
        moved=4 * part * width,
        grid_spec=with_meta(
            (1,),
            [pl.BlockSpec((part, width), lambda i, m: (m[0], 0))],
            whole((width, part)),
        ),
        out_shape=jax.ShapeDtypeStruct((width, part), BF),
    )(at, w)


def pack_kernel(tok, cot_t, out):
    rows = tok.shape[0]
    n, _, piece = out.shape
    v = cot_t.shape[0] // n
    for f in range(n):
        out[f, :rows, :] = tok[:, f * piece:(f + 1) * piece]
        out[f, rows:, :rows] = cot_t[f * v:f * v + v // 2, :]
        out[f, rows:, rows:] = cot_t[f * v + v // 2:(f + 1) * v, :]


def pack(tokens, cot_t, n):
    rows, width = tokens.shape
    piece, v = width // n, cot_t.shape[0] // n
    tall = rows + v * rows // piece
    return call(
        pack_kernel,
        "pack",
        moved=4 * rows * width,
        grid=(n // GROUP,),
        in_specs=[
            pl.BlockSpec((rows, GROUP * piece), lambda f: (0, f)),
            pl.BlockSpec((GROUP * v, rows), lambda f: (f, 0)),
        ],
        out_specs=pl.BlockSpec((GROUP, tall, piece), lambda f: (f, 0, 0)),
        out_shape=jax.ShapeDtypeStruct((n, tall, piece), BF),
    )(tokens, cot_t)


def offer_kernel(slots, meta, down_t, up, keep, give):
    piece, v = down_t.shape[2], up.shape[2]
    keep[...] = jnp.zeros_like(keep)
    give[...] = jnp.zeros_like(give)
    for z in range(keep.shape[0]):
        for out, core in ((keep, meta[CORE]), (give, 1 - meta[CORE])):
            r = jnp.maximum(wanted_by(meta, 2 * z + core, slots), 0)
            out[z, :, :piece] = down_t[r]
            out[z, :, piece:piece + v] = up[r]


def offer(meta, down_t, up, chips, slots):
    _, rank, piece = down_t.shape
    shape = (chips, rank, piece + 128)
    return call(
        functools.partial(offer_kernel, slots),
        "offer",
        moved=8 * chips * rank * piece,
        grid_spec=with_meta(
            (1,), [whole(down_t.shape), whole(up.shape)], [whole(shape), whole(shape)]
        ),
        out_shape=[jax.ShapeDtypeStruct(shape, BF)] * 2,
    )(meta, down_t, up)


def merge_kernel(meta, keep, taken, *outs):
    chips = len(outs)
    for k, out in enumerate(outs):
        z = lax.rem(meta[CHIP] + k, chips)
        out[meta[CORE]] = keep[z]
        out[1 - meta[CORE]] = taken[z]


def merge(meta, keep, taken):
    chips, rank, wide = keep.shape
    shape = (2, rank, wide)
    return call(
        merge_kernel,
        "merge",
        moved=4 * keep.size,
        grid_spec=with_meta(
            (1,), [whole(keep.shape), whole(taken.shape)], [whole(shape)] * chips
        ),
        out_shape=[jax.ShapeDtypeStruct(shape, BF)] * chips,
    )(meta, keep, taken)


def choose_kernel(slots, meta, *refs):
    chips = len(refs) - 3
    got, (down, turned, up) = refs[:chips], refs[chips:]
    piece, v, rank = down.shape[2], up.shape[0], down.shape[1]
    for k in range(chips):
        z = lax.rem(meta[CHIP] + chips - k, chips)
        for core in range(2):
            s = segment_at(meta, 2 * z + core, slots, 2 * chips)

            @pl.when(s >= 0)
            def _():
                down[s] = got[k][core]

    for p in range(slots // 2):
        pair = jnp.concatenate([down[2 * p], down[2 * p + 1]], axis=0).astype(F32)
        cols = slice(2 * rank * p, 2 * rank * (p + 1))
        turned[:, cols] = jnp.transpose(pair[:, :turned.shape[0]]).astype(BF)
        up[:, cols] = jnp.transpose(pair[:, turned.shape[0]:])[:v].astype(BF)


def choose(meta, got, slots, v):
    _, rank, wide = got[0].shape
    piece = wide - 128
    shapes = [(slots, rank, wide), (piece, slots * rank), (v, slots * rank)]
    return call(
        functools.partial(choose_kernel, slots),
        "choose",
        moved=4 * slots * rank * wide,
        grid_spec=with_meta((1,), [whole(g.shape) for g in got], [whole(s) for s in shapes]),
        out_shape=[jax.ShapeDtypeStruct(s, BF) for s in shapes],
    )(meta, *got)


def cot_of(part, rows):
    return jnp.concatenate([part[rows:, :rows], part[rows:, rows:]], axis=0)


def project_kernel(slots, rank, meta, part, down_t, up_t, out):
    group, rows, _ = out.shape
    shape = (rows, 2 * rank)
    low = lax.broadcasted_iota(jnp.int32, shape, 1) < rank
    for g in range(group):
        first = (pl.program_id(0) * group + g) * rows
        block = part[g]
        lr = jnp.dot(block[:rows], down_t[...], preferred_element_type=F32)
        lg = lax.dot_general(
            cot_of(block, rows), up_t[...], (((0,), (0,)), ((), ())), preferred_element_type=F32
        )
        lr_sum = jnp.zeros(shape, F32)
        lg_sum = jnp.zeros(shape, F32)
        for p in range(slots // 2):
            keep = inside_pair(meta, p, first, shape, slots, rank)
            cols = slice(2 * rank * p, 2 * rank * (p + 1))
            lr_sum += jnp.where(keep, lr[:, cols], 0.0)
            lg_sum += jnp.where(keep, lg[:, cols], 0.0)
        lr_sum += pltpu.roll(lr_sum, rank, 1)
        lg_sum += pltpu.roll(lg_sum, rank, 1)
        out[g] = jnp.where(low, lr_sum, ADAPTER_SCALE * lg_sum).astype(BF)


def project(meta, parts, down_t, up_t, rows, slots, rank):
    n, tall, piece = parts.shape
    return call(
        functools.partial(project_kernel, slots, rank),
        "project",
        flops=2 * n * rows * piece * slots * rank,
        moved=2 * n * tall * piece,
        grid_spec=with_meta(
            (n // GROUP,),
            [
                pl.BlockSpec((GROUP, tall, piece), lambda j, m: (j, 0, 0)),
                whole(down_t.shape),
                whole(up_t.shape),
            ],
            pl.BlockSpec((GROUP, rows, 2 * rank), lambda j, m: (j, 0, 0)),
        ),
        out_shape=jax.ShapeDtypeStruct((n, rows, 2 * rank), BF),
    )(meta, parts, down_t, up_t)


def total_kernel(parts, out, copies):
    acc = parts[0].astype(F32)
    for f in range(1, parts.shape[0]):
        acc += parts[f].astype(F32)
    out[...] = acc.astype(BF)
    turned = jnp.transpose(acc).astype(BF)
    for f in range(copies.shape[0]):
        copies[f] = turned


def total(parts):
    n, rows, wide = parts.shape
    return call(
        total_kernel,
        "total",
        moved=4 * parts.size,
        out_shape=[
            jax.ShapeDtypeStruct((rows, wide), BF),
            jax.ShapeDtypeStruct((n, wide, rows), BF),
        ],
    )(parts)


def gradient_kernel(slots, rank, v, meta, part, low, out, acc_down, acc_up):
    group, _, rows = low.shape
    step = pl.program_id(0)

    @pl.when(step == 0)
    def _():
        acc_down[...] = jnp.zeros_like(acc_down)
        acc_up[...] = jnp.zeros_like(acc_up)

    for g in range(group):
        first = (step * group + g) * rows
        for s in range(slots):
            start, end = start_of(meta, s), end_of(meta, s, slots)

            @pl.when((start < first + rows) & (end > first))
            def _():
                token = first + lax.broadcasted_iota(jnp.int32, (2 * rank, rows), 1)
                both = low[g].astype(F32)
                both = jnp.where((token >= start) & (token < end), both, 0.0).astype(BF)
                at = slice(s * rank, (s + 1) * rank)
                acc_down[at, :] += jnp.dot(
                    both[rank:], part[g, :rows, :], preferred_element_type=F32
                )
                acc_up[at, :] += lax.dot_general(
                    both[:rank],
                    cot_of(part[g], rows),
                    (((1,), (1,)), ((), ())),
                    preferred_element_type=F32,
                )

    @pl.when(step == pl.num_programs(0) - 1)
    def _():
        piece = acc_down.shape[1]
        out[...] = jnp.zeros_like(out)
        for s in range(slots):
            at = owner_of(meta, s, slots)
            rows_of = slice(s * rank, (s + 1) * rank)
            out[at, :, :piece] = acc_down[rows_of, :].astype(BF)
            out[at, :, piece:piece + v] = (ADAPTER_SCALE * acc_up[rows_of, :]).astype(BF)


def gradient(meta, parts, low, owners, slots, rank, v):
    n, tall, piece = parts.shape
    rows = low.shape[2]
    shape = (owners, rank, piece + 128)
    return call(
        functools.partial(gradient_kernel, slots, rank, v),
        "gradient",
        flops=2 * n * rows * piece * slots * rank,
        moved=2 * n * tall * piece,
        grid_spec=with_meta(
            (n // GROUP,),
            [
                pl.BlockSpec((GROUP, tall, piece), lambda j, m: (j, 0, 0)),
                pl.BlockSpec((GROUP, 2 * rank, rows), lambda j, m: (j, 0, 0)),
            ],
            whole(shape),
            [pltpu.VMEM((slots * rank, piece), F32), pltpu.VMEM((slots * rank, v), F32)],
        ),
        out_shape=jax.ShapeDtypeStruct(shape, BF),
    )(meta, parts, low)


def collect_kernel(slots, scale, meta, got, down, up):
    piece, v = down.shape[2], up.shape[2]
    down[...] = jnp.zeros_like(down)
    up[...] = jnp.zeros_like(up)
    for b in range(got.shape[0]):
        r = wanted_by(meta, b, slots)

        @pl.when(r >= 0)
        def _():
            down[r] += got[b, :, :piece].astype(F32) * scale
            up[r] += got[b, :, piece:piece + v].astype(F32) * scale


def collect(meta, got, rows, v, slots, scale):
    _, rank, wide = got.shape
    shapes = [(rows, rank, wide - 128), (rows, rank, v)]
    return call(
        functools.partial(collect_kernel, slots, scale),
        "collect",
        moved=2 * got.size,
        grid_spec=with_meta((1,), [whole(got.shape)], [whole(s) for s in shapes]),
        out_shape=[jax.ShapeDtypeStruct(s, F32) for s in shapes],
    )(meta, got)


def base_kernel(meta, cot, mine, near, mine_o, near_o, out):
    group, _, part = mine.shape
    even = lax.rem(meta[CHIP], 2) == 0
    lower = meta[CORE] == 0
    for g in range(group):
        w = jnp.concatenate([mine[g], near[g], mine_o[g], near_o[g]], axis=1)
        r = jnp.dot(cot[...], w, preferred_element_type=F32)
        r = [r[:, part * q:part * (q + 1)] for q in range(4)]
        r = [
            jnp.where(even, r[0], r[1]),
            jnp.where(even, r[1], r[0]),
            jnp.where(even, r[2], r[3]),
            jnp.where(even, r[3], r[2]),
        ]
        for q in range(4):
            at = (4 * g + q) * part
            out[:, at:at + part] = jnp.where(lower, r[q], r[(q + 2) % 4])


def base(meta, cot, mine, near, mine_o, near_o, upper):
    n, width, part = near.shape
    rows = cot.shape[0]
    group = 2
    skip = n // group if upper else 0
    spec = pl.BlockSpec((group, width, part), lambda f, m: (f, 0, 0))
    offset = pl.BlockSpec((group, width, part), lambda f, m: (f + skip, 0, 0))
    return call(
        base_kernel,
        "base",
        flops=8 * rows * n * part * width,
        moved=8 * n * part * width + 16 * rows * n * part,
        grid_spec=with_meta(
            (n // group,),
            [whole(cot.shape), offset, spec, offset, spec],
            pl.BlockSpec((rows, 4 * group * part), lambda f, m: (0, f)),
        ),
        out_shape=jax.ShapeDtypeStruct((rows, 4 * n * part), F32),
    )(meta, cot, mine, near, mine_o, near_o)


def input_kernel(slots, rank, meta, low, base_a, base_b, down, out, lg):
    @pl.when(pl.program_id(0) == 0)
    def _():
        both = low[...].astype(F32)
        half = jnp.where(
            lax.broadcasted_iota(jnp.int32, both.shape, 1) < rank,
            pltpu.roll(both, rank, 1),
            both,
        )
        for p in range(slots // 2):
            keep = inside_pair(meta, p, meta[FIRST], both.shape, slots, rank)
            lg[:, 2 * rank * p:2 * rank * (p + 1)] = jnp.where(keep, half, 0.0).astype(BF)

    group, _, piece = down.shape
    first = pl.program_id(0) < pl.num_programs(0) // 2
    for g in range(group):
        cols = slice(g * piece, (g + 1) * piece)
        term = jnp.dot(lg[...], down[g], preferred_element_type=F32)
        out[:, cols] = (term + jnp.where(first, base_a[:, cols], base_b[:, cols])).astype(BF)


def input_gradient(meta, low, base_a, base_b, down, slots, rank):
    n, _, piece = down.shape
    rows = base_a.shape[0]
    group = 2
    steps = n // group
    return call(
        functools.partial(input_kernel, slots, rank),
        "input_gradient",
        flops=2 * rows * n * piece * slots * rank,
        moved=2 * n * piece * (slots * rank + 3 * rows),
        grid_spec=with_meta(
            (steps,),
            [
                whole(low.shape),
                pl.BlockSpec(
                    (rows, group * piece), lambda f, m: (0, jnp.minimum(f, steps // 2 - 1))
                ),
                pl.BlockSpec(
                    (rows, group * piece), lambda f, m: (0, jnp.maximum(f - steps // 2, 0))
                ),
                pl.BlockSpec((group, slots * rank, piece), lambda f, m: (f, 0, 0)),
            ],
            pl.BlockSpec((rows, group * piece), lambda f, m: (0, f)),
            [pltpu.VMEM((rows, slots * rank), BF)],
        ),
        out_shape=jax.ShapeDtypeStruct((rows, n * piece), BF),
    )(meta, low, base_a, base_b, down)


def exchange(x, axis):
    return lax.all_to_all(x, axis, 0, 0, tiled=True)


def swap(x, bins):
    return lax.ppermute(x, "dp", [(i, i ^ 1) for i in range(bins)])


def shift(x, k, bins):
    chips = bins // 2
    return lax.ppermute(
        x, "dp", [(i, (i // 2 + k) % chips * 2 + i % 2) for i in range(bins)]
    )


def scalars(segment_tenant, segment_lengths, tenant_stored_row, own, rows):
    bins, slots = segment_tenant.shape
    me = lax.axis_index("dp")
    tenants = jnp.arange(tenant_stored_row.shape[0], dtype=jnp.int32)
    stored = jnp.sum(
        jnp.where(segment_tenant[:, :, None] == tenants, tenant_stored_row, 0), axis=2
    )
    owners = lax.dynamic_index_in_dim(stored, me, 0, keepdims=False) // own
    lengths = lax.dynamic_index_in_dim(segment_lengths, me, 0, keepdims=False)
    place = jnp.arange(slots, dtype=jnp.int32)
    starts = jnp.sum(jnp.where(place[None, :] < place[:, None], lengths[None, :], 0), axis=1)
    wanted = jnp.max(jnp.where(stored // own == me, stored % own, -1), axis=1)
    every = jnp.arange(bins, dtype=jnp.int32)
    segment = jnp.max(jnp.where(owners[None, :] == every[:, None], place[None, :], -1), axis=1)
    head = jnp.stack([me % 2, lax.axis_index("fsdp") * rows, me // 2])
    return jnp.concatenate([head, starts, starts + lengths, owners, wanted, segment]).astype(
        jnp.int32
    )


def local(
    tokens,
    cotangent,
    value_weight,
    adapter_down_weight,
    adapter_up_weight,
    segment_tenant,
    segment_lengths,
    tenant_stored_row,
):
    own, piece, rank = adapter_down_weight.shape
    v = adapter_up_weight.shape[2]
    bins, slots = segment_tenant.shape
    chips = bins // 2
    rows = tokens.shape[0]
    n = lax.axis_size("fsdp")
    scale = (n * rows) ** (-0.5)
    meta = scalars(segment_tenant, segment_lengths, tenant_stored_row, own, rows)

    me = lax.axis_index("dp")
    quarter = 2 * (me % 2) + me // 2 % 2
    mine = lax.all_gather(
        turn(quarter.astype(jnp.int32).reshape(1), value_weight), "fsdp", axis=0
    )
    parts = exchange(pack(tokens, jnp.swapaxes(cotangent, 0, 1), n), "fsdp")

    keep, give = offer(
        meta, jnp.swapaxes(adapter_down_weight, 1, 2), adapter_up_weight, chips, slots
    )
    blocks = merge(meta, keep, swap(give, bins))
    got = [blocks[0]] + [shift(blocks[k], k, bins) for k in range(1, chips)]
    parts, got, mine = lax.optimization_barrier((parts, got, mine))
    down, down_t, up_t = choose(meta, got, slots, v)
    down_all = lax.all_gather(
        down[:, :, :piece].reshape(slots * rank, piece), "fsdp", axis=0
    )

    sums = exchange(project(meta, parts, down_t, up_t, rows, slots, rank), "fsdp")
    near_a = shift(mine[:n // 2], chips - 1, bins)
    near_b = shift(mine[n // 2:], 1, bins)
    mine_o = swap(mine, bins)
    sums, near_a, near_b, mine_o = lax.optimization_barrier((sums, near_a, near_b, mine_o))
    low, copies = total(sums)
    low_all = exchange(copies, "fsdp")
    near_ao, near_bo = swap(near_a, bins), swap(near_b, bins)
    low_all, near_ao, near_bo = lax.optimization_barrier((low_all, near_ao, near_bo))
    sent = exchange(gradient(meta, parts, low_all, bins, slots, rank, v), "dp")
    base_a = base(meta, cotangent, mine, near_a, mine_o, near_ao, False)
    base_b = base(meta, cotangent, mine, near_b, mine_o, near_bo, True)
    grad = input_gradient(meta, low, base_a, base_b, down_all, slots, rank)
    sent, grad = lax.optimization_barrier((sent, grad))
    down_grad, up_grad = collect(meta, sent, own, v, slots, scale)
    return grad, jnp.swapaxes(down_grad, 1, 2), up_grad


def solution(mesh):
    placed = (
        P(("dp", "fsdp"), None),
        P(("dp", "fsdp"), None),
        P("fsdp", None),
        P("dp", "fsdp", None),
        P("dp", None, "fsdp"),
        P(),
        P(),
        P(),
    )
    return jax.shard_map(
        local,
        mesh=mesh,
        in_specs=placed,
        out_specs=(P(("dp", "fsdp"), None), P("dp", "fsdp", None), P("dp", None, "fsdp")),
        check_vma=False,
    )
```

```python
import functools

import jax
import jax.numpy as jnp
from jax import lax
from jax.experimental import pallas as pl
from jax.experimental.pallas import tpu as pltpu
from jax.sharding import PartitionSpec as P

ADAPTER_SCALE = 2.0
BF = jnp.bfloat16
F32 = jnp.float32
VMEM_BYTES = 40 * 1024 * 1024
VMEM_MOST = 58 * 1024 * 1024
WINDOW = 4
GROUP = 4
CORE, FIRST, CHIP, LIST = 0, 1, 2, 3


def call(kernel, name, flops=0, moved=0, vmem=VMEM_BYTES, **kw):
    return pl.pallas_call(
        kernel,
        compiler_params=pltpu.CompilerParams(vmem_limit_bytes=vmem),
        cost_estimate=pl.CostEstimate(flops=flops, bytes_accessed=moved, transcendentals=0),
        name=name,
        **kw,
    )


def whole(shape):
    return pl.BlockSpec(shape, lambda i, m: (0,) * len(shape))


def with_meta(grid, in_specs, out_specs, scratch=()):
    return pltpu.PrefetchScalarGridSpec(
        num_scalar_prefetch=1,
        grid=grid,
        in_specs=in_specs,
        out_specs=out_specs,
        scratch_shapes=list(scratch),
    )


def start_of(meta, s):
    return meta[LIST + s]


def end_of(meta, s, slots):
    return meta[LIST + slots + s]


def owner_of(meta, s, slots):
    return meta[LIST + 2 * slots + s]


def wanted_by(meta, b, slots):
    return meta[LIST + 3 * slots + b]


def segment_at(meta, owner, slots, bins):
    return meta[LIST + 3 * slots + bins + owner]


def inside_pair(meta, pair, first, shape, slots, rank):
    row = first + lax.broadcasted_iota(jnp.int32, shape, 0)
    low = lax.broadcasted_iota(jnp.int32, shape, 1) < rank
    begin = jnp.where(low, start_of(meta, 2 * pair), start_of(meta, 2 * pair + 1))
    end = jnp.where(low, end_of(meta, 2 * pair, slots), end_of(meta, 2 * pair + 1, slots))
    return (row >= begin) & (row < end)


def turn_kernel(at, w, out):
    out[...] = jnp.transpose(w[...].astype(F32)).astype(BF)


def turn(at, w, slices):
    piece, width = w.shape
    part = width // slices
    return call(
        turn_kernel,
        "turn",
        moved=4 * part * piece,
        grid_spec=with_meta(
            (1,),
            [pl.BlockSpec((piece, part), lambda i, m: (0, m[0]))],
            whole((part, piece)),
        ),
        out_shape=jax.ShapeDtypeStruct((part, piece), BF),
    )(at, w)


def pack_kernel(tok, cot_t, out):
    rows = tok.shape[0]
    n, _, piece = out.shape
    v = cot_t.shape[0] // n
    for f in range(n):
        out[f, :rows, :] = tok[:, f * piece:(f + 1) * piece]
        out[f, rows:, :rows] = cot_t[f * v:f * v + v // 2, :]
        out[f, rows:, rows:] = cot_t[f * v + v // 2:(f + 1) * v, :]


def pack(tokens, cot_t, n):
    rows, width = tokens.shape
    piece, v = width // n, cot_t.shape[0] // n
    tall = rows + v * rows // piece
    return call(
        pack_kernel,
        "pack",
        moved=4 * rows * width,
        vmem=VMEM_MOST,
        grid=(n // GROUP,),
        in_specs=[
            pl.BlockSpec((rows, GROUP * piece), lambda f: (0, f)),
            pl.BlockSpec((GROUP * v, rows), lambda f: (f, 0)),
        ],
        out_specs=pl.BlockSpec((GROUP, tall, piece), lambda f: (f, 0, 0)),
        out_shape=jax.ShapeDtypeStruct((n, tall, piece), BF),
    )(tokens, cot_t)


def offer_kernel(slots, meta, down_t, up, keep, give):
    piece, v = down_t.shape[2], up.shape[2]
    keep[...] = jnp.zeros_like(keep)
    give[...] = jnp.zeros_like(give)
    for z in range(keep.shape[0]):
        for out, core in ((keep, meta[CORE]), (give, 1 - meta[CORE])):
            r = jnp.maximum(wanted_by(meta, 2 * z + core, slots), 0)
            out[z, :, :piece] = down_t[r]
            out[z, :, piece:piece + v] = up[r]


def offer(meta, down_t, up, chips, slots):
    _, rank, piece = down_t.shape
    shape = (chips, rank, piece + 128)
    return call(
        functools.partial(offer_kernel, slots),
        "offer",
        moved=8 * chips * rank * piece,
        grid_spec=with_meta(
            (1,), [whole(down_t.shape), whole(up.shape)], [whole(shape), whole(shape)]
        ),
        out_shape=[jax.ShapeDtypeStruct(shape, BF)] * 2,
    )(meta, down_t, up)


def merge_kernel(meta, keep, taken, *outs):
    chips = len(outs)
    for k, out in enumerate(outs):
        z = lax.rem(meta[CHIP] + k, chips)
        out[meta[CORE]] = keep[z]
        out[1 - meta[CORE]] = taken[z]


def merge(meta, keep, taken):
    chips, rank, wide = keep.shape
    shape = (2, rank, wide)
    return call(
        merge_kernel,
        "merge",
        moved=4 * keep.size,
        grid_spec=with_meta(
            (1,), [whole(keep.shape), whole(taken.shape)], [whole(shape)] * chips
        ),
        out_shape=[jax.ShapeDtypeStruct(shape, BF)] * chips,
    )(meta, keep, taken)


def choose_kernel(slots, meta, *refs):
    chips = len(refs) - 3
    got, (down, turned, up) = refs[:chips], refs[chips:]
    piece, v, rank = down.shape[2], up.shape[0], down.shape[1]
    for k in range(chips):
        z = lax.rem(meta[CHIP] + chips - k, chips)
        for core in range(2):
            s = segment_at(meta, 2 * z + core, slots, 2 * chips)

            @pl.when(s >= 0)
            def _():
                down[s] = got[k][core]

    for p in range(slots // 2):
        pair = jnp.concatenate([down[2 * p], down[2 * p + 1]], axis=0).astype(F32)
        cols = slice(2 * rank * p, 2 * rank * (p + 1))
        turned[:, cols] = jnp.transpose(pair[:, :turned.shape[0]]).astype(BF)
        up[:, cols] = jnp.transpose(pair[:, turned.shape[0]:])[:v].astype(BF)


def choose(meta, got, slots, v):
    _, rank, wide = got[0].shape
    piece = wide - 128
    shapes = [(slots, rank, wide), (piece, slots * rank), (v, slots * rank)]
    return call(
        functools.partial(choose_kernel, slots),
        "choose",
        moved=4 * slots * rank * wide,
        grid_spec=with_meta((1,), [whole(g.shape) for g in got], [whole(s) for s in shapes]),
        out_shape=[jax.ShapeDtypeStruct(s, BF) for s in shapes],
    )(meta, *got)


def cot_of(part, rows):
    return jnp.concatenate([part[rows:, :rows], part[rows:, rows:]], axis=0)


def project_kernel(slots, rank, meta, part, down_t, up_t, out):
    group, rows, _ = out.shape
    shape = (rows, 2 * rank)
    low = lax.broadcasted_iota(jnp.int32, shape, 1) < rank
    for g in range(group):
        first = (pl.program_id(0) * group + g) * rows
        block = part[g]
        lr = jnp.dot(block[:rows], down_t[...], preferred_element_type=F32)
        lg = lax.dot_general(
            cot_of(block, rows), up_t[...], (((0,), (0,)), ((), ())), preferred_element_type=F32
        )
        lr_sum = jnp.zeros(shape, F32)
        lg_sum = jnp.zeros(shape, F32)
        for p in range(slots // 2):
            keep = inside_pair(meta, p, first, shape, slots, rank)
            cols = slice(2 * rank * p, 2 * rank * (p + 1))
            lr_sum += jnp.where(keep, lr[:, cols], 0.0)
            lg_sum += jnp.where(keep, lg[:, cols], 0.0)
        lr_sum += pltpu.roll(lr_sum, rank, 1)
        lg_sum += pltpu.roll(lg_sum, rank, 1)
        out[g] = jnp.where(low, lr_sum, ADAPTER_SCALE * lg_sum).astype(BF)


def project(meta, parts, down_t, up_t, rows, slots, rank):
    n, tall, piece = parts.shape
    return call(
        functools.partial(project_kernel, slots, rank),
        "project",
        flops=2 * n * rows * piece * slots * rank,
        moved=2 * n * tall * piece,
        grid_spec=with_meta(
            (n // GROUP,),
            [
                pl.BlockSpec((GROUP, tall, piece), lambda j, m: (j, 0, 0)),
                whole(down_t.shape),
                whole(up_t.shape),
            ],
            pl.BlockSpec((GROUP, rows, 2 * rank), lambda j, m: (j, 0, 0)),
        ),
        out_shape=jax.ShapeDtypeStruct((n, rows, 2 * rank), BF),
    )(meta, parts, down_t, up_t)


def total_kernel(parts, out, copies):
    acc = parts[0].astype(F32)
    for f in range(1, parts.shape[0]):
        acc += parts[f].astype(F32)
    out[...] = acc.astype(BF)
    turned = jnp.transpose(acc).astype(BF)
    for f in range(copies.shape[0]):
        copies[f] = turned


def total(parts):
    n, rows, wide = parts.shape
    return call(
        total_kernel,
        "total",
        moved=4 * parts.size,
        out_shape=[
            jax.ShapeDtypeStruct((rows, wide), BF),
            jax.ShapeDtypeStruct((n, wide, rows), BF),
        ],
    )(parts)


def gradient_kernel(slots, rank, v, meta, part, low, out, acc_down, acc_up):
    group, _, rows = low.shape
    step = pl.program_id(0)

    @pl.when(step == 0)
    def _():
        acc_down[...] = jnp.zeros_like(acc_down)
        acc_up[...] = jnp.zeros_like(acc_up)

    for g in range(group):
        first = (step * group + g) * rows
        for s in range(slots):
            start, end = start_of(meta, s), end_of(meta, s, slots)

            @pl.when((start < first + rows) & (end > first))
            def _():
                token = first + lax.broadcasted_iota(jnp.int32, (2 * rank, rows), 1)
                both = low[g].astype(F32)
                both = jnp.where((token >= start) & (token < end), both, 0.0).astype(BF)
                at = slice(s * rank, (s + 1) * rank)
                acc_down[at, :] += jnp.dot(
                    both[rank:], part[g, :rows, :], preferred_element_type=F32
                )
                acc_up[at, :] += lax.dot_general(
                    both[:rank],
                    cot_of(part[g], rows),
                    (((1,), (1,)), ((), ())),
                    preferred_element_type=F32,
                )

    @pl.when(step == pl.num_programs(0) - 1)
    def _():
        piece = acc_down.shape[1]
        out[...] = jnp.zeros_like(out)
        for s in range(slots):
            at = owner_of(meta, s, slots)
            rows_of = slice(s * rank, (s + 1) * rank)
            out[at, :, :piece] = acc_down[rows_of, :].astype(BF)
            out[at, :, piece:piece + v] = (ADAPTER_SCALE * acc_up[rows_of, :]).astype(BF)


def gradient(meta, parts, low, owners, slots, rank, v):
    n, tall, piece = parts.shape
    rows = low.shape[2]
    shape = (owners, rank, piece + 128)
    return call(
        functools.partial(gradient_kernel, slots, rank, v),
        "gradient",
        flops=2 * n * rows * piece * slots * rank,
        moved=2 * n * tall * piece,
        grid_spec=with_meta(
            (n // GROUP,),
            [
                pl.BlockSpec((GROUP, tall, piece), lambda j, m: (j, 0, 0)),
                pl.BlockSpec((GROUP, 2 * rank, rows), lambda j, m: (j, 0, 0)),
            ],
            whole(shape),
            [pltpu.VMEM((slots * rank, piece), F32), pltpu.VMEM((slots * rank, v), F32)],
        ),
        out_shape=jax.ShapeDtypeStruct(shape, BF),
    )(meta, parts, low)


def collect_kernel(slots, scale, meta, got, down, up):
    piece, v = down.shape[2], up.shape[2]
    down[...] = jnp.zeros_like(down)
    up[...] = jnp.zeros_like(up)
    for b in range(got.shape[0]):
        r = wanted_by(meta, b, slots)

        @pl.when(r >= 0)
        def _():
            down[r] += got[b, :, :piece].astype(F32) * scale
            up[r] += got[b, :, piece:piece + v].astype(F32) * scale


def collect(meta, got, rows, v, slots, scale):
    _, rank, wide = got.shape
    shapes = [(rows, rank, wide - 128), (rows, rank, v)]
    return call(
        functools.partial(collect_kernel, slots, scale),
        "collect",
        moved=2 * got.size,
        grid_spec=with_meta((1,), [whole(got.shape)], [whole(s) for s in shapes]),
        out_shape=[jax.ShapeDtypeStruct(s, F32) for s in shapes],
    )(meta, got)


def slice_columns(cot, meta, step, core, part):
    chip = lax.rem(meta[CHIP] + step + WINDOW, WINDOW)
    at = pl.multiple_of((2 * chip + core) * part, part)
    return cot[:, pl.ds(at, part)]


def base_kernel(steps, meta, cot, *refs):
    slices, (out, lhs) = refs[:-2], refs[-2:]
    group, part, piece = slices[0].shape

    @pl.when(pl.program_id(0) == 0)
    def _():
        for k, step in enumerate(steps):
            for j in range(2):
                core = meta[CORE] if j == 0 else 1 - meta[CORE]
                at = (2 * k + j) * part
                lhs[:, at:at + part] = slice_columns(cot, meta, step, core, part)

    for g in range(group):
        w = jnp.concatenate([x[g] for x in slices], axis=0)
        out[:, g * piece:(g + 1) * piece] = jnp.dot(
            lhs[...], w, preferred_element_type=F32
        )


def base(meta, cot, steps, slices):
    n, part, piece = slices[0].shape
    rows = cot.shape[0]
    group = 2
    return call(
        functools.partial(base_kernel, steps),
        "base",
        flops=2 * rows * n * part * piece * len(slices),
        moved=2 * n * part * piece * len(slices) + 4 * rows * n * piece,
        vmem=VMEM_MOST,
        grid_spec=with_meta(
            (n // group,),
            [whole(cot.shape)]
            + [pl.BlockSpec((group, part, piece), lambda f, m: (f, 0, 0))] * len(slices),
            pl.BlockSpec((rows, group * piece), lambda f, m: (0, f)),
            [pltpu.VMEM((rows, part * len(slices)), BF)],
        ),
        out_shape=jax.ShapeDtypeStruct((rows, n * piece), F32),
    )(meta, cot, *slices)


def input_kernel(slots, rank, meta, low, cot, done, table, *refs):
    far, (out, lhs) = refs[:-2], refs[-2:]
    group, part, piece = far[0].shape
    quarters = len(far) // 2
    each = pl.num_programs(0) // quarters

    @pl.when(pl.program_id(0) == 0)
    def _():
        lhs[:, :part] = slice_columns(cot, meta, WINDOW // 2, meta[CORE], part)
        lhs[:, part:2 * part] = slice_columns(cot, meta, WINDOW // 2, 1 - meta[CORE], part)
        both = low[...].astype(F32)
        half = jnp.where(
            lax.broadcasted_iota(jnp.int32, both.shape, 1) < rank,
            pltpu.roll(both, rank, 1),
            both,
        )
        for p in range(slots // 2):
            keep = inside_pair(meta, p, meta[FIRST], both.shape, slots, rank)
            at = 2 * part + 2 * rank * p
            lhs[:, at:at + 2 * rank] = jnp.where(keep, half, 0.0).astype(BF)

    def add(mine, other):
        for g in range(group):
            cols = slice(g * piece, (g + 1) * piece)
            w = jnp.concatenate([mine[g], other[g], table[g]], axis=0)
            term = jnp.dot(lhs[...], w, preferred_element_type=F32)
            out[:, cols] = (done[:, cols] + term).astype(BF)

    for q in range(quarters):
        pl.when(pl.program_id(0) // each == q)(
            functools.partial(add, far[q], far[quarters + q])
        )


def input_gradient(meta, low, cot, done, table, far, far_o, slots, rank):
    n, _, piece = table.shape
    part = far[0].shape[1]
    rows = cot.shape[0]
    group = 2
    steps = n // group
    each = steps // len(far)

    def quarter(q):
        return pl.BlockSpec(
            (group, part, piece),
            lambda f, m: (jnp.clip(f - q * each, 0, each - 1), 0, 0),
        )

    return call(
        functools.partial(input_kernel, slots, rank),
        "input_gradient",
        flops=2 * rows * n * piece * (slots * rank + 2 * part),
        moved=2 * n * piece * (slots * rank + 2 * part + 3 * rows),
        vmem=VMEM_MOST,
        grid_spec=with_meta(
            (steps,),
            [
                whole(low.shape),
                whole(cot.shape),
                pl.BlockSpec((rows, group * piece), lambda f, m: (0, f)),
                pl.BlockSpec((group, slots * rank, piece), lambda f, m: (f, 0, 0)),
            ]
            + [quarter(q) for q in range(len(far))] * 2,
            pl.BlockSpec((rows, group * piece), lambda f, m: (0, f)),
            [pltpu.VMEM((rows, slots * rank + 2 * part), BF)],
        ),
        out_shape=jax.ShapeDtypeStruct((rows, n * piece), BF),
    )(meta, low, cot, done, table, *far, *far_o)


def exchange(x, axis):
    return lax.all_to_all(x, axis, 0, 0, tiled=True)


def swap(x, bins):
    return lax.ppermute(x, "dp", [(i, i ^ 1) for i in range(bins)])


def shift(x, k, bins):
    chips = bins // 2
    return lax.ppermute(
        x, "dp", [(i, (i // 2 + k) % chips * 2 + i % 2) for i in range(bins)]
    )


def scalars(segment_tenant, segment_lengths, tenant_stored_row, own, rows):
    bins, slots = segment_tenant.shape
    me = lax.axis_index("dp")
    tenants = jnp.arange(tenant_stored_row.shape[0], dtype=jnp.int32)
    stored = jnp.sum(
        jnp.where(segment_tenant[:, :, None] == tenants, tenant_stored_row, 0), axis=2
    )
    owners = lax.dynamic_index_in_dim(stored, me, 0, keepdims=False) // own
    lengths = lax.dynamic_index_in_dim(segment_lengths, me, 0, keepdims=False)
    place = jnp.arange(slots, dtype=jnp.int32)
    starts = jnp.sum(jnp.where(place[None, :] < place[:, None], lengths[None, :], 0), axis=1)
    wanted = jnp.max(jnp.where(stored // own == me, stored % own, -1), axis=1)
    every = jnp.arange(bins, dtype=jnp.int32)
    segment = jnp.max(jnp.where(owners[None, :] == every[:, None], place[None, :], -1), axis=1)
    head = jnp.stack([me % 2, lax.axis_index("fsdp") * rows, me // 2])
    return jnp.concatenate([head, starts, starts + lengths, owners, wanted, segment]).astype(
        jnp.int32
    )


def local(
    tokens,
    cotangent,
    value_weight,
    adapter_down_weight,
    adapter_up_weight,
    segment_tenant,
    segment_lengths,
    tenant_stored_row,
):
    own, piece, rank = adapter_down_weight.shape
    v = adapter_up_weight.shape[2]
    bins, slots = segment_tenant.shape
    chips = bins // 2
    rows = tokens.shape[0]
    n = lax.axis_size("fsdp")
    scale = (n * rows) ** (-0.5)
    meta = scalars(segment_tenant, segment_lengths, tenant_stored_row, own, rows)

    me = lax.axis_index("dp")
    at = 2 * (me // 2 % WINDOW) + me % 2
    mine = lax.all_gather(
        turn(at.astype(jnp.int32).reshape(1), value_weight, 2 * WINDOW), "fsdp", axis=0
    )
    parts = exchange(pack(tokens, jnp.swapaxes(cotangent, 0, 1), n), "fsdp")

    keep, give = offer(
        meta, jnp.swapaxes(adapter_down_weight, 1, 2), adapter_up_weight, chips, slots
    )
    blocks = merge(meta, keep, swap(give, bins))
    got = [blocks[0]] + [shift(blocks[k], k, bins) for k in range(1, chips)]
    parts, got, mine = lax.optimization_barrier((parts, got, mine))
    down, down_t, up_t = choose(meta, got, slots, v)
    table = lax.all_gather(down[:, :, :piece].reshape(slots * rank, piece), "fsdp", axis=0)

    above, below = shift(mine, chips - 1, bins), shift(mine, 1, bins)
    sums = exchange(project(meta, parts, down_t, up_t, rows, slots, rank), "fsdp")
    sums, above, below = lax.optimization_barrier((sums, above, below))
    low, copies = total(sums)
    part = n // 4
    far = [
        shift(mine[q * part:(q + 1) * part], chips - 2 if q < 2 else 2, bins) for q in range(4)
    ]
    mine_o, above_o, below_o = swap(mine, bins), swap(above, bins), swap(below, bins)
    low_all = exchange(copies, "fsdp")
    low_all, mine_o, above_o, below_o, far[0], far[2] = lax.optimization_barrier(
        (low_all, mine_o, above_o, below_o, far[0], far[2])
    )
    due = gradient(meta, parts, low_all, bins, slots, rank, v)
    sent = exchange(due, "dp")
    done = base(
        meta, cotangent, (0, 1, -1), [mine, mine_o, above, above_o, below, below_o]
    )
    far[1], far[3], _ = lax.optimization_barrier((far[1], far[3], due))
    far_o = [swap(x, bins) for x in far]
    grad = input_gradient(meta, low, cotangent, done, table, far, far_o, slots, rank)
    sent, grad = lax.optimization_barrier((sent, grad))
    down_grad, up_grad = collect(meta, sent, own, v, slots, scale)
    return grad, jnp.swapaxes(down_grad, 1, 2), up_grad


def solution(mesh):
    placed = (
        P(("dp", "fsdp"), None),
        P(("dp", "fsdp"), None),
        P("fsdp", None),
        P("dp", "fsdp", None),
        P("dp", None, "fsdp"),
        P(),
        P(),
        P(),
    )
    return jax.shard_map(
        local,
        mesh=mesh,
        in_specs=placed,
        out_specs=(P(("dp", "fsdp"), None), P("dp", "fsdp", None), P("dp", None, "fsdp")),
        check_vma=False,
    )
```

```python
import functools

import jax
import jax.numpy as jnp
from jax import lax
from jax.experimental import pallas as pl
from jax.experimental.pallas import tpu as pltpu
from jax.sharding import PartitionSpec as P

ADAPTER_SCALE = 2.0
BF = jnp.bfloat16
F32 = jnp.float32
VMEM_BYTES = 40 * 1024 * 1024
VMEM_MOST = 58 * 1024 * 1024
GROUP = 4
SIDE = 4
CORE, FIRST, CHIP, PIECE, LIST = 0, 1, 2, 3, 4


def call(kernel, name, flops=0, moved=0, vmem=VMEM_BYTES, **kw):
    return pl.pallas_call(
        kernel,
        compiler_params=pltpu.CompilerParams(vmem_limit_bytes=vmem),
        cost_estimate=pl.CostEstimate(flops=flops, bytes_accessed=moved, transcendentals=0),
        name=name,
        **kw,
    )


def whole(shape):
    return pl.BlockSpec(shape, lambda i, m: (0,) * len(shape))


def with_meta(grid, in_specs, out_specs, scratch=()):
    return pltpu.PrefetchScalarGridSpec(
        num_scalar_prefetch=1,
        grid=grid,
        in_specs=in_specs,
        out_specs=out_specs,
        scratch_shapes=list(scratch),
    )


def start_of(meta, s):
    return meta[LIST + s]


def end_of(meta, s, slots):
    return meta[LIST + slots + s]


def owner_of(meta, s, slots):
    return meta[LIST + 2 * slots + s]


def wanted_by(meta, b, slots):
    return meta[LIST + 3 * slots + b]


def segment_at(meta, owner, slots, bins):
    return meta[LIST + 3 * slots + bins + owner]


def inside_pair(meta, pair, first, shape, slots, rank):
    row = first + lax.broadcasted_iota(jnp.int32, shape, 0)
    low = lax.broadcasted_iota(jnp.int32, shape, 1) < rank
    begin = jnp.where(low, start_of(meta, 2 * pair), start_of(meta, 2 * pair + 1))
    end = jnp.where(low, end_of(meta, 2 * pair, slots), end_of(meta, 2 * pair + 1, slots))
    return (row >= begin) & (row < end)


def turn_kernel(at, w, out):
    both = jnp.transpose(w[...].astype(F32)).astype(BF)
    part = out.shape[0]
    low = lax.rem(at[0], 2) == 0
    out[...] = jnp.where(low, both[:part], both[part:])


def turn(at, w, slices):
    piece, width = w.shape
    part = width // slices
    return call(
        turn_kernel,
        "turn",
        moved=4 * part * piece,
        grid_spec=with_meta(
            (1,),
            [pl.BlockSpec((piece, 2 * part), lambda i, m: (0, m[0] // 2))],
            whole((part, piece)),
        ),
        out_shape=jax.ShapeDtypeStruct((part, piece), BF),
    )(at, w)


def pack_kernel(tok, cot_t, out):
    rows = tok.shape[0]
    n, _, piece = out.shape
    v = cot_t.shape[0] // n
    for f in range(n):
        out[f, :rows, :] = tok[:, f * piece:(f + 1) * piece]
        out[f, rows:, :rows] = cot_t[f * v:f * v + v // 2, :]
        out[f, rows:, rows:] = cot_t[f * v + v // 2:(f + 1) * v, :]


def pack(tokens, cot_t, n):
    rows, width = tokens.shape
    piece, v = width // n, cot_t.shape[0] // n
    tall = rows + v * rows // piece
    return call(
        pack_kernel,
        "pack",
        moved=4 * rows * width,
        vmem=VMEM_MOST,
        grid=(n // GROUP,),
        in_specs=[
            pl.BlockSpec((rows, GROUP * piece), lambda f: (0, f)),
            pl.BlockSpec((GROUP * v, rows), lambda f: (f, 0)),
        ],
        out_specs=pl.BlockSpec((GROUP, tall, piece), lambda f: (f, 0, 0)),
        out_shape=jax.ShapeDtypeStruct((n, tall, piece), BF),
    )(tokens, cot_t)


def offer_kernel(slots, meta, down_t, up, keep, give):
    piece, v = down_t.shape[2], up.shape[2]
    keep[...] = jnp.zeros_like(keep)
    give[...] = jnp.zeros_like(give)
    for z in range(keep.shape[0]):
        for out, core in ((keep, meta[CORE]), (give, 1 - meta[CORE])):
            r = jnp.maximum(wanted_by(meta, 2 * z + core, slots), 0)
            out[z, :, :piece] = down_t[r]
            out[z, :, piece:piece + v] = up[r]


def offer(meta, down_t, up, chips, slots):
    _, rank, piece = down_t.shape
    shape = (chips, rank, piece + 128)
    return call(
        functools.partial(offer_kernel, slots),
        "offer",
        moved=8 * chips * rank * piece,
        grid_spec=with_meta(
            (1,), [whole(down_t.shape), whole(up.shape)], [whole(shape), whole(shape)]
        ),
        out_shape=[jax.ShapeDtypeStruct(shape, BF)] * 2,
    )(meta, down_t, up)


def merge_kernel(meta, keep, taken, *outs):
    chips = len(outs)
    for k, out in enumerate(outs):
        z = lax.rem(meta[CHIP] + k, chips)
        out[meta[CORE]] = keep[z]
        out[1 - meta[CORE]] = taken[z]


def merge(meta, keep, taken):
    chips, rank, wide = keep.shape
    shape = (2, rank, wide)
    return call(
        merge_kernel,
        "merge",
        moved=4 * keep.size,
        grid_spec=with_meta(
            (1,), [whole(keep.shape), whole(taken.shape)], [whole(shape)] * chips
        ),
        out_shape=[jax.ShapeDtypeStruct(shape, BF)] * chips,
    )(meta, keep, taken)


def choose_kernel(slots, meta, *refs):
    chips = len(refs) - 3
    got, (down, turned, up) = refs[:chips], refs[chips:]
    piece, v, rank = down.shape[2], up.shape[0], down.shape[1]
    for k in range(chips):
        z = lax.rem(meta[CHIP] + chips - k, chips)
        for core in range(2):
            s = segment_at(meta, 2 * z + core, slots, 2 * chips)

            @pl.when(s >= 0)
            def _():
                down[s] = got[k][core]

    for p in range(slots // 2):
        pair = jnp.concatenate([down[2 * p], down[2 * p + 1]], axis=0).astype(F32)
        cols = slice(2 * rank * p, 2 * rank * (p + 1))
        turned[:, cols] = jnp.transpose(pair[:, :turned.shape[0]]).astype(BF)
        up[:, cols] = jnp.transpose(pair[:, turned.shape[0]:])[:v].astype(BF)


def choose(meta, got, slots, v):
    _, rank, wide = got[0].shape
    piece = wide - 128
    shapes = [(slots, rank, wide), (piece, slots * rank), (v, slots * rank)]
    return call(
        functools.partial(choose_kernel, slots),
        "choose",
        moved=4 * slots * rank * wide,
        grid_spec=with_meta((1,), [whole(g.shape) for g in got], [whole(s) for s in shapes]),
        out_shape=[jax.ShapeDtypeStruct(s, BF) for s in shapes],
    )(meta, *got)


def cot_of(part, rows):
    return jnp.concatenate([part[rows:, :rows], part[rows:, rows:]], axis=0)


def project_kernel(slots, rank, meta, part, down_t, up_t, out):
    group, rows, _ = out.shape
    shape = (rows, 2 * rank)
    low = lax.broadcasted_iota(jnp.int32, shape, 1) < rank
    for g in range(group):
        first = (pl.program_id(0) * group + g) * rows
        block = part[g]
        lr = jnp.dot(block[:rows], down_t[...], preferred_element_type=F32)
        lg = lax.dot_general(
            cot_of(block, rows), up_t[...], (((0,), (0,)), ((), ())), preferred_element_type=F32
        )
        lr_sum = jnp.zeros(shape, F32)
        lg_sum = jnp.zeros(shape, F32)
        for p in range(slots // 2):
            keep = inside_pair(meta, p, first, shape, slots, rank)
            cols = slice(2 * rank * p, 2 * rank * (p + 1))
            lr_sum += jnp.where(keep, lr[:, cols], 0.0)
            lg_sum += jnp.where(keep, lg[:, cols], 0.0)
        lr_sum += pltpu.roll(lr_sum, rank, 1)
        lg_sum += pltpu.roll(lg_sum, rank, 1)
        out[g] = jnp.where(low, lr_sum, ADAPTER_SCALE * lg_sum).astype(BF)


def project(meta, parts, down_t, up_t, rows, slots, rank):
    n, tall, piece = parts.shape
    return call(
        functools.partial(project_kernel, slots, rank),
        "project",
        flops=2 * n * rows * piece * slots * rank,
        moved=2 * n * tall * piece,
        grid_spec=with_meta(
            (n // GROUP,),
            [
                pl.BlockSpec((GROUP, tall, piece), lambda j, m: (j, 0, 0)),
                whole(down_t.shape),
                whole(up_t.shape),
            ],
            pl.BlockSpec((GROUP, rows, 2 * rank), lambda j, m: (j, 0, 0)),
        ),
        out_shape=jax.ShapeDtypeStruct((n, rows, 2 * rank), BF),
    )(meta, parts, down_t, up_t)


def total_kernel(parts, copies):
    acc = parts[0].astype(F32)
    for f in range(1, parts.shape[0]):
        acc += parts[f].astype(F32)
    turned = jnp.transpose(acc).astype(BF)
    for f in range(copies.shape[0]):
        copies[f] = turned


def total(parts):
    n, rows, wide = parts.shape
    return call(
        total_kernel,
        "total",
        moved=4 * parts.size,
        out_shape=jax.ShapeDtypeStruct((n, wide, rows), BF),
    )(parts)


def gradient_kernel(slots, rank, v, meta, part, low, keep, give, acc_down, acc_up):
    group, _, rows = low.shape
    step = pl.program_id(0)

    @pl.when(step == 0)
    def _():
        acc_down[...] = jnp.zeros_like(acc_down)
        acc_up[...] = jnp.zeros_like(acc_up)

    for g in range(group):
        first = (step * group + g) * rows
        for s in range(slots):
            start, end = start_of(meta, s), end_of(meta, s, slots)

            @pl.when((start < first + rows) & (end > first))
            def _():
                token = first + lax.broadcasted_iota(jnp.int32, (2 * rank, rows), 1)
                both = low[g].astype(F32)
                both = jnp.where((token >= start) & (token < end), both, 0.0).astype(BF)
                at = slice(s * rank, (s + 1) * rank)
                acc_down[at, :] += jnp.dot(
                    both[rank:], part[g, :rows, :], preferred_element_type=F32
                )
                acc_up[at, :] += lax.dot_general(
                    both[:rank],
                    cot_of(part[g], rows),
                    (((1,), (1,)), ((), ())),
                    preferred_element_type=F32,
                )

    @pl.when(step == pl.num_programs(0) - 1)
    def _():
        piece = acc_down.shape[1]
        keep[...] = jnp.zeros_like(keep)
        give[...] = jnp.zeros_like(give)
        for s in range(slots):
            owner = owner_of(meta, s, slots)
            chip, same = owner // 2, lax.rem(owner, 2) == meta[CORE]
            rows_of = slice(s * rank, (s + 1) * rank)

            def put(out):
                out[chip, :, :piece] = acc_down[rows_of, :].astype(BF)
                out[chip, :, piece:piece + v] = (ADAPTER_SCALE * acc_up[rows_of, :]).astype(BF)

            pl.when(same)(functools.partial(put, keep))
            pl.when(jnp.logical_not(same))(functools.partial(put, give))


def gradient(meta, parts, low, chips, slots, rank, v):
    n, tall, piece = parts.shape
    rows = low.shape[2]
    shape = (chips, rank, piece + 128)
    return call(
        functools.partial(gradient_kernel, slots, rank, v),
        "gradient",
        flops=2 * n * rows * piece * slots * rank,
        moved=2 * n * tall * piece,
        grid_spec=with_meta(
            (n // GROUP,),
            [
                pl.BlockSpec((GROUP, tall, piece), lambda j, m: (j, 0, 0)),
                pl.BlockSpec((GROUP, 2 * rank, rows), lambda j, m: (j, 0, 0)),
            ],
            [whole(shape), whole(shape)],
            [pltpu.VMEM((slots * rank, piece), F32), pltpu.VMEM((slots * rank, v), F32)],
        ),
        out_shape=[jax.ShapeDtypeStruct(shape, BF)] * 2,
    )(meta, parts, low)


def collect_kernel(slots, scale, meta, *refs):
    got, (down, up) = refs[:-2], refs[-2:]
    chips = len(got)
    piece, v = down.shape[2], up.shape[2]
    down[...] = jnp.zeros_like(down)
    up[...] = jnp.zeros_like(up)
    for k in range(chips):
        z = lax.rem(meta[CHIP] + chips - k, chips)
        for core in range(2):
            r = wanted_by(meta, 2 * z + core, slots)

            @pl.when(r >= 0)
            def _():
                down[r] += got[k][core, :, :piece].astype(F32) * scale
                up[r] += got[k][core, :, piece:piece + v].astype(F32) * scale


def collect(meta, got, rows, v, slots, scale):
    _, rank, wide = got[0].shape
    shapes = [(rows, rank, wide - 128), (rows, rank, v)]
    return call(
        functools.partial(collect_kernel, slots, scale),
        "collect",
        moved=2 * len(got) * got[0].size,
        grid_spec=with_meta((1,), [whole(g.shape) for g in got], [whole(s) for s in shapes]),
        out_shape=[jax.ShapeDtypeStruct(s, F32) for s in shapes],
    )(meta, *got)


def term_kernel(slots, rank, meta, low, down, out, acc):
    group, _, rows = low.shape
    piece = out.shape[2]
    for g in range(group):
        first = (pl.program_id(0) * group + g) * rows
        acc[...] = jnp.zeros_like(acc)
        for s in range(slots):
            start, end = start_of(meta, s), end_of(meta, s, slots)

            @pl.when((start < first + rows) & (end > first))
            def _():
                token = first + lax.broadcasted_iota(jnp.int32, (rank, rows), 1)
                lg = low[g, rank:, :].astype(F32)
                lg = jnp.where((token >= start) & (token < end), lg, 0.0).astype(BF)
                acc[...] += lax.dot_general(
                    lg, down[s, :, :piece], (((0,), (0,)), ((), ())), preferred_element_type=F32
                )

        out[g] = acc[...].astype(BF)


def term(meta, low, down, piece, slots, rank):
    n, wide, rows = low.shape
    return call(
        functools.partial(term_kernel, slots, rank),
        "term",
        flops=2 * n * rows * piece * 2 * rank,
        moved=2 * n * rows * piece,
        grid_spec=with_meta(
            (n // GROUP,),
            [pl.BlockSpec((GROUP, wide, rows), lambda j, m: (j, 0, 0)), whole(down.shape)],
            pl.BlockSpec((GROUP, rows, piece), lambda j, m: (j, 0, 0)),
            [pltpu.VMEM((rows, piece), F32)],
        ),
        out_shape=jax.ShapeDtypeStruct((n, rows, piece), BF),
    )(meta, low, down)


def base_kernel(meta, cot, w, out):
    out[...] = jnp.dot(
        cot[...],
        jnp.concatenate([w[e, 0] for e in range(w.shape[0])], axis=0),
        preferred_element_type=F32,
    )


def base(meta, cot, w):
    slices, n, part, piece = w.shape
    rows, width = cot.shape

    def place(f, m):
        y = lax.rem(m[PIECE] // SIDE + SIDE - f // SIDE, SIDE)
        x = lax.rem(lax.rem(m[PIECE], SIDE) + SIDE - lax.rem(f, SIDE), SIDE)
        return (0, y * SIDE + x)

    return call(
        base_kernel,
        "base",
        flops=2 * rows * n * piece * width,
        moved=2 * n * piece * width + 4 * rows * n * piece,
        grid_spec=with_meta(
            (n,),
            [
                whole(cot.shape),
                pl.BlockSpec((slices, 1, part, piece), lambda f, m: (0, f, 0, 0)),
            ],
            pl.BlockSpec((rows, piece), place),
        ),
        out_shape=jax.ShapeDtypeStruct((rows, n * piece), F32),
    )(meta, cot, w)


def join_kernel(done, terms, out):
    group, _, piece = terms.shape
    for g in range(group):
        cols = slice(g * piece, (g + 1) * piece)
        out[:, cols] = (done[:, cols] + terms[g].astype(F32)).astype(BF)


def join(done, terms):
    n, rows, piece = terms.shape
    group = 2
    return call(
        join_kernel,
        "join",
        moved=8 * n * rows * piece,
        grid=(n // group,),
        in_specs=[
            pl.BlockSpec((rows, group * piece), lambda f: (0, f)),
            pl.BlockSpec((group, rows, piece), lambda f: (f, 0, 0)),
        ],
        out_specs=pl.BlockSpec((rows, group * piece), lambda f: (0, f)),
        out_shape=jax.ShapeDtypeStruct((rows, n * piece), BF),
    )(done, terms)


def exchange(x, axis):
    return lax.all_to_all(x, axis, 0, 0, tiled=True)


def swap(x, bins):
    return lax.ppermute(x, "dp", [(i, i ^ 1) for i in range(bins)])


def shift(x, k, bins):
    chips = bins // 2
    return lax.ppermute(
        x, "dp", [(i, (i // 2 + k) % chips * 2 + i % 2) for i in range(bins)]
    )


def spread(meta, keep, give, bins):
    blocks = merge(meta, keep, swap(give, bins))
    return [blocks[0]] + [shift(blocks[k], k, bins) for k in range(1, bins // 2)]


def across(x, dy, dx, n):
    return lax.ppermute(
        x,
        "fsdp",
        [
            (i, (i // SIDE + dy) % SIDE * SIDE + (i % SIDE + dx) % SIDE)
            for i in range(n)
        ],
    )


def scalars(segment_tenant, segment_lengths, tenant_stored_row, own, rows):
    bins, slots = segment_tenant.shape
    me = lax.axis_index("dp")
    tenants = jnp.arange(tenant_stored_row.shape[0], dtype=jnp.int32)
    stored = jnp.sum(
        jnp.where(segment_tenant[:, :, None] == tenants, tenant_stored_row, 0), axis=2
    )
    owners = lax.dynamic_index_in_dim(stored, me, 0, keepdims=False) // own
    lengths = lax.dynamic_index_in_dim(segment_lengths, me, 0, keepdims=False)
    place = jnp.arange(slots, dtype=jnp.int32)
    starts = jnp.sum(jnp.where(place[None, :] < place[:, None], lengths[None, :], 0), axis=1)
    wanted = jnp.max(jnp.where(stored // own == me, stored % own, -1), axis=1)
    every = jnp.arange(bins, dtype=jnp.int32)
    segment = jnp.max(jnp.where(owners[None, :] == every[:, None], place[None, :], -1), axis=1)
    place_f = lax.axis_index("fsdp")
    head = jnp.stack([me % 2, place_f * rows, me // 2, place_f])
    return jnp.concatenate([head, starts, starts + lengths, owners, wanted, segment]).astype(
        jnp.int32
    )


def local(
    tokens,
    cotangent,
    value_weight,
    adapter_down_weight,
    adapter_up_weight,
    segment_tenant,
    segment_lengths,
    tenant_stored_row,
):
    own, piece, rank = adapter_down_weight.shape
    v = adapter_up_weight.shape[2]
    bins, slots = segment_tenant.shape
    chips = bins // 2
    rows = tokens.shape[0]
    n = lax.axis_size("fsdp")
    scale = (n * rows) ** (-0.5)
    meta = scalars(segment_tenant, segment_lengths, tenant_stored_row, own, rows)

    packed = pack(tokens, jnp.swapaxes(cotangent, 0, 1), n)
    me = lax.axis_index("dp").astype(jnp.int32).reshape(1)
    packed, me = lax.optimization_barrier((packed, me))
    parts = exchange(packed, "fsdp")
    mine = turn(me, value_weight, bins)[None]
    mine = jnp.concatenate([mine] + [across(mine, 0, k, n) for k in range(1, SIDE)])
    mine = jnp.concatenate([mine] + [across(mine, k, 0, n) for k in range(1, SIDE)])
    weight = lax.all_gather(mine, "dp", axis=0)

    keep, give = offer(
        meta, jnp.swapaxes(adapter_down_weight, 1, 2), adapter_up_weight, chips, slots
    )
    got = spread(meta, keep, give, bins)
    parts, got, mine = lax.optimization_barrier((parts, got, mine))
    down, down_t, up_t = choose(meta, got, slots, v)

    sums = exchange(project(meta, parts, down_t, up_t, rows, slots, rank), "fsdp")
    low_all = exchange(total(sums), "fsdp")
    terms = term(meta, low_all, down, piece, slots, rank)
    terms, low_all = lax.optimization_barrier((terms, low_all))
    terms = exchange(terms, "fsdp")
    sent = spread(meta, *gradient(meta, parts, low_all, chips, slots, rank, v), bins)
    done = base(meta, cotangent, weight)
    terms, sent, done = lax.optimization_barrier((terms, sent, done))
    grad = join(done, terms)
    down_grad, up_grad = collect(meta, sent, own, v, slots, scale)
    return grad, jnp.swapaxes(down_grad, 1, 2), up_grad


def solution(mesh):
    placed = (
        P(("dp", "fsdp"), None),
        P(("dp", "fsdp"), None),
        P("fsdp", None),
        P("dp", "fsdp", None),
        P("dp", None, "fsdp"),
        P(),
        P(),
        P(),
    )
    return jax.shard_map(
        local,
        mesh=mesh,
        in_specs=placed,
        out_specs=(P(("dp", "fsdp"), None), P("dp", "fsdp", None), P("dp", None, "fsdp")),
        check_vma=False,
    )
```

```python
import functools

import jax
import jax.numpy as jnp
from jax import lax
from jax.experimental import pallas as pl
from jax.experimental.pallas import tpu as pltpu
from jax.sharding import PartitionSpec as P

ADAPTER_SCALE = 2.0
BF = jnp.bfloat16
F32 = jnp.float32
VMEM_BYTES = 40 * 1024 * 1024
VMEM_MOST = 58 * 1024 * 1024
GROUP = 4
CORE, CHIP, LIST = 0, 1, 2


def call(kernel, name, flops=0, moved=0, vmem=VMEM_BYTES, **kw):
    return pl.pallas_call(
        kernel,
        compiler_params=pltpu.CompilerParams(vmem_limit_bytes=vmem),
        cost_estimate=pl.CostEstimate(flops=flops, bytes_accessed=moved, transcendentals=0),
        name=name,
        **kw,
    )


def whole(shape):
    return pl.BlockSpec(shape, lambda i, m: (0,) * len(shape))


def with_meta(grid, in_specs, out_specs, scratch=()):
    return pltpu.PrefetchScalarGridSpec(
        num_scalar_prefetch=1,
        grid=grid,
        in_specs=in_specs,
        out_specs=out_specs,
        scratch_shapes=list(scratch),
    )


def start_of(meta, s):
    return meta[LIST + s]


def end_of(meta, s, slots):
    return meta[LIST + slots + s]


def owner_of(meta, s, slots):
    return meta[LIST + 2 * slots + s]


def wanted_by(meta, b, slots):
    return meta[LIST + 3 * slots + b]


def segment_at(meta, owner, slots, bins):
    return meta[LIST + 3 * slots + bins + owner]


def inside_pair(meta, pair, first, shape, slots, rank):
    row = first + lax.broadcasted_iota(jnp.int32, shape, 0)
    low = lax.broadcasted_iota(jnp.int32, shape, 1) < rank
    begin = jnp.where(low, start_of(meta, 2 * pair), start_of(meta, 2 * pair + 1))
    end = jnp.where(low, end_of(meta, 2 * pair, slots), end_of(meta, 2 * pair + 1, slots))
    return (row >= begin) & (row < end)


def turn_kernel(w, out):
    out[...] = jnp.transpose(w[...].astype(F32)).astype(BF)


def turn(w):
    piece, width = w.shape
    block = width // GROUP
    return call(
        turn_kernel,
        "turn",
        moved=4 * width * piece,
        grid=(GROUP,),
        in_specs=[pl.BlockSpec((piece, block), lambda i: (0, i))],
        out_specs=pl.BlockSpec((block, piece), lambda i: (i, 0)),
        out_shape=jax.ShapeDtypeStruct((width, piece), BF),
    )(w)


def pack_kernel(tok, cot_t, out):
    rows = tok.shape[0]
    n, _, piece = out.shape
    v = cot_t.shape[0] // n
    for f in range(n):
        out[f, :rows, :] = tok[:, f * piece:(f + 1) * piece]
        out[f, rows:, :rows] = cot_t[f * v:f * v + v // 2, :]
        out[f, rows:, rows:] = cot_t[f * v + v // 2:(f + 1) * v, :]


def pack(tokens, cot_t, n):
    rows, width = tokens.shape
    piece, v = width // n, cot_t.shape[0] // n
    tall = rows + v * rows // piece
    return call(
        pack_kernel,
        "pack",
        moved=4 * rows * width,
        vmem=VMEM_MOST,
        grid=(n // GROUP,),
        in_specs=[
            pl.BlockSpec((rows, GROUP * piece), lambda f: (0, f)),
            pl.BlockSpec((GROUP * v, rows), lambda f: (f, 0)),
        ],
        out_specs=pl.BlockSpec((GROUP, tall, piece), lambda f: (f, 0, 0)),
        out_shape=jax.ShapeDtypeStruct((n, tall, piece), BF),
    )(tokens, cot_t)


def offer_kernel(slots, meta, down_t, up, keep, give):
    piece, v = down_t.shape[2], up.shape[2]
    keep[...] = jnp.zeros_like(keep)
    give[...] = jnp.zeros_like(give)
    for z in range(keep.shape[0]):
        for out, core in ((keep, meta[CORE]), (give, 1 - meta[CORE])):
            r = jnp.maximum(wanted_by(meta, 2 * z + core, slots), 0)
            out[z, :, :piece] = down_t[r]
            out[z, :, piece:piece + v] = up[r]


def offer(meta, down_t, up, chips, slots):
    _, rank, piece = down_t.shape
    shape = (chips, rank, piece + 128)
    return call(
        functools.partial(offer_kernel, slots),
        "offer",
        moved=8 * chips * rank * piece,
        grid_spec=with_meta(
            (1,), [whole(down_t.shape), whole(up.shape)], [whole(shape), whole(shape)]
        ),
        out_shape=[jax.ShapeDtypeStruct(shape, BF)] * 2,
    )(meta, down_t, up)


def merge_kernel(meta, keep, taken, *outs):
    chips = len(outs)
    for k, out in enumerate(outs):
        z = lax.rem(meta[CHIP] + k, chips)
        out[meta[CORE]] = keep[z]
        out[1 - meta[CORE]] = taken[z]


def merge(meta, keep, taken):
    chips, rank, wide = keep.shape
    shape = (2, rank, wide)
    return call(
        merge_kernel,
        "merge",
        moved=4 * keep.size,
        grid_spec=with_meta(
            (1,), [whole(keep.shape), whole(taken.shape)], [whole(shape)] * chips
        ),
        out_shape=[jax.ShapeDtypeStruct(shape, BF)] * chips,
    )(meta, keep, taken)


def choose_kernel(slots, meta, *refs):
    chips = len(refs) - 3
    got, (down, turned, up) = refs[:chips], refs[chips:]
    piece, v, rank = down.shape[2], up.shape[0], down.shape[1]
    for k in range(chips):
        z = lax.rem(meta[CHIP] + chips - k, chips)
        for core in range(2):
            s = segment_at(meta, 2 * z + core, slots, 2 * chips)

            @pl.when(s >= 0)
            def _():
                down[s] = got[k][core]

    for p in range(slots // 2):
        pair = jnp.concatenate([down[2 * p], down[2 * p + 1]], axis=0).astype(F32)
        cols = slice(2 * rank * p, 2 * rank * (p + 1))
        turned[:, cols] = jnp.transpose(pair[:, :turned.shape[0]]).astype(BF)
        up[:, cols] = jnp.transpose(pair[:, turned.shape[0]:])[:v].astype(BF)


def choose(meta, got, slots, v):
    _, rank, wide = got[0].shape
    piece = wide - 128
    shapes = [(slots, rank, wide), (piece, slots * rank), (v, slots * rank)]
    return call(
        functools.partial(choose_kernel, slots),
        "choose",
        moved=4 * slots * rank * wide,
        grid_spec=with_meta((1,), [whole(g.shape) for g in got], [whole(s) for s in shapes]),
        out_shape=[jax.ShapeDtypeStruct(s, BF) for s in shapes],
    )(meta, *got)


def cot_of(part, rows):
    return jnp.concatenate([part[rows:, :rows], part[rows:, rows:]], axis=0)


def project_kernel(slots, rank, meta, part, down_t, up_t, out):
    group, rows, _ = out.shape
    shape = (rows, 2 * rank)
    low = lax.broadcasted_iota(jnp.int32, shape, 1) < rank
    for g in range(group):
        first = (pl.program_id(0) * group + g) * rows
        block = part[g]
        lr = jnp.dot(block[:rows], down_t[...], preferred_element_type=F32)
        lg = lax.dot_general(
            cot_of(block, rows), up_t[...], (((0,), (0,)), ((), ())), preferred_element_type=F32
        )
        lr_sum = jnp.zeros(shape, F32)
        lg_sum = jnp.zeros(shape, F32)
        for p in range(slots // 2):
            keep = inside_pair(meta, p, first, shape, slots, rank)
            cols = slice(2 * rank * p, 2 * rank * (p + 1))
            lr_sum += jnp.where(keep, lr[:, cols], 0.0)
            lg_sum += jnp.where(keep, lg[:, cols], 0.0)
        lr_sum += pltpu.roll(lr_sum, rank, 1)
        lg_sum += pltpu.roll(lg_sum, rank, 1)
        out[g] = jnp.where(low, lr_sum, ADAPTER_SCALE * lg_sum).astype(BF)


def project(meta, parts, down_t, up_t, rows, slots, rank):
    n, tall, piece = parts.shape
    return call(
        functools.partial(project_kernel, slots, rank),
        "project",
        flops=2 * n * rows * piece * slots * rank,
        moved=2 * n * tall * piece,
        grid_spec=with_meta(
            (n // GROUP,),
            [
                pl.BlockSpec((GROUP, tall, piece), lambda j, m: (j, 0, 0)),
                whole(down_t.shape),
                whole(up_t.shape),
            ],
            pl.BlockSpec((GROUP, rows, 2 * rank), lambda j, m: (j, 0, 0)),
        ),
        out_shape=jax.ShapeDtypeStruct((n, rows, 2 * rank), BF),
    )(meta, parts, down_t, up_t)


def total_kernel(parts, copies):
    acc = parts[0].astype(F32)
    for f in range(1, parts.shape[0]):
        acc += parts[f].astype(F32)
    turned = jnp.transpose(acc).astype(BF)
    for f in range(copies.shape[0]):
        copies[f] = turned


def total(parts):
    n, rows, wide = parts.shape
    return call(
        total_kernel,
        "total",
        moved=4 * parts.size,
        out_shape=jax.ShapeDtypeStruct((n, wide, rows), BF),
    )(parts)


def gradient_kernel(slots, rank, v, meta, part, low, keep, give, acc_down, acc_up):
    group, _, rows = low.shape
    step = pl.program_id(0)

    @pl.when(step == 0)
    def _():
        acc_down[...] = jnp.zeros_like(acc_down)
        acc_up[...] = jnp.zeros_like(acc_up)

    for g in range(group):
        first = (step * group + g) * rows
        for s in range(slots):
            start, end = start_of(meta, s), end_of(meta, s, slots)

            @pl.when((start < first + rows) & (end > first))
            def _():
                token = first + lax.broadcasted_iota(jnp.int32, (2 * rank, rows), 1)
                both = low[g].astype(F32)
                both = jnp.where((token >= start) & (token < end), both, 0.0).astype(BF)
                at = slice(s * rank, (s + 1) * rank)
                acc_down[at, :] += jnp.dot(
                    both[rank:], part[g, :rows, :], preferred_element_type=F32
                )
                acc_up[at, :] += lax.dot_general(
                    both[:rank],
                    cot_of(part[g], rows),
                    (((1,), (1,)), ((), ())),
                    preferred_element_type=F32,
                )

    @pl.when(step == pl.num_programs(0) - 1)
    def _():
        piece = acc_down.shape[1]
        keep[...] = jnp.zeros_like(keep)
        give[...] = jnp.zeros_like(give)
        for s in range(slots):
            owner = owner_of(meta, s, slots)
            chip, same = owner // 2, lax.rem(owner, 2) == meta[CORE]
            rows_of = slice(s * rank, (s + 1) * rank)

            def put(out):
                out[chip, :, :piece] = acc_down[rows_of, :].astype(BF)
                out[chip, :, piece:piece + v] = (ADAPTER_SCALE * acc_up[rows_of, :]).astype(BF)

            pl.when(same)(functools.partial(put, keep))
            pl.when(jnp.logical_not(same))(functools.partial(put, give))


def gradient(meta, parts, low, chips, slots, rank, v):
    n, tall, piece = parts.shape
    rows = low.shape[2]
    shape = (chips, rank, piece + 128)
    return call(
        functools.partial(gradient_kernel, slots, rank, v),
        "gradient",
        flops=2 * n * rows * piece * slots * rank,
        moved=2 * n * tall * piece,
        grid_spec=with_meta(
            (n // GROUP,),
            [
                pl.BlockSpec((GROUP, tall, piece), lambda j, m: (j, 0, 0)),
                pl.BlockSpec((GROUP, 2 * rank, rows), lambda j, m: (j, 0, 0)),
            ],
            [whole(shape), whole(shape)],
            [pltpu.VMEM((slots * rank, piece), F32), pltpu.VMEM((slots * rank, v), F32)],
        ),
        out_shape=[jax.ShapeDtypeStruct(shape, BF)] * 2,
    )(meta, parts, low)


def collect_kernel(slots, scale, meta, *refs):
    got, (down, up) = refs[:-2], refs[-2:]
    chips = len(got)
    piece, v = down.shape[2], up.shape[2]
    down[...] = jnp.zeros_like(down)
    up[...] = jnp.zeros_like(up)
    for k in range(chips):
        z = lax.rem(meta[CHIP] + chips - k, chips)
        for core in range(2):
            r = wanted_by(meta, 2 * z + core, slots)

            @pl.when(r >= 0)
            def _():
                down[r] += got[k][core, :, :piece].astype(F32) * scale
                up[r] += got[k][core, :, piece:piece + v].astype(F32) * scale


def collect(meta, got, rows, v, slots, scale):
    _, rank, wide = got[0].shape
    shapes = [(rows, rank, wide - 128), (rows, rank, v)]
    return call(
        functools.partial(collect_kernel, slots, scale),
        "collect",
        moved=2 * len(got) * got[0].size,
        grid_spec=with_meta((1,), [whole(g.shape) for g in got], [whole(s) for s in shapes]),
        out_shape=[jax.ShapeDtypeStruct(s, F32) for s in shapes],
    )(meta, *got)


def term_kernel(slots, rank, meta, low, cot, w, down, out):
    group, _, rows = low.shape
    piece = out.shape[2]
    table = jnp.concatenate([down[s, :, :piece] for s in range(slots)], axis=0)
    for g in range(group):
        first = (pl.program_id(0) * group + g) * rows
        lg = low[g, rank:, :].astype(F32)
        lg = jnp.transpose(jnp.concatenate([lg, lg], axis=0))
        lg = [
            jnp.where(inside_pair(meta, p, first, lg.shape, slots, rank), lg, 0.0)
            for p in range(slots // 2)
        ]
        lg = jnp.concatenate(lg, axis=1).astype(BF)
        acc = jnp.dot(cot[g], w[...], preferred_element_type=F32)
        acc += jnp.dot(lg, table, preferred_element_type=F32)
        out[g] = acc.astype(BF)


def term(meta, low, cot, w, down, slots, rank):
    n, wide, rows = low.shape
    width, piece = w.shape
    group = 2
    return call(
        functools.partial(term_kernel, slots, rank),
        "term",
        flops=2 * n * rows * piece * (width + slots * rank),
        moved=2 * n * rows * (piece + width),
        vmem=VMEM_MOST,
        grid_spec=with_meta(
            (n // group,),
            [
                pl.BlockSpec((group, wide, rows), lambda j, m: (j, 0, 0)),
                pl.BlockSpec((group, rows, width), lambda j, m: (j, 0, 0)),
                whole(w.shape),
                whole(down.shape),
            ],
            pl.BlockSpec((group, rows, piece), lambda j, m: (j, 0, 0)),
        ),
        out_shape=jax.ShapeDtypeStruct((n, rows, piece), BF),
    )(meta, low, cot, w, down)


def lay_kernel(blocks, out):
    group, _, piece = blocks.shape
    for g in range(group):
        out[:, g * piece:(g + 1) * piece] = blocks[g]


def lay(blocks):
    n, rows, piece = blocks.shape
    return call(
        lay_kernel,
        "lay",
        moved=4 * n * rows * piece,
        vmem=VMEM_MOST,
        grid=(n // GROUP,),
        in_specs=[pl.BlockSpec((GROUP, rows, piece), lambda f: (f, 0, 0))],
        out_specs=pl.BlockSpec((rows, GROUP * piece), lambda f: (0, f)),
        out_shape=jax.ShapeDtypeStruct((rows, n * piece), BF),
    )(blocks)


def exchange(x, axis):
    return lax.all_to_all(x, axis, 0, 0, tiled=True)


def swap(x, bins):
    return lax.ppermute(x, "dp", [(i, i ^ 1) for i in range(bins)])


def shift(x, k, bins):
    chips = bins // 2
    return lax.ppermute(
        x, "dp", [(i, (i // 2 + k) % chips * 2 + i % 2) for i in range(bins)]
    )


def spread(meta, keep, give, bins):
    blocks = merge(meta, keep, swap(give, bins))
    return [blocks[0]] + [shift(blocks[k], k, bins) for k in range(1, bins // 2)]


def scalars(segment_tenant, segment_lengths, tenant_stored_row, own):
    bins, slots = segment_tenant.shape
    me = lax.axis_index("dp")
    tenants = jnp.arange(tenant_stored_row.shape[0], dtype=jnp.int32)
    stored = jnp.sum(
        jnp.where(segment_tenant[:, :, None] == tenants, tenant_stored_row, 0), axis=2
    )
    owners = lax.dynamic_index_in_dim(stored, me, 0, keepdims=False) // own
    lengths = lax.dynamic_index_in_dim(segment_lengths, me, 0, keepdims=False)
    place = jnp.arange(slots, dtype=jnp.int32)
    starts = jnp.sum(jnp.where(place[None, :] < place[:, None], lengths[None, :], 0), axis=1)
    wanted = jnp.max(jnp.where(stored // own == me, stored % own, -1), axis=1)
    every = jnp.arange(bins, dtype=jnp.int32)
    segment = jnp.max(jnp.where(owners[None, :] == every[:, None], place[None, :], -1), axis=1)
    head = jnp.stack([me % 2, me // 2])
    return jnp.concatenate([head, starts, starts + lengths, owners, wanted, segment]).astype(
        jnp.int32
    )


def local(
    tokens,
    cotangent,
    value_weight,
    adapter_down_weight,
    adapter_up_weight,
    segment_tenant,
    segment_lengths,
    tenant_stored_row,
):
    own, piece, rank = adapter_down_weight.shape
    v = adapter_up_weight.shape[2]
    bins, slots = segment_tenant.shape
    chips = bins // 2
    rows = tokens.shape[0]
    n = lax.axis_size("fsdp")
    scale = (n * rows) ** (-0.5)
    meta = scalars(segment_tenant, segment_lengths, tenant_stored_row, own)

    parts = exchange(pack(tokens, jnp.swapaxes(cotangent, 0, 1), n), "fsdp")
    cot = lax.all_gather(cotangent, "fsdp", axis=0)
    keep, give = offer(
        meta, jnp.swapaxes(adapter_down_weight, 1, 2), adapter_up_weight, chips, slots
    )
    got = spread(meta, keep, give, bins)
    parts, got = lax.optimization_barrier((parts, got))
    down, down_t, up_t = choose(meta, got, slots, v)

    sums = exchange(project(meta, parts, down_t, up_t, rows, slots, rank), "fsdp")
    low_all = exchange(total(sums), "fsdp")
    terms = term(meta, low_all, cot, turn(value_weight), down, slots, rank)
    terms, low_all = lax.optimization_barrier((terms, low_all))
    terms = exchange(terms, "fsdp")
    sent = spread(meta, *gradient(meta, parts, low_all, chips, slots, rank, v), bins)
    down_grad, up_grad = collect(meta, sent, own, v, slots, scale)
    terms, down_grad, up_grad = lax.optimization_barrier((terms, down_grad, up_grad))
    return lay(terms), jnp.swapaxes(down_grad, 1, 2), up_grad


def solution(mesh):
    placed = (
        P(("dp", "fsdp"), None),
        P(("dp", "fsdp"), None),
        P("fsdp", None),
        P("dp", "fsdp", None),
        P("dp", None, "fsdp"),
        P(),
        P(),
        P(),
    )
    return jax.shard_map(
        local,
        mesh=mesh,
        in_specs=placed,
        out_specs=(P(("dp", "fsdp"), None), P("dp", "fsdp", None), P("dp", None, "fsdp")),
        check_vma=False,
    )
```

```python
import functools

import jax
import jax.numpy as jnp
from jax import lax
from jax.experimental import pallas as pl
from jax.experimental.pallas import tpu as pltpu
from jax.sharding import PartitionSpec as P

ADAPTER_SCALE = 2.0
BF = jnp.bfloat16
F32 = jnp.float32
VMEM_BYTES = 40 * 1024 * 1024
VMEM_MOST = 58 * 1024 * 1024
GROUP = 4
CORE, CHIP, LIST = 0, 1, 2


def call(kernel, name, flops=0, moved=0, vmem=VMEM_BYTES, **kw):
    return pl.pallas_call(
        kernel,
        compiler_params=pltpu.CompilerParams(vmem_limit_bytes=vmem),
        cost_estimate=pl.CostEstimate(flops=flops, bytes_accessed=moved, transcendentals=0),
        name=name,
        **kw,
    )


def whole(shape):
    return pl.BlockSpec(shape, lambda i, m: (0,) * len(shape))


def with_meta(grid, in_specs, out_specs, scratch=()):
    return pltpu.PrefetchScalarGridSpec(
        num_scalar_prefetch=1,
        grid=grid,
        in_specs=in_specs,
        out_specs=out_specs,
        scratch_shapes=list(scratch),
    )


def start_of(meta, s):
    return meta[LIST + s]


def end_of(meta, s, slots):
    return meta[LIST + slots + s]


def owner_of(meta, s, slots):
    return meta[LIST + 2 * slots + s]


def wanted_by(meta, b, slots):
    return meta[LIST + 3 * slots + b]


def segment_at(meta, owner, slots, bins):
    return meta[LIST + 3 * slots + bins + owner]


def inside_pair(meta, pair, first, shape, slots, rank):
    row = first + lax.broadcasted_iota(jnp.int32, shape, 0)
    low = lax.broadcasted_iota(jnp.int32, shape, 1) < rank
    begin = jnp.where(low, start_of(meta, 2 * pair), start_of(meta, 2 * pair + 1))
    end = jnp.where(low, end_of(meta, 2 * pair, slots), end_of(meta, 2 * pair + 1, slots))
    return (row >= begin) & (row < end)


def turn_kernel(at, w, out):
    both = jnp.transpose(w[...].astype(F32)).astype(BF)
    part = out.shape[0]
    low = lax.rem(at[0], 2) == 0
    out[...] = jnp.where(low, both[:part], both[part:])


def turn(at, w, slices):
    piece, width = w.shape
    part = width // slices
    return call(
        turn_kernel,
        "turn",
        moved=4 * part * piece,
        grid_spec=with_meta(
            (1,),
            [pl.BlockSpec((piece, 2 * part), lambda i, m: (0, m[0] // 2))],
            whole((part, piece)),
        ),
        out_shape=jax.ShapeDtypeStruct((part, piece), BF),
    )(at, w)


def pack_kernel(tok, cot_t, out):
    rows = tok.shape[0]
    n, _, piece = out.shape
    v = cot_t.shape[0] // n
    for f in range(n):
        out[f, :rows, :] = tok[:, f * piece:(f + 1) * piece]
        out[f, rows:, :rows] = cot_t[f * v:f * v + v // 2, :]
        out[f, rows:, rows:] = cot_t[f * v + v // 2:(f + 1) * v, :]


def pack(tokens, cot_t, n):
    rows, width = tokens.shape
    piece, v = width // n, cot_t.shape[0] // n
    tall = rows + v * rows // piece
    return call(
        pack_kernel,
        "pack",
        moved=4 * rows * width,
        vmem=VMEM_MOST,
        grid=(n // GROUP,),
        in_specs=[
            pl.BlockSpec((rows, GROUP * piece), lambda f: (0, f)),
            pl.BlockSpec((GROUP * v, rows), lambda f: (f, 0)),
        ],
        out_specs=pl.BlockSpec((GROUP, tall, piece), lambda f: (f, 0, 0)),
        out_shape=jax.ShapeDtypeStruct((n, tall, piece), BF),
    )(tokens, cot_t)


def offer_kernel(slots, meta, down_t, up, keep, give):
    piece, v = down_t.shape[2], up.shape[2]
    keep[...] = jnp.zeros_like(keep)
    give[...] = jnp.zeros_like(give)
    for z in range(keep.shape[0]):
        for out, core in ((keep, meta[CORE]), (give, 1 - meta[CORE])):
            r = jnp.maximum(wanted_by(meta, 2 * z + core, slots), 0)
            out[z, :, :piece] = down_t[r]
            out[z, :, piece:piece + v] = up[r]


def offer(meta, down_t, up, chips, slots):
    _, rank, piece = down_t.shape
    shape = (chips, rank, piece + 128)
    return call(
        functools.partial(offer_kernel, slots),
        "offer",
        moved=8 * chips * rank * piece,
        grid_spec=with_meta(
            (1,), [whole(down_t.shape), whole(up.shape)], [whole(shape), whole(shape)]
        ),
        out_shape=[jax.ShapeDtypeStruct(shape, BF)] * 2,
    )(meta, down_t, up)


def merge_kernel(meta, keep, taken, *outs):
    chips = len(outs)
    for k, out in enumerate(outs):
        z = lax.rem(meta[CHIP] + k, chips)
        out[meta[CORE]] = keep[z]
        out[1 - meta[CORE]] = taken[z]


def merge(meta, keep, taken):
    chips, rank, wide = keep.shape
    shape = (2, rank, wide)
    return call(
        merge_kernel,
        "merge",
        moved=4 * keep.size,
        grid_spec=with_meta(
            (1,), [whole(keep.shape), whole(taken.shape)], [whole(shape)] * chips
        ),
        out_shape=[jax.ShapeDtypeStruct(shape, BF)] * chips,
    )(meta, keep, taken)


def choose_kernel(slots, meta, *refs):
    chips = len(refs) - 3
    got, (down, turned, up) = refs[:chips], refs[chips:]
    piece, v, rank = down.shape[2], up.shape[0], down.shape[1]
    for k in range(chips):
        z = lax.rem(meta[CHIP] + chips - k, chips)
        for core in range(2):
            s = segment_at(meta, 2 * z + core, slots, 2 * chips)

            @pl.when(s >= 0)
            def _():
                down[s] = got[k][core]

    for p in range(slots // 2):
        pair = jnp.concatenate([down[2 * p], down[2 * p + 1]], axis=0).astype(F32)
        cols = slice(2 * rank * p, 2 * rank * (p + 1))
        turned[:, cols] = jnp.transpose(pair[:, :turned.shape[0]]).astype(BF)
        up[:, cols] = jnp.transpose(pair[:, turned.shape[0]:])[:v].astype(BF)


def choose(meta, got, slots, v):
    _, rank, wide = got[0].shape
    piece = wide - 128
    shapes = [(slots, rank, wide), (piece, slots * rank), (v, slots * rank)]
    return call(
        functools.partial(choose_kernel, slots),
        "choose",
        moved=4 * slots * rank * wide,
        grid_spec=with_meta((1,), [whole(g.shape) for g in got], [whole(s) for s in shapes]),
        out_shape=[jax.ShapeDtypeStruct(s, BF) for s in shapes],
    )(meta, *got)


def cot_of(part, rows):
    return jnp.concatenate([part[rows:, :rows], part[rows:, rows:]], axis=0)


def project_kernel(slots, rank, meta, part, down_t, up_t, out):
    group, rows, _ = out.shape
    shape = (rows, 2 * rank)
    low = lax.broadcasted_iota(jnp.int32, shape, 1) < rank
    for g in range(group):
        first = (pl.program_id(0) * group + g) * rows
        block = part[g]
        lr = jnp.dot(block[:rows], down_t[...], preferred_element_type=F32)
        lg = lax.dot_general(
            cot_of(block, rows), up_t[...], (((0,), (0,)), ((), ())), preferred_element_type=F32
        )
        lr_sum = jnp.zeros(shape, F32)
        lg_sum = jnp.zeros(shape, F32)
        for p in range(slots // 2):
            keep = inside_pair(meta, p, first, shape, slots, rank)
            cols = slice(2 * rank * p, 2 * rank * (p + 1))
            lr_sum += jnp.where(keep, lr[:, cols], 0.0)
            lg_sum += jnp.where(keep, lg[:, cols], 0.0)
        lr_sum += pltpu.roll(lr_sum, rank, 1)
        lg_sum += pltpu.roll(lg_sum, rank, 1)
        out[g] = jnp.where(low, lr_sum, ADAPTER_SCALE * lg_sum).astype(BF)


def project(meta, parts, down_t, up_t, rows, slots, rank):
    n, tall, piece = parts.shape
    return call(
        functools.partial(project_kernel, slots, rank),
        "project",
        flops=2 * n * rows * piece * slots * rank,
        moved=2 * n * tall * piece,
        grid_spec=with_meta(
            (n // GROUP,),
            [
                pl.BlockSpec((GROUP, tall, piece), lambda j, m: (j, 0, 0)),
                whole(down_t.shape),
                whole(up_t.shape),
            ],
            pl.BlockSpec((GROUP, rows, 2 * rank), lambda j, m: (j, 0, 0)),
        ),
        out_shape=jax.ShapeDtypeStruct((n, rows, 2 * rank), BF),
    )(meta, parts, down_t, up_t)


def total_kernel(parts, copies):
    acc = parts[0].astype(F32)
    for f in range(1, parts.shape[0]):
        acc += parts[f].astype(F32)
    turned = jnp.transpose(acc).astype(BF)
    for f in range(copies.shape[0]):
        copies[f] = turned


def total(parts):
    n, rows, wide = parts.shape
    return call(
        total_kernel,
        "total",
        moved=4 * parts.size,
        out_shape=jax.ShapeDtypeStruct((n, wide, rows), BF),
    )(parts)


def gradient_kernel(slots, rank, v, meta, part, low, keep, give, acc_down, acc_up):
    group, _, rows = low.shape
    step = pl.program_id(0)

    @pl.when(step == 0)
    def _():
        acc_down[...] = jnp.zeros_like(acc_down)
        acc_up[...] = jnp.zeros_like(acc_up)

    for g in range(group):
        first = (step * group + g) * rows
        for s in range(slots):
            start, end = start_of(meta, s), end_of(meta, s, slots)

            @pl.when((start < first + rows) & (end > first))
            def _():
                token = first + lax.broadcasted_iota(jnp.int32, (2 * rank, rows), 1)
                both = low[g].astype(F32)
                both = jnp.where((token >= start) & (token < end), both, 0.0).astype(BF)
                at = slice(s * rank, (s + 1) * rank)
                acc_down[at, :] += jnp.dot(
                    both[rank:], part[g, :rows, :], preferred_element_type=F32
                )
                acc_up[at, :] += lax.dot_general(
                    both[:rank],
                    cot_of(part[g], rows),
                    (((1,), (1,)), ((), ())),
                    preferred_element_type=F32,
                )

    @pl.when(step == pl.num_programs(0) - 1)
    def _():
        piece = acc_down.shape[1]
        keep[...] = jnp.zeros_like(keep)
        give[...] = jnp.zeros_like(give)
        for s in range(slots):
            owner = owner_of(meta, s, slots)
            chip, same = owner // 2, lax.rem(owner, 2) == meta[CORE]
            rows_of = slice(s * rank, (s + 1) * rank)

            def put(out):
                out[chip, :, :piece] = acc_down[rows_of, :].astype(BF)
                out[chip, :, piece:piece + v] = (ADAPTER_SCALE * acc_up[rows_of, :]).astype(BF)

            pl.when(same)(functools.partial(put, keep))
            pl.when(jnp.logical_not(same))(functools.partial(put, give))


def gradient(meta, parts, low, chips, slots, rank, v):
    n, tall, piece = parts.shape
    rows = low.shape[2]
    shape = (chips, rank, piece + 128)
    return call(
        functools.partial(gradient_kernel, slots, rank, v),
        "gradient",
        flops=2 * n * rows * piece * slots * rank,
        moved=2 * n * tall * piece,
        grid_spec=with_meta(
            (n // GROUP,),
            [
                pl.BlockSpec((GROUP, tall, piece), lambda j, m: (j, 0, 0)),
                pl.BlockSpec((GROUP, 2 * rank, rows), lambda j, m: (j, 0, 0)),
            ],
            [whole(shape), whole(shape)],
            [pltpu.VMEM((slots * rank, piece), F32), pltpu.VMEM((slots * rank, v), F32)],
        ),
        out_shape=[jax.ShapeDtypeStruct(shape, BF)] * 2,
    )(meta, parts, low)


def collect_kernel(slots, scale, meta, *refs):
    got, (down, up) = refs[:-2], refs[-2:]
    chips = len(got)
    piece, v = down.shape[2], up.shape[2]
    down[...] = jnp.zeros_like(down)
    up[...] = jnp.zeros_like(up)
    for k in range(chips):
        z = lax.rem(meta[CHIP] + chips - k, chips)
        for core in range(2):
            r = wanted_by(meta, 2 * z + core, slots)

            @pl.when(r >= 0)
            def _():
                down[r] += got[k][core, :, :piece].astype(F32) * scale
                up[r] += got[k][core, :, piece:piece + v].astype(F32) * scale


def collect(meta, got, rows, v, slots, scale):
    _, rank, wide = got[0].shape
    shapes = [(rows, rank, wide - 128), (rows, rank, v)]
    return call(
        functools.partial(collect_kernel, slots, scale),
        "collect",
        moved=2 * len(got) * got[0].size,
        grid_spec=with_meta((1,), [whole(g.shape) for g in got], [whole(s) for s in shapes]),
        out_shape=[jax.ShapeDtypeStruct(s, F32) for s in shapes],
    )(meta, *got)


def term_kernel(slots, rank, meta, low, down, out):
    group, _, rows = low.shape
    piece = out.shape[2]
    table = jnp.concatenate([down[s, :, :piece] for s in range(slots)], axis=0)
    for g in range(group):
        first = (pl.program_id(0) * group + g) * rows
        lg = low[g, rank:, :].astype(F32)
        lg = jnp.transpose(jnp.concatenate([lg, lg], axis=0))
        lg = [
            jnp.where(inside_pair(meta, p, first, lg.shape, slots, rank), lg, 0.0)
            for p in range(slots // 2)
        ]
        lg = jnp.concatenate(lg, axis=1).astype(BF)
        out[g] = jnp.dot(lg, table, preferred_element_type=F32).astype(BF)


def term(meta, low, down, piece, slots, rank):
    n, wide, rows = low.shape
    return call(
        functools.partial(term_kernel, slots, rank),
        "term",
        flops=2 * n * rows * piece * slots * rank,
        moved=2 * n * rows * piece,
        vmem=VMEM_MOST,
        grid_spec=with_meta(
            (n // GROUP,),
            [pl.BlockSpec((GROUP, wide, rows), lambda j, m: (j, 0, 0)), whole(down.shape)],
            pl.BlockSpec((GROUP, rows, piece), lambda j, m: (j, 0, 0)),
        ),
        out_shape=jax.ShapeDtypeStruct((n, rows, piece), BF),
    )(meta, low, down)


def base_kernel(cot, w, out):
    slices, group, _, piece = w.shape
    for g in range(group):
        out[:, g * piece:(g + 1) * piece] = jnp.dot(
            cot[...],
            jnp.concatenate([w[e, g] for e in range(slices)], axis=0),
            preferred_element_type=F32,
        )


def base(cot, w):
    slices, n, part, piece = w.shape
    rows, width = cot.shape
    group = 2
    return call(
        base_kernel,
        "base",
        flops=2 * rows * n * piece * width,
        moved=2 * n * piece * width + 4 * rows * n * piece,
        vmem=VMEM_MOST,
        grid=(n // group,),
        in_specs=[
            pl.BlockSpec(cot.shape, lambda f: (0, 0)),
            pl.BlockSpec((slices, group, part, piece), lambda f: (0, f, 0, 0)),
        ],
        out_specs=pl.BlockSpec((rows, group * piece), lambda f: (0, f)),
        out_shape=jax.ShapeDtypeStruct((rows, n * piece), F32),
    )(cot, w)


def join_kernel(done, terms, out):
    group, _, piece = terms.shape
    for g in range(group):
        cols = slice(g * piece, (g + 1) * piece)
        out[:, cols] = (done[:, cols] + terms[g].astype(F32)).astype(BF)


def join(done, terms):
    n, rows, piece = terms.shape
    group = 2
    return call(
        join_kernel,
        "join",
        moved=8 * n * rows * piece,
        vmem=VMEM_MOST,
        grid=(n // group,),
        in_specs=[
            pl.BlockSpec((rows, group * piece), lambda f: (0, f)),
            pl.BlockSpec((group, rows, piece), lambda f: (f, 0, 0)),
        ],
        out_specs=pl.BlockSpec((rows, group * piece), lambda f: (0, f)),
        out_shape=jax.ShapeDtypeStruct((rows, n * piece), BF),
    )(done, terms)


def exchange(x, axis):
    return lax.all_to_all(x, axis, 0, 0, tiled=True)


def swap(x, bins):
    return lax.ppermute(x, "dp", [(i, i ^ 1) for i in range(bins)])


def shift(x, k, bins):
    chips = bins // 2
    return lax.ppermute(
        x, "dp", [(i, (i // 2 + k) % chips * 2 + i % 2) for i in range(bins)]
    )


def spread(meta, keep, give, bins):
    blocks = merge(meta, keep, swap(give, bins))
    return [blocks[0]] + [shift(blocks[k], k, bins) for k in range(1, bins // 2)]


def scalars(segment_tenant, segment_lengths, tenant_stored_row, own):
    bins, slots = segment_tenant.shape
    me = lax.axis_index("dp")
    tenants = jnp.arange(tenant_stored_row.shape[0], dtype=jnp.int32)
    stored = jnp.sum(
        jnp.where(segment_tenant[:, :, None] == tenants, tenant_stored_row, 0), axis=2
    )
    owners = lax.dynamic_index_in_dim(stored, me, 0, keepdims=False) // own
    lengths = lax.dynamic_index_in_dim(segment_lengths, me, 0, keepdims=False)
    place = jnp.arange(slots, dtype=jnp.int32)
    starts = jnp.sum(jnp.where(place[None, :] < place[:, None], lengths[None, :], 0), axis=1)
    wanted = jnp.max(jnp.where(stored // own == me, stored % own, -1), axis=1)
    every = jnp.arange(bins, dtype=jnp.int32)
    segment = jnp.max(jnp.where(owners[None, :] == every[:, None], place[None, :], -1), axis=1)
    head = jnp.stack([me % 2, me // 2])
    return jnp.concatenate([head, starts, starts + lengths, owners, wanted, segment]).astype(
        jnp.int32
    )


def local(
    tokens,
    cotangent,
    value_weight,
    adapter_down_weight,
    adapter_up_weight,
    segment_tenant,
    segment_lengths,
    tenant_stored_row,
):
    own, piece, rank = adapter_down_weight.shape
    v = adapter_up_weight.shape[2]
    bins, slots = segment_tenant.shape
    chips = bins // 2
    rows = tokens.shape[0]
    n = lax.axis_size("fsdp")
    scale = (n * rows) ** (-0.5)
    meta = scalars(segment_tenant, segment_lengths, tenant_stored_row, own)

    me = lax.axis_index("dp").astype(jnp.int32).reshape(1)
    weight = lax.all_gather(turn(me, value_weight, bins), ("dp", "fsdp"), axis=0)
    weight = weight.reshape((bins, n) + weight.shape[1:])

    parts = exchange(pack(tokens, jnp.swapaxes(cotangent, 0, 1), n), "fsdp")
    keep, give = offer(
        meta, jnp.swapaxes(adapter_down_weight, 1, 2), adapter_up_weight, chips, slots
    )
    got = spread(meta, keep, give, bins)
    parts, got = lax.optimization_barrier((parts, got))
    down, down_t, up_t = choose(meta, got, slots, v)

    sums = exchange(project(meta, parts, down_t, up_t, rows, slots, rank), "fsdp")
    low_all = exchange(total(sums), "fsdp")
    terms = term(meta, low_all, down, piece, slots, rank)
    terms, low_all = lax.optimization_barrier((terms, low_all))
    terms = exchange(terms, "fsdp")
    sent = spread(meta, *gradient(meta, parts, low_all, chips, slots, rank, v), bins)
    down_grad, up_grad = collect(meta, sent, own, v, slots, scale)
    done = base(cotangent, weight)
    terms, down_grad, up_grad, done = lax.optimization_barrier(
        (terms, down_grad, up_grad, done)
    )
    return join(done, terms), jnp.swapaxes(down_grad, 1, 2), up_grad


def solution(mesh):
    placed = (
        P(("dp", "fsdp"), None),
        P(("dp", "fsdp"), None),
        P("fsdp", None),
        P("dp", "fsdp", None),
        P("dp", None, "fsdp"),
        P(),
        P(),
        P(),
    )
    return jax.shard_map(
        local,
        mesh=mesh,
        in_specs=placed,
        out_specs=(P(("dp", "fsdp"), None), P("dp", "fsdp", None), P("dp", None, "fsdp")),
        check_vma=False,
    )
```

```python
import functools

import jax
import jax.numpy as jnp
from jax import lax
from jax.experimental import pallas as pl
from jax.experimental.pallas import tpu as pltpu
from jax.sharding import PartitionSpec as P

ADAPTER_SCALE = 2.0
BF = jnp.bfloat16
F32 = jnp.float32
VMEM_BYTES = 40 * 1024 * 1024
VMEM_MOST = 58 * 1024 * 1024
GROUP = 4
SIDE = 4
CORE, CHIP, PIECE, LIST = 0, 1, 2, 3


def call(kernel, name, flops=0, moved=0, vmem=VMEM_BYTES, **kw):
    return pl.pallas_call(
        kernel,
        compiler_params=pltpu.CompilerParams(vmem_limit_bytes=vmem),
        cost_estimate=pl.CostEstimate(flops=flops, bytes_accessed=moved, transcendentals=0),
        name=name,
        **kw,
    )


def whole(shape):
    return pl.BlockSpec(shape, lambda i, m: (0,) * len(shape))


def with_meta(grid, in_specs, out_specs, scratch=()):
    return pltpu.PrefetchScalarGridSpec(
        num_scalar_prefetch=1,
        grid=grid,
        in_specs=in_specs,
        out_specs=out_specs,
        scratch_shapes=list(scratch),
    )


def start_of(meta, s):
    return meta[LIST + s]


def end_of(meta, s, slots):
    return meta[LIST + slots + s]


def owner_of(meta, s, slots):
    return meta[LIST + 2 * slots + s]


def wanted_by(meta, b, slots):
    return meta[LIST + 3 * slots + b]


def segment_at(meta, owner, slots, bins):
    return meta[LIST + 3 * slots + bins + owner]


def inside_pair(meta, pair, first, shape, slots, rank):
    row = first + lax.broadcasted_iota(jnp.int32, shape, 0)
    low = lax.broadcasted_iota(jnp.int32, shape, 1) < rank
    begin = jnp.where(low, start_of(meta, 2 * pair), start_of(meta, 2 * pair + 1))
    end = jnp.where(low, end_of(meta, 2 * pair, slots), end_of(meta, 2 * pair + 1, slots))
    return (row >= begin) & (row < end)


def turn_kernel(at, w, out):
    both = jnp.transpose(w[...].astype(F32)).astype(BF)
    part = out.shape[0]
    low = lax.rem(at[0], 2) == 0
    out[...] = jnp.where(low, both[:part], both[part:])


def turn(at, w, slices):
    piece, width = w.shape
    part = width // slices
    return call(
        turn_kernel,
        "turn",
        moved=4 * part * piece,
        grid_spec=with_meta(
            (1,),
            [pl.BlockSpec((piece, 2 * part), lambda i, m: (0, m[0] // 2))],
            whole((part, piece)),
        ),
        out_shape=jax.ShapeDtypeStruct((part, piece), BF),
    )(at, w)


def pack_kernel(tok, cot_t, out):
    rows = tok.shape[0]
    n, _, piece = out.shape
    v = cot_t.shape[0] // n
    for f in range(n):
        out[f, :rows, :] = tok[:, f * piece:(f + 1) * piece]
        out[f, rows:, :rows] = cot_t[f * v:f * v + v // 2, :]
        out[f, rows:, rows:] = cot_t[f * v + v // 2:(f + 1) * v, :]


def pack(tokens, cot_t, n):
    rows, width = tokens.shape
    piece, v = width // n, cot_t.shape[0] // n
    tall = rows + v * rows // piece
    return call(
        pack_kernel,
        "pack",
        moved=4 * rows * width,
        vmem=VMEM_MOST,
        grid=(n // GROUP,),
        in_specs=[
            pl.BlockSpec((rows, GROUP * piece), lambda f: (0, f)),
            pl.BlockSpec((GROUP * v, rows), lambda f: (f, 0)),
        ],
        out_specs=pl.BlockSpec((GROUP, tall, piece), lambda f: (f, 0, 0)),
        out_shape=jax.ShapeDtypeStruct((n, tall, piece), BF),
    )(tokens, cot_t)


def offer_kernel(slots, meta, down_t, up, keep, give):
    piece, v = down_t.shape[2], up.shape[2]
    keep[...] = jnp.zeros_like(keep)
    give[...] = jnp.zeros_like(give)
    for z in range(keep.shape[0]):
        for out, core in ((keep, meta[CORE]), (give, 1 - meta[CORE])):
            r = jnp.maximum(wanted_by(meta, 2 * z + core, slots), 0)
            out[z, :, :piece] = down_t[r]
            out[z, :, piece:piece + v] = up[r]


def offer(meta, down_t, up, chips, slots):
    _, rank, piece = down_t.shape
    shape = (chips, rank, piece + 128)
    return call(
        functools.partial(offer_kernel, slots),
        "offer",
        moved=8 * chips * rank * piece,
        grid_spec=with_meta(
            (1,), [whole(down_t.shape), whole(up.shape)], [whole(shape), whole(shape)]
        ),
        out_shape=[jax.ShapeDtypeStruct(shape, BF)] * 2,
    )(meta, down_t, up)


def merge_kernel(meta, keep, taken, *outs):
    chips = len(outs)
    for k, out in enumerate(outs):
        z = lax.rem(meta[CHIP] + k, chips)
        out[meta[CORE]] = keep[z]
        out[1 - meta[CORE]] = taken[z]


def merge(meta, keep, taken):
    chips, rank, wide = keep.shape
    shape = (2, rank, wide)
    return call(
        merge_kernel,
        "merge",
        moved=4 * keep.size,
        grid_spec=with_meta(
            (1,), [whole(keep.shape), whole(taken.shape)], [whole(shape)] * chips
        ),
        out_shape=[jax.ShapeDtypeStruct(shape, BF)] * chips,
    )(meta, keep, taken)


def choose_kernel(slots, meta, *refs):
    chips = len(refs) - 3
    got, (down, turned, up) = refs[:chips], refs[chips:]
    piece, v, rank = down.shape[2], up.shape[0], down.shape[1]
    for k in range(chips):
        z = lax.rem(meta[CHIP] + chips - k, chips)
        for core in range(2):
            s = segment_at(meta, 2 * z + core, slots, 2 * chips)

            @pl.when(s >= 0)
            def _():
                down[s] = got[k][core]

    for p in range(slots // 2):
        pair = jnp.concatenate([down[2 * p], down[2 * p + 1]], axis=0).astype(F32)
        cols = slice(2 * rank * p, 2 * rank * (p + 1))
        turned[:, cols] = jnp.transpose(pair[:, :turned.shape[0]]).astype(BF)
        up[:, cols] = jnp.transpose(pair[:, turned.shape[0]:])[:v].astype(BF)


def choose(meta, got, slots, v):
    _, rank, wide = got[0].shape
    piece = wide - 128
    shapes = [(slots, rank, wide), (piece, slots * rank), (v, slots * rank)]
    return call(
        functools.partial(choose_kernel, slots),
        "choose",
        moved=4 * slots * rank * wide,
        grid_spec=with_meta((1,), [whole(g.shape) for g in got], [whole(s) for s in shapes]),
        out_shape=[jax.ShapeDtypeStruct(s, BF) for s in shapes],
    )(meta, *got)


def cot_of(part, rows):
    return jnp.concatenate([part[rows:, :rows], part[rows:, rows:]], axis=0)


def project_kernel(slots, rank, meta, part, down_t, up_t, out):
    group, rows, _ = out.shape
    shape = (rows, 2 * rank)
    low = lax.broadcasted_iota(jnp.int32, shape, 1) < rank
    for g in range(group):
        first = (pl.program_id(0) * group + g) * rows
        block = part[g]
        lr = jnp.dot(block[:rows], down_t[...], preferred_element_type=F32)
        lg = lax.dot_general(
            cot_of(block, rows), up_t[...], (((0,), (0,)), ((), ())), preferred_element_type=F32
        )
        lr_sum = jnp.zeros(shape, F32)
        lg_sum = jnp.zeros(shape, F32)
        for p in range(slots // 2):
            keep = inside_pair(meta, p, first, shape, slots, rank)
            cols = slice(2 * rank * p, 2 * rank * (p + 1))
            lr_sum += jnp.where(keep, lr[:, cols], 0.0)
            lg_sum += jnp.where(keep, lg[:, cols], 0.0)
        lr_sum += pltpu.roll(lr_sum, rank, 1)
        lg_sum += pltpu.roll(lg_sum, rank, 1)
        out[g] = jnp.where(low, lr_sum, ADAPTER_SCALE * lg_sum).astype(BF)


def project(meta, parts, down_t, up_t, rows, slots, rank):
    n, tall, piece = parts.shape
    return call(
        functools.partial(project_kernel, slots, rank),
        "project",
        flops=2 * n * rows * piece * slots * rank,
        moved=2 * n * tall * piece,
        grid_spec=with_meta(
            (n // GROUP,),
            [
                pl.BlockSpec((GROUP, tall, piece), lambda j, m: (j, 0, 0)),
                whole(down_t.shape),
                whole(up_t.shape),
            ],
            pl.BlockSpec((GROUP, rows, 2 * rank), lambda j, m: (j, 0, 0)),
        ),
        out_shape=jax.ShapeDtypeStruct((n, rows, 2 * rank), BF),
    )(meta, parts, down_t, up_t)


def total_kernel(parts, copies):
    acc = parts[0].astype(F32)
    for f in range(1, parts.shape[0]):
        acc += parts[f].astype(F32)
    turned = jnp.transpose(acc).astype(BF)
    for f in range(copies.shape[0]):
        copies[f] = turned


def total(parts):
    n, rows, wide = parts.shape
    return call(
        total_kernel,
        "total",
        moved=4 * parts.size,
        out_shape=jax.ShapeDtypeStruct((n, wide, rows), BF),
    )(parts)


def gradient_kernel(slots, rank, v, meta, part, low, keep, give, acc_down, acc_up):
    group, _, rows = low.shape
    step = pl.program_id(0)

    @pl.when(step == 0)
    def _():
        acc_down[...] = jnp.zeros_like(acc_down)
        acc_up[...] = jnp.zeros_like(acc_up)

    for g in range(group):
        first = (step * group + g) * rows
        for s in range(slots):
            start, end = start_of(meta, s), end_of(meta, s, slots)

            @pl.when((start < first + rows) & (end > first))
            def _():
                token = first + lax.broadcasted_iota(jnp.int32, (2 * rank, rows), 1)
                both = low[g].astype(F32)
                both = jnp.where((token >= start) & (token < end), both, 0.0).astype(BF)
                at = slice(s * rank, (s + 1) * rank)
                acc_down[at, :] += jnp.dot(
                    both[rank:], part[g, :rows, :], preferred_element_type=F32
                )
                acc_up[at, :] += lax.dot_general(
                    both[:rank],
                    cot_of(part[g], rows),
                    (((1,), (1,)), ((), ())),
                    preferred_element_type=F32,
                )

    @pl.when(step == pl.num_programs(0) - 1)
    def _():
        piece = acc_down.shape[1]
        keep[...] = jnp.zeros_like(keep)
        give[...] = jnp.zeros_like(give)
        for s in range(slots):
            owner = owner_of(meta, s, slots)
            chip, same = owner // 2, lax.rem(owner, 2) == meta[CORE]
            rows_of = slice(s * rank, (s + 1) * rank)

            def put(out):
                out[chip, :, :piece] = acc_down[rows_of, :].astype(BF)
                out[chip, :, piece:piece + v] = (ADAPTER_SCALE * acc_up[rows_of, :]).astype(BF)

            pl.when(same)(functools.partial(put, keep))
            pl.when(jnp.logical_not(same))(functools.partial(put, give))


def gradient(meta, parts, low, chips, slots, rank, v):
    n, tall, piece = parts.shape
    rows = low.shape[2]
    shape = (chips, rank, piece + 128)
    return call(
        functools.partial(gradient_kernel, slots, rank, v),
        "gradient",
        flops=2 * n * rows * piece * slots * rank,
        moved=2 * n * tall * piece,
        grid_spec=with_meta(
            (n // GROUP,),
            [
                pl.BlockSpec((GROUP, tall, piece), lambda j, m: (j, 0, 0)),
                pl.BlockSpec((GROUP, 2 * rank, rows), lambda j, m: (j, 0, 0)),
            ],
            [whole(shape), whole(shape)],
            [pltpu.VMEM((slots * rank, piece), F32), pltpu.VMEM((slots * rank, v), F32)],
        ),
        out_shape=[jax.ShapeDtypeStruct(shape, BF)] * 2,
    )(meta, parts, low)


def collect_kernel(slots, scale, meta, *refs):
    got, (down, up) = refs[:-2], refs[-2:]
    chips = len(got)
    piece, v = down.shape[2], up.shape[2]
    down[...] = jnp.zeros_like(down)
    up[...] = jnp.zeros_like(up)
    for k in range(chips):
        z = lax.rem(meta[CHIP] + chips - k, chips)
        for core in range(2):
            r = wanted_by(meta, 2 * z + core, slots)

            @pl.when(r >= 0)
            def _():
                down[r] += got[k][core, :, :piece].astype(F32) * scale
                up[r] += got[k][core, :, piece:piece + v].astype(F32) * scale


def collect(meta, got, rows, v, slots, scale):
    _, rank, wide = got[0].shape
    shapes = [(rows, rank, wide - 128), (rows, rank, v)]
    return call(
        functools.partial(collect_kernel, slots, scale),
        "collect",
        moved=2 * len(got) * got[0].size,
        grid_spec=with_meta((1,), [whole(g.shape) for g in got], [whole(s) for s in shapes]),
        out_shape=[jax.ShapeDtypeStruct(s, F32) for s in shapes],
    )(meta, *got)


def term_kernel(slots, rank, meta, low, down, out):
    group, _, rows = low.shape
    piece = out.shape[2]
    table = jnp.concatenate([down[s, :, :piece] for s in range(slots)], axis=0)
    for g in range(group):
        first = (pl.program_id(0) * group + g) * rows
        lg = low[g, rank:, :].astype(F32)
        lg = jnp.transpose(jnp.concatenate([lg, lg], axis=0))
        lg = [
            jnp.where(inside_pair(meta, p, first, lg.shape, slots, rank), lg, 0.0)
            for p in range(slots // 2)
        ]
        lg = jnp.concatenate(lg, axis=1).astype(BF)
        out[g] = jnp.dot(lg, table, preferred_element_type=F32).astype(BF)


def term(meta, low, down, piece, slots, rank):
    n, wide, rows = low.shape
    return call(
        functools.partial(term_kernel, slots, rank),
        "term",
        flops=2 * n * rows * piece * slots * rank,
        moved=2 * n * rows * piece,
        vmem=VMEM_MOST,
        grid_spec=with_meta(
            (n // GROUP,),
            [pl.BlockSpec((GROUP, wide, rows), lambda j, m: (j, 0, 0)), whole(down.shape)],
            pl.BlockSpec((GROUP, rows, piece), lambda j, m: (j, 0, 0)),
        ),
        out_shape=jax.ShapeDtypeStruct((n, rows, piece), BF),
    )(meta, low, down)


def base_kernel(meta, cot, w, out):
    out[...] = jnp.dot(
        cot[...],
        jnp.concatenate([w[e, 0] for e in range(w.shape[0])], axis=0),
        preferred_element_type=F32,
    )


def base(meta, cot, w):
    slices, n, part, piece = w.shape
    rows, width = cot.shape

    def place(f, m):
        y = lax.rem(m[PIECE] // SIDE + SIDE - f // SIDE, SIDE)
        x = lax.rem(lax.rem(m[PIECE], SIDE) + SIDE - lax.rem(f, SIDE), SIDE)
        return (0, y * SIDE + x)

    return call(
        base_kernel,
        "base",
        flops=2 * rows * n * piece * width,
        moved=2 * n * piece * width + 4 * rows * n * piece,
        vmem=VMEM_MOST,
        grid_spec=with_meta(
            (n,),
            [
                whole(cot.shape),
                pl.BlockSpec((slices, 1, part, piece), lambda f, m: (0, f, 0, 0)),
            ],
            pl.BlockSpec((rows, piece), place),
        ),
        out_shape=jax.ShapeDtypeStruct((rows, n * piece), F32),
    )(meta, cot, w)


def join_kernel(done, terms, out):
    group, _, piece = terms.shape
    for g in range(group):
        cols = slice(g * piece, (g + 1) * piece)
        out[:, cols] = (done[:, cols] + terms[g].astype(F32)).astype(BF)


def join(done, terms):
    n, rows, piece = terms.shape
    group = 2
    return call(
        join_kernel,
        "join",
        moved=8 * n * rows * piece,
        vmem=VMEM_MOST,
        grid=(n // group,),
        in_specs=[
            pl.BlockSpec((rows, group * piece), lambda f: (0, f)),
            pl.BlockSpec((group, rows, piece), lambda f: (f, 0, 0)),
        ],
        out_specs=pl.BlockSpec((rows, group * piece), lambda f: (0, f)),
        out_shape=jax.ShapeDtypeStruct((rows, n * piece), BF),
    )(done, terms)


def exchange(x, axis):
    return lax.all_to_all(x, axis, 0, 0, tiled=True)


def swap(x, bins):
    return lax.ppermute(x, "dp", [(i, i ^ 1) for i in range(bins)])


def shift(x, k, bins):
    chips = bins // 2
    return lax.ppermute(
        x, "dp", [(i, (i // 2 + k) % chips * 2 + i % 2) for i in range(bins)]
    )


def spread(meta, keep, give, bins):
    blocks = merge(meta, keep, swap(give, bins))
    return [blocks[0]] + [shift(blocks[k], k, bins) for k in range(1, bins // 2)]


def across(x, dy, dx, n):
    return lax.ppermute(
        x,
        "fsdp",
        [
            (i, (i // SIDE + dy) % SIDE * SIDE + (i % SIDE + dx) % SIDE)
            for i in range(n)
        ],
    )


def scalars(segment_tenant, segment_lengths, tenant_stored_row, own):
    bins, slots = segment_tenant.shape
    me = lax.axis_index("dp")
    tenants = jnp.arange(tenant_stored_row.shape[0], dtype=jnp.int32)
    stored = jnp.sum(
        jnp.where(segment_tenant[:, :, None] == tenants, tenant_stored_row, 0), axis=2
    )
    owners = lax.dynamic_index_in_dim(stored, me, 0, keepdims=False) // own
    lengths = lax.dynamic_index_in_dim(segment_lengths, me, 0, keepdims=False)
    place = jnp.arange(slots, dtype=jnp.int32)
    starts = jnp.sum(jnp.where(place[None, :] < place[:, None], lengths[None, :], 0), axis=1)
    wanted = jnp.max(jnp.where(stored // own == me, stored % own, -1), axis=1)
    every = jnp.arange(bins, dtype=jnp.int32)
    segment = jnp.max(jnp.where(owners[None, :] == every[:, None], place[None, :], -1), axis=1)
    head = jnp.stack([me % 2, me // 2, lax.axis_index("fsdp")])
    return jnp.concatenate([head, starts, starts + lengths, owners, wanted, segment]).astype(
        jnp.int32
    )


def local(
    tokens,
    cotangent,
    value_weight,
    adapter_down_weight,
    adapter_up_weight,
    segment_tenant,
    segment_lengths,
    tenant_stored_row,
):
    own, piece, rank = adapter_down_weight.shape
    v = adapter_up_weight.shape[2]
    bins, slots = segment_tenant.shape
    chips = bins // 2
    rows = tokens.shape[0]
    n = lax.axis_size("fsdp")
    scale = (n * rows) ** (-0.5)
    meta = scalars(segment_tenant, segment_lengths, tenant_stored_row, own)

    me = lax.axis_index("dp").astype(jnp.int32).reshape(1)
    mine = turn(me, value_weight, bins)[None]
    near = [across(mine, 0, k, n) for k in range(1, SIDE)]
    packed = pack(tokens, jnp.swapaxes(cotangent, 0, 1), n)
    packed, near, mine = lax.optimization_barrier((packed, near, mine))
    mine = jnp.concatenate([mine] + near)
    near = [across(mine, k, 0, n) for k in range(1, SIDE)]
    keep, give = offer(
        meta, jnp.swapaxes(adapter_down_weight, 1, 2), adapter_up_weight, chips, slots
    )
    packed, keep, give, near, mine = lax.optimization_barrier((packed, keep, give, near, mine))
    weight = lax.all_gather(jnp.concatenate([mine] + near), "dp", axis=0)

    parts = exchange(packed, "fsdp")
    got = spread(meta, keep, give, bins)
    parts, got = lax.optimization_barrier((parts, got))
    down, down_t, up_t = choose(meta, got, slots, v)

    sums = exchange(project(meta, parts, down_t, up_t, rows, slots, rank), "fsdp")
    low_all = exchange(total(sums), "fsdp")
    terms = term(meta, low_all, down, piece, slots, rank)
    terms, low_all = lax.optimization_barrier((terms, low_all))
    terms = exchange(terms, "fsdp")
    sent = spread(meta, *gradient(meta, parts, low_all, chips, slots, rank, v), bins)
    done = base(meta, cotangent, weight)
    sent, done = lax.optimization_barrier((sent, done))
    down_grad, up_grad = collect(meta, sent, own, v, slots, scale)
    terms, down_grad, up_grad = lax.optimization_barrier((terms, down_grad, up_grad))
    return join(done, terms), jnp.swapaxes(down_grad, 1, 2), up_grad


def solution(mesh):
    placed = (
        P(("dp", "fsdp"), None),
        P(("dp", "fsdp"), None),
        P("fsdp", None),
        P("dp", "fsdp", None),
        P("dp", None, "fsdp"),
        P(),
        P(),
        P(),
    )
    return jax.shard_map(
        local,
        mesh=mesh,
        in_specs=placed,
        out_specs=(P(("dp", "fsdp"), None), P("dp", "fsdp", None), P("dp", None, "fsdp")),
        check_vma=False,
    )
```

```python
import functools

import jax
import jax.numpy as jnp
from jax import lax
from jax.experimental import pallas as pl
from jax.experimental.pallas import tpu as pltpu
from jax.sharding import PartitionSpec as P

ADAPTER_SCALE = 2.0
BF = jnp.bfloat16
F32 = jnp.float32
VMEM_BYTES = 40 * 1024 * 1024
VMEM_MOST = 58 * 1024 * 1024
GROUP = 4
SIDE = 4
CORE, CHIP, PIECE, LIST = 0, 1, 2, 3


def call(kernel, name, flops=0, moved=0, vmem=VMEM_BYTES, **kw):
    return pl.pallas_call(
        kernel,
        compiler_params=pltpu.CompilerParams(vmem_limit_bytes=vmem),
        cost_estimate=pl.CostEstimate(flops=flops, bytes_accessed=moved, transcendentals=0),
        name=name,
        **kw,
    )


def whole(shape):
    return pl.BlockSpec(shape, lambda i, m: (0,) * len(shape))


def with_meta(grid, in_specs, out_specs, scratch=()):
    return pltpu.PrefetchScalarGridSpec(
        num_scalar_prefetch=1,
        grid=grid,
        in_specs=in_specs,
        out_specs=out_specs,
        scratch_shapes=list(scratch),
    )


def start_of(meta, s):
    return meta[LIST + s]


def end_of(meta, s, slots):
    return meta[LIST + slots + s]


def owner_of(meta, s, slots):
    return meta[LIST + 2 * slots + s]


def wanted_by(meta, b, slots):
    return meta[LIST + 3 * slots + b]


def segment_at(meta, owner, slots, bins):
    return meta[LIST + 3 * slots + bins + owner]


def inside_pair(meta, pair, first, shape, slots, rank):
    row = first + lax.broadcasted_iota(jnp.int32, shape, 0)
    low = lax.broadcasted_iota(jnp.int32, shape, 1) < rank
    begin = jnp.where(low, start_of(meta, 2 * pair), start_of(meta, 2 * pair + 1))
    end = jnp.where(low, end_of(meta, 2 * pair, slots), end_of(meta, 2 * pair + 1, slots))
    return (row >= begin) & (row < end)


def turn_kernel(at, w, out):
    both = jnp.transpose(w[...].astype(F32)).astype(BF)
    part = out.shape[0]
    low = lax.rem(at[0], 2) == 0
    out[...] = jnp.where(low, both[:part], both[part:])


def turn(at, w, slices):
    piece, width = w.shape
    part = width // slices
    return call(
        turn_kernel,
        "turn",
        moved=4 * part * piece,
        grid_spec=with_meta(
            (1,),
            [pl.BlockSpec((piece, 2 * part), lambda i, m: (0, m[0] // 2))],
            whole((part, piece)),
        ),
        out_shape=jax.ShapeDtypeStruct((part, piece), BF),
    )(at, w)


def pack_kernel(tok, cot_t, out):
    rows = tok.shape[0]
    n, _, piece = out.shape
    v = cot_t.shape[0] // n
    for f in range(n):
        out[f, :rows, :] = tok[:, f * piece:(f + 1) * piece]
        out[f, rows:, :rows] = cot_t[f * v:f * v + v // 2, :]
        out[f, rows:, rows:] = cot_t[f * v + v // 2:(f + 1) * v, :]


def pack(tokens, cot_t, n):
    rows, width = tokens.shape
    piece, v = width // n, cot_t.shape[0] // n
    tall = rows + v * rows // piece
    return call(
        pack_kernel,
        "pack",
        moved=4 * rows * width,
        vmem=VMEM_MOST,
        grid=(n // GROUP,),
        in_specs=[
            pl.BlockSpec((rows, GROUP * piece), lambda f: (0, f)),
            pl.BlockSpec((GROUP * v, rows), lambda f: (f, 0)),
        ],
        out_specs=pl.BlockSpec((GROUP, tall, piece), lambda f: (f, 0, 0)),
        out_shape=jax.ShapeDtypeStruct((n, tall, piece), BF),
    )(tokens, cot_t)


def offer_kernel(slots, meta, down_t, up, keep, give):
    piece, v = down_t.shape[2], up.shape[2]
    keep[...] = jnp.zeros_like(keep)
    give[...] = jnp.zeros_like(give)
    for z in range(keep.shape[0]):
        for out, core in ((keep, meta[CORE]), (give, 1 - meta[CORE])):
            r = jnp.maximum(wanted_by(meta, 2 * z + core, slots), 0)
            out[z, :, :piece] = down_t[r]
            out[z, :, piece:piece + v] = up[r]


def offer(meta, down_t, up, chips, slots):
    _, rank, piece = down_t.shape
    shape = (chips, rank, piece + 128)
    return call(
        functools.partial(offer_kernel, slots),
        "offer",
        moved=8 * chips * rank * piece,
        grid_spec=with_meta(
            (1,), [whole(down_t.shape), whole(up.shape)], [whole(shape), whole(shape)]
        ),
        out_shape=[jax.ShapeDtypeStruct(shape, BF)] * 2,
    )(meta, down_t, up)


def merge_kernel(meta, keep, taken, *outs):
    chips = len(outs)
    for k, out in enumerate(outs):
        z = lax.rem(meta[CHIP] + k, chips)
        out[meta[CORE]] = keep[z]
        out[1 - meta[CORE]] = taken[z]


def merge(meta, keep, taken):
    chips, rank, wide = keep.shape
    shape = (2, rank, wide)
    return call(
        merge_kernel,
        "merge",
        moved=4 * keep.size,
        grid_spec=with_meta(
            (1,), [whole(keep.shape), whole(taken.shape)], [whole(shape)] * chips
        ),
        out_shape=[jax.ShapeDtypeStruct(shape, BF)] * chips,
    )(meta, keep, taken)


def choose_kernel(slots, meta, *refs):
    chips = len(refs) - 3
    got, (down, turned, up) = refs[:chips], refs[chips:]
    piece, v, rank = down.shape[2], up.shape[0], down.shape[1]
    for k in range(chips):
        z = lax.rem(meta[CHIP] + chips - k, chips)
        for core in range(2):
            s = segment_at(meta, 2 * z + core, slots, 2 * chips)

            @pl.when(s >= 0)
            def _():
                down[s] = got[k][core]

    for p in range(slots // 2):
        pair = jnp.concatenate([down[2 * p], down[2 * p + 1]], axis=0).astype(F32)
        cols = slice(2 * rank * p, 2 * rank * (p + 1))
        turned[:, cols] = jnp.transpose(pair[:, :turned.shape[0]]).astype(BF)
        up[:, cols] = jnp.transpose(pair[:, turned.shape[0]:])[:v].astype(BF)


def choose(meta, got, slots, v):
    _, rank, wide = got[0].shape
    piece = wide - 128
    shapes = [(slots, rank, wide), (piece, slots * rank), (v, slots * rank)]
    return call(
        functools.partial(choose_kernel, slots),
        "choose",
        moved=4 * slots * rank * wide,
        grid_spec=with_meta((1,), [whole(g.shape) for g in got], [whole(s) for s in shapes]),
        out_shape=[jax.ShapeDtypeStruct(s, BF) for s in shapes],
    )(meta, *got)


def cot_of(part, rows):
    return jnp.concatenate([part[rows:, :rows], part[rows:, rows:]], axis=0)


def project_kernel(slots, rank, meta, part, down_t, up_t, out):
    group, rows, _ = out.shape
    shape = (rows, 2 * rank)
    low = lax.broadcasted_iota(jnp.int32, shape, 1) < rank
    for g in range(group):
        first = (pl.program_id(0) * group + g) * rows
        block = part[g]
        lr = jnp.dot(block[:rows], down_t[...], preferred_element_type=F32)
        lg = lax.dot_general(
            cot_of(block, rows), up_t[...], (((0,), (0,)), ((), ())), preferred_element_type=F32
        )
        lr_sum = jnp.zeros(shape, F32)
        lg_sum = jnp.zeros(shape, F32)
        for p in range(slots // 2):
            keep = inside_pair(meta, p, first, shape, slots, rank)
            cols = slice(2 * rank * p, 2 * rank * (p + 1))
            lr_sum += jnp.where(keep, lr[:, cols], 0.0)
            lg_sum += jnp.where(keep, lg[:, cols], 0.0)
        lr_sum += pltpu.roll(lr_sum, rank, 1)
        lg_sum += pltpu.roll(lg_sum, rank, 1)
        out[g] = jnp.where(low, lr_sum, ADAPTER_SCALE * lg_sum).astype(BF)


def project(meta, parts, down_t, up_t, rows, slots, rank):
    n, tall, piece = parts.shape
    return call(
        functools.partial(project_kernel, slots, rank),
        "project",
        flops=2 * n * rows * piece * slots * rank,
        moved=2 * n * tall * piece,
        grid_spec=with_meta(
            (n // GROUP,),
            [
                pl.BlockSpec((GROUP, tall, piece), lambda j, m: (j, 0, 0)),
                whole(down_t.shape),
                whole(up_t.shape),
            ],
            pl.BlockSpec((GROUP, rows, 2 * rank), lambda j, m: (j, 0, 0)),
        ),
        out_shape=jax.ShapeDtypeStruct((n, rows, 2 * rank), BF),
    )(meta, parts, down_t, up_t)


def total_kernel(parts, copies):
    acc = parts[0].astype(F32)
    for f in range(1, parts.shape[0]):
        acc += parts[f].astype(F32)
    turned = jnp.transpose(acc).astype(BF)
    for f in range(copies.shape[0]):
        copies[f] = turned


def total(parts):
    n, rows, wide = parts.shape
    return call(
        total_kernel,
        "total",
        moved=4 * parts.size,
        out_shape=jax.ShapeDtypeStruct((n, wide, rows), BF),
    )(parts)


def gradient_kernel(slots, rank, v, meta, part, low, keep, give, acc_down, acc_up):
    group, _, rows = low.shape
    step = pl.program_id(0)

    @pl.when(step == 0)
    def _():
        acc_down[...] = jnp.zeros_like(acc_down)
        acc_up[...] = jnp.zeros_like(acc_up)

    for g in range(group):
        first = (step * group + g) * rows
        for s in range(slots):
            start, end = start_of(meta, s), end_of(meta, s, slots)

            @pl.when((start < first + rows) & (end > first))
            def _():
                token = first + lax.broadcasted_iota(jnp.int32, (2 * rank, rows), 1)
                both = low[g].astype(F32)
                both = jnp.where((token >= start) & (token < end), both, 0.0).astype(BF)
                at = slice(s * rank, (s + 1) * rank)
                acc_down[at, :] += jnp.dot(
                    both[rank:], part[g, :rows, :], preferred_element_type=F32
                )
                acc_up[at, :] += lax.dot_general(
                    both[:rank],
                    cot_of(part[g], rows),
                    (((1,), (1,)), ((), ())),
                    preferred_element_type=F32,
                )

    @pl.when(step == pl.num_programs(0) - 1)
    def _():
        piece = acc_down.shape[1]
        keep[...] = jnp.zeros_like(keep)
        give[...] = jnp.zeros_like(give)
        for s in range(slots):
            owner = owner_of(meta, s, slots)
            chip, same = owner // 2, lax.rem(owner, 2) == meta[CORE]
            rows_of = slice(s * rank, (s + 1) * rank)

            def put(out):
                out[chip, :, :piece] = acc_down[rows_of, :].astype(BF)
                out[chip, :, piece:piece + v] = (ADAPTER_SCALE * acc_up[rows_of, :]).astype(BF)

            pl.when(same)(functools.partial(put, keep))
            pl.when(jnp.logical_not(same))(functools.partial(put, give))


def gradient(meta, parts, low, chips, slots, rank, v):
    n, tall, piece = parts.shape
    rows = low.shape[2]
    shape = (chips, rank, piece + 128)
    return call(
        functools.partial(gradient_kernel, slots, rank, v),
        "gradient",
        flops=2 * n * rows * piece * slots * rank,
        moved=2 * n * tall * piece,
        grid_spec=with_meta(
            (n // GROUP,),
            [
                pl.BlockSpec((GROUP, tall, piece), lambda j, m: (j, 0, 0)),
                pl.BlockSpec((GROUP, 2 * rank, rows), lambda j, m: (j, 0, 0)),
            ],
            [whole(shape), whole(shape)],
            [pltpu.VMEM((slots * rank, piece), F32), pltpu.VMEM((slots * rank, v), F32)],
        ),
        out_shape=[jax.ShapeDtypeStruct(shape, BF)] * 2,
    )(meta, parts, low)


def collect_kernel(slots, scale, meta, *refs):
    got, (down, up) = refs[:-2], refs[-2:]
    chips = len(got)
    piece, v = down.shape[2], up.shape[2]
    down[...] = jnp.zeros_like(down)
    up[...] = jnp.zeros_like(up)
    for k in range(chips):
        z = lax.rem(meta[CHIP] + chips - k, chips)
        for core in range(2):
            r = wanted_by(meta, 2 * z + core, slots)

            @pl.when(r >= 0)
            def _():
                down[r] += got[k][core, :, :piece].astype(F32) * scale
                up[r] += got[k][core, :, piece:piece + v].astype(F32) * scale


def collect(meta, got, rows, v, slots, scale):
    _, rank, wide = got[0].shape
    shapes = [(rows, rank, wide - 128), (rows, rank, v)]
    return call(
        functools.partial(collect_kernel, slots, scale),
        "collect",
        moved=2 * len(got) * got[0].size,
        grid_spec=with_meta((1,), [whole(g.shape) for g in got], [whole(s) for s in shapes]),
        out_shape=[jax.ShapeDtypeStruct(s, F32) for s in shapes],
    )(meta, *got)


def term_kernel(slots, rank, meta, low, down, out):
    group, _, rows = low.shape
    piece = out.shape[2]
    table = jnp.concatenate([down[s, :, :piece] for s in range(slots)], axis=0)
    for g in range(group):
        first = (pl.program_id(0) * group + g) * rows
        lg = low[g, rank:, :].astype(F32)
        lg = jnp.transpose(jnp.concatenate([lg, lg], axis=0))
        lg = [
            jnp.where(inside_pair(meta, p, first, lg.shape, slots, rank), lg, 0.0)
            for p in range(slots // 2)
        ]
        lg = jnp.concatenate(lg, axis=1).astype(BF)
        out[g] = jnp.dot(lg, table, preferred_element_type=F32).astype(BF)


def term(meta, low, down, piece, slots, rank):
    n, wide, rows = low.shape
    return call(
        functools.partial(term_kernel, slots, rank),
        "term",
        flops=2 * n * rows * piece * slots * rank,
        moved=2 * n * rows * piece,
        vmem=VMEM_MOST,
        grid_spec=with_meta(
            (n // GROUP,),
            [pl.BlockSpec((GROUP, wide, rows), lambda j, m: (j, 0, 0)), whole(down.shape)],
            pl.BlockSpec((GROUP, rows, piece), lambda j, m: (j, 0, 0)),
        ),
        out_shape=jax.ShapeDtypeStruct((n, rows, piece), BF),
    )(meta, low, down)


def base_kernel(meta, cot, w, out):
    slices, group, _, piece = w.shape
    dx = lax.rem(pl.program_id(0) * group, SIDE)
    for g in range(group):
        x = lax.rem(lax.rem(meta[PIECE], SIDE) + SIDE - dx - g, SIDE)
        r = jnp.dot(
            cot[...],
            jnp.concatenate([w[e, g] for e in range(slices)], axis=0),
            preferred_element_type=F32,
        )
        out[:, pl.ds(pl.multiple_of(x * piece, piece), piece)] = r.astype(BF)


def base(meta, cot, w):
    slices, n, part, piece = w.shape
    rows, width = cot.shape
    group = SIDE // 2

    def place(f, m):
        return (0, lax.rem(m[PIECE] // SIDE + SIDE - f * group // SIDE, SIDE))

    return call(
        base_kernel,
        "base",
        flops=2 * rows * n * piece * width,
        moved=2 * n * piece * (width + rows),
        vmem=VMEM_MOST,
        grid_spec=with_meta(
            (n // group,),
            [
                whole(cot.shape),
                pl.BlockSpec((slices, group, part, piece), lambda f, m: (0, f, 0, 0)),
            ],
            pl.BlockSpec((rows, SIDE * piece), place),
        ),
        out_shape=jax.ShapeDtypeStruct((rows, n * piece), BF),
    )(meta, cot, w)


def join_kernel(done, terms, out):
    group, _, piece = terms.shape
    for g in range(group):
        cols = slice(g * piece, (g + 1) * piece)
        out[:, cols] = (done[:, cols].astype(F32) + terms[g].astype(F32)).astype(BF)


def join(done, terms):
    n, rows, piece = terms.shape
    return call(
        join_kernel,
        "join",
        moved=6 * n * rows * piece,
        vmem=VMEM_MOST,
        grid=(n // GROUP,),
        in_specs=[
            pl.BlockSpec((rows, GROUP * piece), lambda f: (0, f)),
            pl.BlockSpec((GROUP, rows, piece), lambda f: (f, 0, 0)),
        ],
        out_specs=pl.BlockSpec((rows, GROUP * piece), lambda f: (0, f)),
        out_shape=jax.ShapeDtypeStruct((rows, n * piece), BF),
    )(done, terms)


def exchange(x, axis):
    return lax.all_to_all(x, axis, 0, 0, tiled=True)


def swap(x, bins):
    return lax.ppermute(x, "dp", [(i, i ^ 1) for i in range(bins)])


def shift(x, k, bins):
    chips = bins // 2
    return lax.ppermute(
        x, "dp", [(i, (i // 2 + k) % chips * 2 + i % 2) for i in range(bins)]
    )


def spread(meta, keep, give, bins):
    blocks = merge(meta, keep, swap(give, bins))
    return [blocks[0]] + [shift(blocks[k], k, bins) for k in range(1, bins // 2)]


def across(x, dy, dx, n):
    return lax.ppermute(
        x,
        "fsdp",
        [
            (i, (i // SIDE + dy) % SIDE * SIDE + (i % SIDE + dx) % SIDE)
            for i in range(n)
        ],
    )


def scalars(segment_tenant, segment_lengths, tenant_stored_row, own):
    bins, slots = segment_tenant.shape
    me = lax.axis_index("dp")
    tenants = jnp.arange(tenant_stored_row.shape[0], dtype=jnp.int32)
    stored = jnp.sum(
        jnp.where(segment_tenant[:, :, None] == tenants, tenant_stored_row, 0), axis=2
    )
    owners = lax.dynamic_index_in_dim(stored, me, 0, keepdims=False) // own
    lengths = lax.dynamic_index_in_dim(segment_lengths, me, 0, keepdims=False)
    place = jnp.arange(slots, dtype=jnp.int32)
    starts = jnp.sum(jnp.where(place[None, :] < place[:, None], lengths[None, :], 0), axis=1)
    wanted = jnp.max(jnp.where(stored // own == me, stored % own, -1), axis=1)
    every = jnp.arange(bins, dtype=jnp.int32)
    segment = jnp.max(jnp.where(owners[None, :] == every[:, None], place[None, :], -1), axis=1)
    head = jnp.stack([me % 2, me // 2, lax.axis_index("fsdp")])
    return jnp.concatenate([head, starts, starts + lengths, owners, wanted, segment]).astype(
        jnp.int32
    )


def local(
    tokens,
    cotangent,
    value_weight,
    adapter_down_weight,
    adapter_up_weight,
    segment_tenant,
    segment_lengths,
    tenant_stored_row,
):
    own, piece, rank = adapter_down_weight.shape
    v = adapter_up_weight.shape[2]
    bins, slots = segment_tenant.shape
    chips = bins // 2
    rows = tokens.shape[0]
    n = lax.axis_size("fsdp")
    scale = (n * rows) ** (-0.5)
    meta = scalars(segment_tenant, segment_lengths, tenant_stored_row, own)

    me = lax.axis_index("dp").astype(jnp.int32).reshape(1)
    mine = turn(me, value_weight, bins)[None]
    near = [across(mine, 0, k, n) for k in range(1, SIDE)]
    mine = jnp.concatenate([mine] + near)
    near = [across(mine, k, 0, n) for k in range(1, SIDE)]
    packed = pack(tokens, jnp.swapaxes(cotangent, 0, 1), n)
    keep, give = offer(
        meta, jnp.swapaxes(adapter_down_weight, 1, 2), adapter_up_weight, chips, slots
    )
    packed, keep, give, near, mine = lax.optimization_barrier((packed, keep, give, near, mine))
    weight = lax.all_gather(jnp.concatenate([mine] + near), "dp", axis=0)

    parts = exchange(packed, "fsdp")
    got = spread(meta, keep, give, bins)
    parts, got = lax.optimization_barrier((parts, got))
    down, down_t, up_t = choose(meta, got, slots, v)

    sums = exchange(project(meta, parts, down_t, up_t, rows, slots, rank), "fsdp")
    low_all = exchange(total(sums), "fsdp")
    terms = term(meta, low_all, down, piece, slots, rank)
    terms, low_all = lax.optimization_barrier((terms, low_all))
    terms = exchange(terms, "fsdp")
    sent = spread(meta, *gradient(meta, parts, low_all, chips, slots, rank, v), bins)
    done = base(meta, cotangent, weight)
    sent, done = lax.optimization_barrier((sent, done))
    down_grad, up_grad = collect(meta, sent, own, v, slots, scale)
    terms, down_grad, up_grad = lax.optimization_barrier((terms, down_grad, up_grad))
    return join(done, terms), jnp.swapaxes(down_grad, 1, 2), up_grad


def solution(mesh):
    placed = (
        P(("dp", "fsdp"), None),
        P(("dp", "fsdp"), None),
        P("fsdp", None),
        P("dp", "fsdp", None),
        P("dp", None, "fsdp"),
        P(),
        P(),
        P(),
    )
    return jax.shard_map(
        local,
        mesh=mesh,
        in_specs=placed,
        out_specs=(P(("dp", "fsdp"), None), P("dp", "fsdp", None), P("dp", None, "fsdp")),
        check_vma=False,
    )
```

```python
import functools

import jax
import jax.numpy as jnp
from jax import lax
from jax.experimental import pallas as pl
from jax.experimental.pallas import tpu as pltpu
from jax.sharding import PartitionSpec as P

ADAPTER_SCALE = 2.0
BF = jnp.bfloat16
F32 = jnp.float32
VMEM_BYTES = 40 * 1024 * 1024
VMEM_MOST = 58 * 1024 * 1024
GROUP = 4
SIDE = 4
CORE, CHIP, PIECE, LIST = 0, 1, 2, 3


def call(kernel, name, flops=0, moved=0, vmem=VMEM_BYTES, **kw):
    return pl.pallas_call(
        kernel,
        compiler_params=pltpu.CompilerParams(vmem_limit_bytes=vmem),
        cost_estimate=pl.CostEstimate(flops=flops, bytes_accessed=moved, transcendentals=0),
        name=name,
        **kw,
    )


def whole(shape):
    return pl.BlockSpec(shape, lambda i, m: (0,) * len(shape))


def with_meta(grid, in_specs, out_specs, scratch=()):
    return pltpu.PrefetchScalarGridSpec(
        num_scalar_prefetch=1,
        grid=grid,
        in_specs=in_specs,
        out_specs=out_specs,
        scratch_shapes=list(scratch),
    )


def start_of(meta, s):
    return meta[LIST + s]


def end_of(meta, s, slots):
    return meta[LIST + slots + s]


def owner_of(meta, s, slots):
    return meta[LIST + 2 * slots + s]


def wanted_by(meta, b, slots):
    return meta[LIST + 3 * slots + b]


def segment_at(meta, owner, slots, bins):
    return meta[LIST + 3 * slots + bins + owner]


def inside_pair(meta, pair, first, shape, slots, rank):
    row = first + lax.broadcasted_iota(jnp.int32, shape, 0)
    low = lax.broadcasted_iota(jnp.int32, shape, 1) < rank
    begin = jnp.where(low, start_of(meta, 2 * pair), start_of(meta, 2 * pair + 1))
    end = jnp.where(low, end_of(meta, 2 * pair, slots), end_of(meta, 2 * pair + 1, slots))
    return (row >= begin) & (row < end)


def turn_kernel(at, w, out):
    both = jnp.transpose(w[...].astype(F32)).astype(BF)
    part = out.shape[0]
    low = lax.rem(at[0], 2) == 0
    out[...] = jnp.where(low, both[:part], both[part:])


def turn(at, w, slices):
    piece, width = w.shape
    part = width // slices
    return call(
        turn_kernel,
        "turn",
        moved=4 * part * piece,
        grid_spec=with_meta(
            (1,),
            [pl.BlockSpec((piece, 2 * part), lambda i, m: (0, m[0] // 2))],
            whole((part, piece)),
        ),
        out_shape=jax.ShapeDtypeStruct((part, piece), BF),
    )(at, w)


def pack_kernel(tok, cot_t, out):
    rows = tok.shape[0]
    n, _, piece = out.shape
    v = cot_t.shape[0] // n
    for f in range(n):
        out[f, :rows, :] = tok[:, f * piece:(f + 1) * piece]
        out[f, rows:, :rows] = cot_t[f * v:f * v + v // 2, :]
        out[f, rows:, rows:] = cot_t[f * v + v // 2:(f + 1) * v, :]


def pack(tokens, cot_t, n):
    rows, width = tokens.shape
    piece, v = width // n, cot_t.shape[0] // n
    tall = rows + v * rows // piece
    return call(
        pack_kernel,
        "pack",
        moved=4 * rows * width,
        vmem=VMEM_MOST,
        grid=(n // GROUP,),
        in_specs=[
            pl.BlockSpec((rows, GROUP * piece), lambda f: (0, f)),
            pl.BlockSpec((GROUP * v, rows), lambda f: (f, 0)),
        ],
        out_specs=pl.BlockSpec((GROUP, tall, piece), lambda f: (f, 0, 0)),
        out_shape=jax.ShapeDtypeStruct((n, tall, piece), BF),
    )(tokens, cot_t)


def offer_kernel(slots, meta, down_t, up, keep, give):
    piece, v = down_t.shape[2], up.shape[2]
    keep[...] = jnp.zeros_like(keep)
    give[...] = jnp.zeros_like(give)
    for z in range(keep.shape[0]):
        for out, core in ((keep, meta[CORE]), (give, 1 - meta[CORE])):
            r = jnp.maximum(wanted_by(meta, 2 * z + core, slots), 0)
            out[z, :, :piece] = down_t[r]
            out[z, :, piece:piece + v] = up[r]


def offer(meta, down_t, up, chips, slots):
    _, rank, piece = down_t.shape
    shape = (chips, rank, piece + 128)
    return call(
        functools.partial(offer_kernel, slots),
        "offer",
        moved=8 * chips * rank * piece,
        grid_spec=with_meta(
            (1,), [whole(down_t.shape), whole(up.shape)], [whole(shape), whole(shape)]
        ),
        out_shape=[jax.ShapeDtypeStruct(shape, BF)] * 2,
    )(meta, down_t, up)


def merge_kernel(meta, keep, taken, *outs):
    chips = len(outs)
    for k, out in enumerate(outs):
        z = lax.rem(meta[CHIP] + k, chips)
        out[meta[CORE]] = keep[z]
        out[1 - meta[CORE]] = taken[z]


def merge(meta, keep, taken):
    chips, rank, wide = keep.shape
    shape = (2, rank, wide)
    return call(
        merge_kernel,
        "merge",
        moved=4 * keep.size,
        grid_spec=with_meta(
            (1,), [whole(keep.shape), whole(taken.shape)], [whole(shape)] * chips
        ),
        out_shape=[jax.ShapeDtypeStruct(shape, BF)] * chips,
    )(meta, keep, taken)


def choose_kernel(slots, meta, *refs):
    chips = len(refs) - 3
    got, (down, turned, up) = refs[:chips], refs[chips:]
    piece, v, rank = down.shape[2], up.shape[0], down.shape[1]
    for k in range(chips):
        z = lax.rem(meta[CHIP] + chips - k, chips)
        for core in range(2):
            s = segment_at(meta, 2 * z + core, slots, 2 * chips)

            @pl.when(s >= 0)
            def _():
                down[s] = got[k][core]

    for p in range(slots // 2):
        pair = jnp.concatenate([down[2 * p], down[2 * p + 1]], axis=0).astype(F32)
        cols = slice(2 * rank * p, 2 * rank * (p + 1))
        turned[:, cols] = jnp.transpose(pair[:, :turned.shape[0]]).astype(BF)
        up[:, cols] = jnp.transpose(pair[:, turned.shape[0]:])[:v].astype(BF)


def choose(meta, got, slots, v):
    _, rank, wide = got[0].shape
    piece = wide - 128
    shapes = [(slots, rank, wide), (piece, slots * rank), (v, slots * rank)]
    return call(
        functools.partial(choose_kernel, slots),
        "choose",
        moved=4 * slots * rank * wide,
        grid_spec=with_meta((1,), [whole(g.shape) for g in got], [whole(s) for s in shapes]),
        out_shape=[jax.ShapeDtypeStruct(s, BF) for s in shapes],
    )(meta, *got)


def cot_of(part, rows):
    return jnp.concatenate([part[rows:, :rows], part[rows:, rows:]], axis=0)


def by_half(meta, first, rows, slots, body):
    cut = start_of(meta, slots // 2)
    low, high = first + rows <= cut, first >= cut
    pl.when(low)(lambda: body(range(slots // 4)))
    pl.when(high)(lambda: body(range(slots // 4, slots // 2)))
    pl.when(jnp.logical_not(low | high))(lambda: body(range(slots // 2)))


def project_kernel(slots, rank, meta, part, down_t, up_t, out):
    group, rows, _ = out.shape
    shape = (rows, 2 * rank)

    def block(g, first, pairs):
        cols = slice(2 * rank * pairs[0], 2 * rank * (pairs[-1] + 1))
        lr = jnp.dot(part[g, :rows, :], down_t[:, cols], preferred_element_type=F32)
        lg = lax.dot_general(
            cot_of(part[g], rows),
            up_t[:, cols],
            (((0,), (0,)), ((), ())),
            preferred_element_type=F32,
        )
        lr_sum = jnp.zeros(shape, F32)
        lg_sum = jnp.zeros(shape, F32)
        for k, p in enumerate(pairs):
            keep = inside_pair(meta, p, first, shape, slots, rank)
            at = slice(2 * rank * k, 2 * rank * (k + 1))
            lr_sum += jnp.where(keep, lr[:, at], 0.0)
            lg_sum += jnp.where(keep, lg[:, at], 0.0)
        lr_sum += pltpu.roll(lr_sum, rank, 1)
        lg_sum += pltpu.roll(lg_sum, rank, 1)
        low = lax.broadcasted_iota(jnp.int32, shape, 1) < rank
        out[g] = jnp.where(low, lr_sum, ADAPTER_SCALE * lg_sum).astype(BF)

    for g in range(group):
        first = (pl.program_id(0) * group + g) * rows
        by_half(meta, first, rows, slots, functools.partial(block, g, first))


def project(meta, parts, down_t, up_t, rows, slots, rank):
    n, tall, piece = parts.shape
    return call(
        functools.partial(project_kernel, slots, rank),
        "project",
        flops=2 * n * rows * piece * slots * rank,
        moved=2 * n * tall * piece,
        grid_spec=with_meta(
            (n // GROUP,),
            [
                pl.BlockSpec((GROUP, tall, piece), lambda j, m: (j, 0, 0)),
                whole(down_t.shape),
                whole(up_t.shape),
            ],
            pl.BlockSpec((GROUP, rows, 2 * rank), lambda j, m: (j, 0, 0)),
        ),
        out_shape=jax.ShapeDtypeStruct((n, rows, 2 * rank), BF),
    )(meta, parts, down_t, up_t)


def total_kernel(parts, copies):
    acc = parts[0].astype(F32)
    for f in range(1, parts.shape[0]):
        acc += parts[f].astype(F32)
    turned = jnp.transpose(acc).astype(BF)
    for f in range(copies.shape[0]):
        copies[f] = turned


def total(parts):
    n, rows, wide = parts.shape
    return call(
        total_kernel,
        "total",
        moved=4 * parts.size,
        out_shape=jax.ShapeDtypeStruct((n, wide, rows), BF),
    )(parts)


def gradient_kernel(slots, rank, v, meta, part, low, keep, give, acc_down, acc_up):
    group, _, rows = low.shape
    step = pl.program_id(0)

    @pl.when(step == 0)
    def _():
        acc_down[...] = jnp.zeros_like(acc_down)
        acc_up[...] = jnp.zeros_like(acc_up)

    for g in range(group):
        first = (step * group + g) * rows
        for s in range(slots):
            start, end = start_of(meta, s), end_of(meta, s, slots)

            @pl.when((start < first + rows) & (end > first))
            def _():
                token = first + lax.broadcasted_iota(jnp.int32, (2 * rank, rows), 1)
                both = low[g].astype(F32)
                both = jnp.where((token >= start) & (token < end), both, 0.0).astype(BF)
                at = slice(s * rank, (s + 1) * rank)
                acc_down[at, :] += jnp.dot(
                    both[rank:], part[g, :rows, :], preferred_element_type=F32
                )
                acc_up[at, :] += lax.dot_general(
                    both[:rank],
                    cot_of(part[g], rows),
                    (((1,), (1,)), ((), ())),
                    preferred_element_type=F32,
                )

    @pl.when(step == pl.num_programs(0) - 1)
    def _():
        piece = acc_down.shape[1]
        keep[...] = jnp.zeros_like(keep)
        give[...] = jnp.zeros_like(give)
        for s in range(slots):
            owner = owner_of(meta, s, slots)
            chip, same = owner // 2, lax.rem(owner, 2) == meta[CORE]
            rows_of = slice(s * rank, (s + 1) * rank)

            def put(out):
                out[chip, :, :piece] = acc_down[rows_of, :].astype(BF)
                out[chip, :, piece:piece + v] = (ADAPTER_SCALE * acc_up[rows_of, :]).astype(BF)

            pl.when(same)(functools.partial(put, keep))
            pl.when(jnp.logical_not(same))(functools.partial(put, give))


def gradient(meta, parts, low, chips, slots, rank, v):
    n, tall, piece = parts.shape
    rows = low.shape[2]
    shape = (chips, rank, piece + 128)
    return call(
        functools.partial(gradient_kernel, slots, rank, v),
        "gradient",
        flops=2 * n * rows * piece * slots * rank,
        moved=2 * n * tall * piece,
        grid_spec=with_meta(
            (n // GROUP,),
            [
                pl.BlockSpec((GROUP, tall, piece), lambda j, m: (j, 0, 0)),
                pl.BlockSpec((GROUP, 2 * rank, rows), lambda j, m: (j, 0, 0)),
            ],
            [whole(shape), whole(shape)],
            [pltpu.VMEM((slots * rank, piece), F32), pltpu.VMEM((slots * rank, v), F32)],
        ),
        out_shape=[jax.ShapeDtypeStruct(shape, BF)] * 2,
    )(meta, parts, low)


def collect_kernel(slots, scale, meta, *refs):
    got, (down, up) = refs[:-2], refs[-2:]
    chips = len(got)
    piece, v = down.shape[2], up.shape[2]
    down[...] = jnp.zeros_like(down)
    up[...] = jnp.zeros_like(up)
    for k in range(chips):
        z = lax.rem(meta[CHIP] + chips - k, chips)
        for core in range(2):
            r = wanted_by(meta, 2 * z + core, slots)

            @pl.when(r >= 0)
            def _():
                down[r] += got[k][core, :, :piece].astype(F32) * scale
                up[r] += got[k][core, :, piece:piece + v].astype(F32) * scale


def collect(meta, got, rows, v, slots, scale):
    _, rank, wide = got[0].shape
    shapes = [(rows, rank, wide - 128), (rows, rank, v)]
    return call(
        functools.partial(collect_kernel, slots, scale),
        "collect",
        moved=2 * len(got) * got[0].size,
        grid_spec=with_meta((1,), [whole(g.shape) for g in got], [whole(s) for s in shapes]),
        out_shape=[jax.ShapeDtypeStruct(s, F32) for s in shapes],
    )(meta, *got)


def term_kernel(slots, rank, meta, low, down, out):
    group, _, rows = low.shape
    piece = out.shape[2]

    def block(g, first, pairs):
        table = [down[2 * p + j, :, :piece] for p in pairs for j in range(2)]
        lg = low[g, rank:, :].astype(F32)
        lg = jnp.transpose(jnp.concatenate([lg, lg], axis=0))
        lg = [
            jnp.where(inside_pair(meta, p, first, lg.shape, slots, rank), lg, 0.0)
            for p in pairs
        ]
        lg = jnp.concatenate(lg, axis=1).astype(BF)
        table = jnp.concatenate(table, axis=0)
        out[g] = jnp.dot(lg, table, preferred_element_type=F32).astype(BF)

    for g in range(group):
        first = (pl.program_id(0) * group + g) * rows
        by_half(meta, first, rows, slots, functools.partial(block, g, first))


def term(meta, low, down, piece, slots, rank):
    n, wide, rows = low.shape
    return call(
        functools.partial(term_kernel, slots, rank),
        "term",
        flops=2 * n * rows * piece * slots * rank,
        moved=2 * n * rows * piece,
        vmem=VMEM_MOST,
        grid_spec=with_meta(
            (n // GROUP,),
            [pl.BlockSpec((GROUP, wide, rows), lambda j, m: (j, 0, 0)), whole(down.shape)],
            pl.BlockSpec((GROUP, rows, piece), lambda j, m: (j, 0, 0)),
        ),
        out_shape=jax.ShapeDtypeStruct((n, rows, piece), BF),
    )(meta, low, down)


def base_kernel(meta, cot, w, out):
    slices, group, _, piece = w.shape
    dx = lax.rem(pl.program_id(0) * group, SIDE)
    for g in range(group):
        x = lax.rem(lax.rem(meta[PIECE], SIDE) + SIDE - dx - g, SIDE)
        r = jnp.dot(
            cot[...],
            jnp.concatenate([w[e, g] for e in range(slices)], axis=0),
            preferred_element_type=F32,
        )
        out[:, pl.ds(pl.multiple_of(x * piece, piece), piece)] = r.astype(BF)


def base(meta, cot, w):
    slices, n, part, piece = w.shape
    rows, width = cot.shape
    group = SIDE // 2

    def place(f, m):
        return (0, lax.rem(m[PIECE] // SIDE + SIDE - f * group // SIDE, SIDE))

    return call(
        base_kernel,
        "base",
        flops=2 * rows * n * piece * width,
        moved=2 * n * piece * (width + rows),
        vmem=VMEM_MOST,
        grid_spec=with_meta(
            (n // group,),
            [
                whole(cot.shape),
                pl.BlockSpec((slices, group, part, piece), lambda f, m: (0, f, 0, 0)),
            ],
            pl.BlockSpec((rows, SIDE * piece), place),
        ),
        out_shape=jax.ShapeDtypeStruct((rows, n * piece), BF),
    )(meta, cot, w)


def join_kernel(done, terms, out):
    group, _, piece = terms.shape
    for g in range(group):
        cols = slice(g * piece, (g + 1) * piece)
        out[:, cols] = (done[:, cols].astype(F32) + terms[g].astype(F32)).astype(BF)


def join(done, terms):
    n, rows, piece = terms.shape
    return call(
        join_kernel,
        "join",
        moved=6 * n * rows * piece,
        vmem=VMEM_MOST,
        grid=(n // GROUP,),
        in_specs=[
            pl.BlockSpec((rows, GROUP * piece), lambda f: (0, f)),
            pl.BlockSpec((GROUP, rows, piece), lambda f: (f, 0, 0)),
        ],
        out_specs=pl.BlockSpec((rows, GROUP * piece), lambda f: (0, f)),
        out_shape=jax.ShapeDtypeStruct((rows, n * piece), BF),
    )(done, terms)


def exchange(x, axis):
    return lax.all_to_all(x, axis, 0, 0, tiled=True)


def swap(x, bins):
    return lax.ppermute(x, "dp", [(i, i ^ 1) for i in range(bins)])


def shift(x, k, bins):
    chips = bins // 2
    return lax.ppermute(
        x, "dp", [(i, (i // 2 + k) % chips * 2 + i % 2) for i in range(bins)]
    )


def spread(meta, keep, give, bins):
    blocks = merge(meta, keep, swap(give, bins))
    return [blocks[0]] + [shift(blocks[k], k, bins) for k in range(1, bins // 2)]


def across(x, dy, dx, n):
    return lax.ppermute(
        x,
        "fsdp",
        [
            (i, (i // SIDE + dy) % SIDE * SIDE + (i % SIDE + dx) % SIDE)
            for i in range(n)
        ],
    )


def scalars(segment_tenant, segment_lengths, tenant_stored_row, own):
    bins, slots = segment_tenant.shape
    me = lax.axis_index("dp")
    tenants = jnp.arange(tenant_stored_row.shape[0], dtype=jnp.int32)
    stored = jnp.sum(
        jnp.where(segment_tenant[:, :, None] == tenants, tenant_stored_row, 0), axis=2
    )
    owners = lax.dynamic_index_in_dim(stored, me, 0, keepdims=False) // own
    lengths = lax.dynamic_index_in_dim(segment_lengths, me, 0, keepdims=False)
    place = jnp.arange(slots, dtype=jnp.int32)
    starts = jnp.sum(jnp.where(place[None, :] < place[:, None], lengths[None, :], 0), axis=1)
    wanted = jnp.max(jnp.where(stored // own == me, stored % own, -1), axis=1)
    every = jnp.arange(bins, dtype=jnp.int32)
    segment = jnp.max(jnp.where(owners[None, :] == every[:, None], place[None, :], -1), axis=1)
    head = jnp.stack([me % 2, me // 2, lax.axis_index("fsdp")])
    return jnp.concatenate([head, starts, starts + lengths, owners, wanted, segment]).astype(
        jnp.int32
    )


def local(
    tokens,
    cotangent,
    value_weight,
    adapter_down_weight,
    adapter_up_weight,
    segment_tenant,
    segment_lengths,
    tenant_stored_row,
):
    own, piece, rank = adapter_down_weight.shape
    v = adapter_up_weight.shape[2]
    bins, slots = segment_tenant.shape
    chips = bins // 2
    rows = tokens.shape[0]
    n = lax.axis_size("fsdp")
    scale = (n * rows) ** (-0.5)
    meta = scalars(segment_tenant, segment_lengths, tenant_stored_row, own)

    me = lax.axis_index("dp").astype(jnp.int32).reshape(1)
    mine = turn(me, value_weight, bins)[None]
    near = [across(mine, 0, k, n) for k in range(1, SIDE)]
    mine = jnp.concatenate([mine] + near)
    near = [across(mine, k, 0, n) for k in range(1, SIDE)]
    packed = pack(tokens, jnp.swapaxes(cotangent, 0, 1), n)
    keep, give = offer(
        meta, jnp.swapaxes(adapter_down_weight, 1, 2), adapter_up_weight, chips, slots
    )
    packed, keep, give, near, mine = lax.optimization_barrier((packed, keep, give, near, mine))
    weight = lax.all_gather(jnp.concatenate([mine] + near), "dp", axis=0)

    parts = exchange(packed, "fsdp")
    got = spread(meta, keep, give, bins)
    down, down_t, up_t = choose(meta, got, slots, v)
    parts, down, down_t, up_t = lax.optimization_barrier((parts, down, down_t, up_t))

    sums = exchange(project(meta, parts, down_t, up_t, rows, slots, rank), "fsdp")
    low_all = exchange(total(sums), "fsdp")
    terms = term(meta, low_all, down, piece, slots, rank)
    terms, low_all = lax.optimization_barrier((terms, low_all))
    terms = exchange(terms, "fsdp")
    sent = spread(meta, *gradient(meta, parts, low_all, chips, slots, rank, v), bins)
    done = base(meta, cotangent, weight)
    sent, done = lax.optimization_barrier((sent, done))
    down_grad, up_grad = collect(meta, sent, own, v, slots, scale)
    terms, down_grad, up_grad = lax.optimization_barrier((terms, down_grad, up_grad))
    return join(done, terms), jnp.swapaxes(down_grad, 1, 2), up_grad


def solution(mesh):
    placed = (
        P(("dp", "fsdp"), None),
        P(("dp", "fsdp"), None),
        P("fsdp", None),
        P("dp", "fsdp", None),
        P("dp", None, "fsdp"),
        P(),
        P(),
        P(),
    )
    return jax.shard_map(
        local,
        mesh=mesh,
        in_specs=placed,
        out_specs=(P(("dp", "fsdp"), None), P("dp", "fsdp", None), P("dp", None, "fsdp")),
        check_vma=False,
    )
```

```python
import functools

import jax
import jax.numpy as jnp
from jax import lax
from jax.experimental import pallas as pl
from jax.experimental.pallas import tpu as pltpu
from jax.sharding import PartitionSpec as P

ADAPTER_SCALE = 2.0
BF = jnp.bfloat16
F32 = jnp.float32
VMEM_BYTES = 40 * 1024 * 1024
VMEM_MOST = 58 * 1024 * 1024
GROUP = 4
SIDE = 4
CORE, CHIP, PIECE, LIST = 0, 1, 2, 3


def call(kernel, name, flops=0, moved=0, vmem=VMEM_BYTES, **kw):
    return pl.pallas_call(
        kernel,
        compiler_params=pltpu.CompilerParams(vmem_limit_bytes=vmem),
        cost_estimate=pl.CostEstimate(flops=flops, bytes_accessed=moved, transcendentals=0),
        name=name,
        **kw,
    )


def whole(shape):
    return pl.BlockSpec(shape, lambda i, m: (0,) * len(shape))


def with_meta(grid, in_specs, out_specs, scratch=()):
    return pltpu.PrefetchScalarGridSpec(
        num_scalar_prefetch=1,
        grid=grid,
        in_specs=in_specs,
        out_specs=out_specs,
        scratch_shapes=list(scratch),
    )


def start_of(meta, s):
    return meta[LIST + s]


def end_of(meta, s, slots):
    return meta[LIST + slots + s]


def owner_of(meta, s, slots):
    return meta[LIST + 2 * slots + s]


def wanted_by(meta, b, slots):
    return meta[LIST + 3 * slots + b]


def segment_at(meta, owner, slots, bins):
    return meta[LIST + 3 * slots + bins + owner]


def inside_pair(meta, pair, first, shape, slots, rank):
    row = first + lax.broadcasted_iota(jnp.int32, shape, 0)
    low = lax.broadcasted_iota(jnp.int32, shape, 1) < rank
    begin = jnp.where(low, start_of(meta, 2 * pair), start_of(meta, 2 * pair + 1))
    end = jnp.where(low, end_of(meta, 2 * pair, slots), end_of(meta, 2 * pair + 1, slots))
    return (row >= begin) & (row < end)


def turn_kernel(at, w, out):
    both = jnp.transpose(w[...].astype(F32)).astype(BF)
    part = out.shape[0]
    low = lax.rem(at[0], 2) == 0
    out[...] = jnp.where(low, both[:part], both[part:])


def turn(at, w, slices):
    piece, width = w.shape
    part = width // slices
    return call(
        turn_kernel,
        "turn",
        moved=4 * part * piece,
        grid_spec=with_meta(
            (1,),
            [pl.BlockSpec((piece, 2 * part), lambda i, m: (0, m[0] // 2))],
            whole((part, piece)),
        ),
        out_shape=jax.ShapeDtypeStruct((part, piece), BF),
    )(at, w)


def pack_kernel(tok, cot, out):
    rows = tok.shape[0]
    group, _, piece = out.shape
    v = cot.shape[1] // group
    cot_t = jnp.transpose(cot[...].astype(F32)).astype(BF)
    for f in range(group):
        out[f, :rows, :] = tok[:, f * piece:(f + 1) * piece]
        out[f, rows:, :rows] = cot_t[f * v:f * v + v // 2, :]
        out[f, rows:, rows:] = cot_t[f * v + v // 2:(f + 1) * v, :]


def pack(tokens, cot, n):
    rows, width = tokens.shape
    piece, v = width // n, cot.shape[1] // n
    tall = rows + v * rows // piece
    return call(
        pack_kernel,
        "pack",
        moved=4 * rows * width,
        vmem=VMEM_MOST,
        grid=(n // GROUP,),
        in_specs=[
            pl.BlockSpec((rows, GROUP * piece), lambda f: (0, f)),
            pl.BlockSpec((rows, GROUP * v), lambda f: (0, f)),
        ],
        out_specs=pl.BlockSpec((GROUP, tall, piece), lambda f: (f, 0, 0)),
        out_shape=jax.ShapeDtypeStruct((n, tall, piece), BF),
    )(tokens, cot)


def offer_kernel(slots, meta, down_t, up, keep, give):
    piece, v = down_t.shape[2], up.shape[2]
    keep[...] = jnp.zeros_like(keep)
    give[...] = jnp.zeros_like(give)
    for z in range(keep.shape[0]):
        for out, core in ((keep, meta[CORE]), (give, 1 - meta[CORE])):
            r = jnp.maximum(wanted_by(meta, 2 * z + core, slots), 0)
            out[z, :, :piece] = down_t[r]
            out[z, :, piece:piece + v] = up[r]


def offer(meta, down_t, up, chips, slots):
    _, rank, piece = down_t.shape
    shape = (chips, rank, piece + 128)
    return call(
        functools.partial(offer_kernel, slots),
        "offer",
        moved=8 * chips * rank * piece,
        grid_spec=with_meta(
            (1,), [whole(down_t.shape), whole(up.shape)], [whole(shape), whole(shape)]
        ),
        out_shape=[jax.ShapeDtypeStruct(shape, BF)] * 2,
    )(meta, down_t, up)


def merge_kernel(meta, keep, taken, *outs):
    chips = len(outs)
    for k, out in enumerate(outs):
        z = lax.rem(meta[CHIP] + k, chips)
        out[meta[CORE]] = keep[z]
        out[1 - meta[CORE]] = taken[z]


def merge(meta, keep, taken):
    chips, rank, wide = keep.shape
    shape = (2, rank, wide)
    return call(
        merge_kernel,
        "merge",
        moved=4 * keep.size,
        grid_spec=with_meta(
            (1,), [whole(keep.shape), whole(taken.shape)], [whole(shape)] * chips
        ),
        out_shape=[jax.ShapeDtypeStruct(shape, BF)] * chips,
    )(meta, keep, taken)


def choose_kernel(slots, meta, *refs):
    chips = len(refs) - 3
    got, (down, turned, up) = refs[:chips], refs[chips:]
    piece, v, rank = down.shape[2], up.shape[0], down.shape[1]
    for k in range(chips):
        z = lax.rem(meta[CHIP] + chips - k, chips)
        for core in range(2):
            s = segment_at(meta, 2 * z + core, slots, 2 * chips)

            @pl.when(s >= 0)
            def _():
                down[s] = got[k][core]

    for p in range(slots // 2):
        pair = jnp.concatenate([down[2 * p], down[2 * p + 1]], axis=0).astype(F32)
        cols = slice(2 * rank * p, 2 * rank * (p + 1))
        turned[:, cols] = jnp.transpose(pair[:, :turned.shape[0]]).astype(BF)
        up[:, cols] = jnp.transpose(pair[:, turned.shape[0]:])[:v].astype(BF)


def choose(meta, got, slots, v):
    _, rank, wide = got[0].shape
    piece = wide - 128
    shapes = [(slots, rank, wide), (piece, slots * rank), (v, slots * rank)]
    return call(
        functools.partial(choose_kernel, slots),
        "choose",
        moved=4 * slots * rank * wide,
        grid_spec=with_meta((1,), [whole(g.shape) for g in got], [whole(s) for s in shapes]),
        out_shape=[jax.ShapeDtypeStruct(s, BF) for s in shapes],
    )(meta, *got)


def cot_of(part, rows):
    return jnp.concatenate([part[rows:, :rows], part[rows:, rows:]], axis=0)


def project_kernel(slots, rank, meta, part, down_t, up_t, out):
    group, rows, _ = out.shape
    shape = (rows, 2 * rank)
    low = lax.broadcasted_iota(jnp.int32, shape, 1) < rank
    for g in range(group):
        first = (pl.program_id(0) * group + g) * rows
        block = part[g]
        lr = jnp.dot(block[:rows], down_t[...], preferred_element_type=F32)
        lg = lax.dot_general(
            cot_of(block, rows), up_t[...], (((0,), (0,)), ((), ())), preferred_element_type=F32
        )
        lr_sum = jnp.zeros(shape, F32)
        lg_sum = jnp.zeros(shape, F32)
        for p in range(slots // 2):
            keep = inside_pair(meta, p, first, shape, slots, rank)
            cols = slice(2 * rank * p, 2 * rank * (p + 1))
            lr_sum += jnp.where(keep, lr[:, cols], 0.0)
            lg_sum += jnp.where(keep, lg[:, cols], 0.0)
        lr_sum += pltpu.roll(lr_sum, rank, 1)
        lg_sum += pltpu.roll(lg_sum, rank, 1)
        out[g] = jnp.where(low, lr_sum, ADAPTER_SCALE * lg_sum).astype(BF)


def project(meta, parts, down_t, up_t, rows, slots, rank):
    n, tall, piece = parts.shape
    return call(
        functools.partial(project_kernel, slots, rank),
        "project",
        flops=2 * n * rows * piece * slots * rank,
        moved=2 * n * tall * piece,
        grid_spec=with_meta(
            (n // GROUP,),
            [
                pl.BlockSpec((GROUP, tall, piece), lambda j, m: (j, 0, 0)),
                whole(down_t.shape),
                whole(up_t.shape),
            ],
            pl.BlockSpec((GROUP, rows, 2 * rank), lambda j, m: (j, 0, 0)),
        ),
        out_shape=jax.ShapeDtypeStruct((n, rows, 2 * rank), BF),
    )(meta, parts, down_t, up_t)


def total_kernel(parts, copies):
    acc = parts[0].astype(F32)
    for f in range(1, parts.shape[0]):
        acc += parts[f].astype(F32)
    turned = jnp.transpose(acc).astype(BF)
    for f in range(copies.shape[0]):
        copies[f] = turned


def total(parts):
    n, rows, wide = parts.shape
    return call(
        total_kernel,
        "total",
        moved=4 * parts.size,
        out_shape=jax.ShapeDtypeStruct((n, wide, rows), BF),
    )(parts)


def gradient_kernel(slots, rank, v, meta, part, low, keep, give, acc_down, acc_up):
    group, _, rows = low.shape
    step = pl.program_id(0)

    @pl.when(step == 0)
    def _():
        acc_down[...] = jnp.zeros_like(acc_down)
        acc_up[...] = jnp.zeros_like(acc_up)

    for g in range(group):
        first = (step * group + g) * rows
        for s in range(slots):
            start, end = start_of(meta, s), end_of(meta, s, slots)

            @pl.when((start < first + rows) & (end > first))
            def _():
                token = first + lax.broadcasted_iota(jnp.int32, (2 * rank, rows), 1)
                both = low[g].astype(F32)
                both = jnp.where((token >= start) & (token < end), both, 0.0).astype(BF)
                at = slice(s * rank, (s + 1) * rank)
                acc_down[at, :] += jnp.dot(
                    both[rank:], part[g, :rows, :], preferred_element_type=F32
                )
                acc_up[at, :] += lax.dot_general(
                    both[:rank],
                    cot_of(part[g], rows),
                    (((1,), (1,)), ((), ())),
                    preferred_element_type=F32,
                )

    @pl.when(step == pl.num_programs(0) - 1)
    def _():
        piece = acc_down.shape[1]
        keep[...] = jnp.zeros_like(keep)
        give[...] = jnp.zeros_like(give)
        for s in range(slots):
            owner = owner_of(meta, s, slots)
            chip, same = owner // 2, lax.rem(owner, 2) == meta[CORE]
            rows_of = slice(s * rank, (s + 1) * rank)

            def put(out):
                out[chip, :, :piece] = acc_down[rows_of, :].astype(BF)
                out[chip, :, piece:piece + v] = (ADAPTER_SCALE * acc_up[rows_of, :]).astype(BF)

            pl.when(same)(functools.partial(put, keep))
            pl.when(jnp.logical_not(same))(functools.partial(put, give))


def gradient(meta, parts, low, chips, slots, rank, v):
    n, tall, piece = parts.shape
    rows = low.shape[2]
    shape = (chips, rank, piece + 128)
    return call(
        functools.partial(gradient_kernel, slots, rank, v),
        "gradient",
        flops=2 * n * rows * piece * slots * rank,
        moved=2 * n * tall * piece,
        grid_spec=with_meta(
            (n // GROUP,),
            [
                pl.BlockSpec((GROUP, tall, piece), lambda j, m: (j, 0, 0)),
                pl.BlockSpec((GROUP, 2 * rank, rows), lambda j, m: (j, 0, 0)),
            ],
            [whole(shape), whole(shape)],
            [pltpu.VMEM((slots * rank, piece), F32), pltpu.VMEM((slots * rank, v), F32)],
        ),
        out_shape=[jax.ShapeDtypeStruct(shape, BF)] * 2,
    )(meta, parts, low)


def collect_kernel(slots, scale, meta, *refs):
    got, (down, up) = refs[:-2], refs[-2:]
    chips = len(got)
    piece, v = down.shape[2], up.shape[2]
    down[...] = jnp.zeros_like(down)
    up[...] = jnp.zeros_like(up)
    for k in range(chips):
        z = lax.rem(meta[CHIP] + chips - k, chips)
        for core in range(2):
            r = wanted_by(meta, 2 * z + core, slots)

            @pl.when(r >= 0)
            def _():
                down[r] += got[k][core, :, :piece].astype(F32) * scale
                up[r] += got[k][core, :, piece:piece + v].astype(F32) * scale


def collect(meta, got, rows, v, slots, scale):
    _, rank, wide = got[0].shape
    shapes = [(rows, rank, wide - 128), (rows, rank, v)]
    return call(
        functools.partial(collect_kernel, slots, scale),
        "collect",
        moved=2 * len(got) * got[0].size,
        grid_spec=with_meta((1,), [whole(g.shape) for g in got], [whole(s) for s in shapes]),
        out_shape=[jax.ShapeDtypeStruct(s, F32) for s in shapes],
    )(meta, *got)


def term_kernel(slots, rank, meta, low, down, out):
    group, _, rows = low.shape
    piece = out.shape[2]
    table = jnp.concatenate([down[s, :, :piece] for s in range(slots)], axis=0)
    for g in range(group):
        first = (pl.program_id(0) * group + g) * rows
        lg = low[g, rank:, :].astype(F32)
        lg = jnp.transpose(jnp.concatenate([lg, lg], axis=0))
        lg = [
            jnp.where(inside_pair(meta, p, first, lg.shape, slots, rank), lg, 0.0)
            for p in range(slots // 2)
        ]
        lg = jnp.concatenate(lg, axis=1).astype(BF)
        out[g] = jnp.dot(lg, table, preferred_element_type=F32).astype(BF)


def term(meta, low, down, piece, slots, rank):
    n, wide, rows = low.shape
    return call(
        functools.partial(term_kernel, slots, rank),
        "term",
        flops=2 * n * rows * piece * slots * rank,
        moved=2 * n * rows * piece,
        vmem=VMEM_MOST,
        grid_spec=with_meta(
            (n // GROUP,),
            [pl.BlockSpec((GROUP, wide, rows), lambda j, m: (j, 0, 0)), whole(down.shape)],
            pl.BlockSpec((GROUP, rows, piece), lambda j, m: (j, 0, 0)),
        ),
        out_shape=jax.ShapeDtypeStruct((n, rows, piece), BF),
    )(meta, low, down)


def base_kernel(meta, cot, w, out):
    slices, group, _, piece = w.shape
    dx = lax.rem(pl.program_id(0) * group, SIDE)
    for g in range(group):
        x = lax.rem(lax.rem(meta[PIECE], SIDE) + SIDE - dx - g, SIDE)
        r = jnp.dot(
            cot[...],
            jnp.concatenate([w[e, g] for e in range(slices)], axis=0),
            preferred_element_type=F32,
        )
        out[:, pl.ds(pl.multiple_of(x * piece, piece), piece)] = r.astype(BF)


def base(meta, cot, w):
    slices, n, part, piece = w.shape
    rows, width = cot.shape
    group = SIDE // 2

    def place(f, m):
        return (0, lax.rem(m[PIECE] // SIDE + SIDE - f * group // SIDE, SIDE))

    return call(
        base_kernel,
        "base",
        flops=2 * rows * n * piece * width,
        moved=2 * n * piece * (width + rows),
        vmem=VMEM_MOST,
        grid_spec=with_meta(
            (n // group,),
            [
                whole(cot.shape),
                pl.BlockSpec((slices, group, part, piece), lambda f, m: (0, f, 0, 0)),
            ],
            pl.BlockSpec((rows, SIDE * piece), place),
        ),
        out_shape=jax.ShapeDtypeStruct((rows, n * piece), BF),
    )(meta, cot, w)


def join_kernel(done, terms, out):
    group, _, piece = terms.shape
    for g in range(group):
        cols = slice(g * piece, (g + 1) * piece)
        out[:, cols] = (done[:, cols].astype(F32) + terms[g].astype(F32)).astype(BF)


def join(done, terms):
    n, rows, piece = terms.shape
    return call(
        join_kernel,
        "join",
        moved=6 * n * rows * piece,
        vmem=VMEM_MOST,
        grid=(n // GROUP,),
        in_specs=[
            pl.BlockSpec((rows, GROUP * piece), lambda f: (0, f)),
            pl.BlockSpec((GROUP, rows, piece), lambda f: (f, 0, 0)),
        ],
        out_specs=pl.BlockSpec((rows, GROUP * piece), lambda f: (0, f)),
        out_shape=jax.ShapeDtypeStruct((rows, n * piece), BF),
    )(done, terms)


def exchange(x, axis):
    return lax.all_to_all(x, axis, 0, 0, tiled=True)


def swap(x, bins):
    return lax.ppermute(x, "dp", [(i, i ^ 1) for i in range(bins)])


def shift(x, k, bins):
    chips = bins // 2
    return lax.ppermute(
        x, "dp", [(i, (i // 2 + k) % chips * 2 + i % 2) for i in range(bins)]
    )


def spread(meta, keep, give, bins):
    blocks = merge(meta, keep, swap(give, bins))
    return [blocks[0]] + [shift(blocks[k], k, bins) for k in range(1, bins // 2)]


def across(x, dy, dx, n):
    return lax.ppermute(
        x,
        "fsdp",
        [
            (i, (i // SIDE + dy) % SIDE * SIDE + (i % SIDE + dx) % SIDE)
            for i in range(n)
        ],
    )


def scalars(segment_tenant, segment_lengths, tenant_stored_row, own):
    bins, slots = segment_tenant.shape
    me = lax.axis_index("dp")
    tenants = jnp.arange(tenant_stored_row.shape[0], dtype=jnp.int32)
    stored = jnp.sum(
        jnp.where(segment_tenant[:, :, None] == tenants, tenant_stored_row, 0), axis=2
    )
    owners = lax.dynamic_index_in_dim(stored, me, 0, keepdims=False) // own
    lengths = lax.dynamic_index_in_dim(segment_lengths, me, 0, keepdims=False)
    place = jnp.arange(slots, dtype=jnp.int32)
    starts = jnp.sum(jnp.where(place[None, :] < place[:, None], lengths[None, :], 0), axis=1)
    wanted = jnp.max(jnp.where(stored // own == me, stored % own, -1), axis=1)
    every = jnp.arange(bins, dtype=jnp.int32)
    segment = jnp.max(jnp.where(owners[None, :] == every[:, None], place[None, :], -1), axis=1)
    head = jnp.stack([me % 2, me // 2, lax.axis_index("fsdp")])
    return jnp.concatenate([head, starts, starts + lengths, owners, wanted, segment]).astype(
        jnp.int32
    )


def local(
    tokens,
    cotangent,
    value_weight,
    adapter_down_weight,
    adapter_up_weight,
    segment_tenant,
    segment_lengths,
    tenant_stored_row,
):
    own, piece, rank = adapter_down_weight.shape
    v = adapter_up_weight.shape[2]
    bins, slots = segment_tenant.shape
    chips = bins // 2
    rows = tokens.shape[0]
    n = lax.axis_size("fsdp")
    scale = (n * rows) ** (-0.5)
    meta = scalars(segment_tenant, segment_lengths, tenant_stored_row, own)

    me = lax.axis_index("dp").astype(jnp.int32).reshape(1)
    mine = turn(me, value_weight, bins)[None]
    near = [across(mine, 0, k, n) for k in range(1, SIDE)]
    mine = jnp.concatenate([mine] + near)
    below, above = across(mine, 1, 0, n), across(mine, SIDE - 1, 0, n)
    half = SIDE // 2
    near = [
        below,
        across(below[:half], 1, 0, n),
        across(above[half:], SIDE - 1, 0, n),
        above,
    ]
    packed = pack(tokens, cotangent, n)
    packed, near, mine = lax.optimization_barrier((packed, near, mine))
    weight = lax.all_gather(jnp.concatenate([mine] + near), "dp", axis=0)

    keep, give = offer(
        meta, jnp.swapaxes(adapter_down_weight, 1, 2), adapter_up_weight, chips, slots
    )
    parts = exchange(packed, "fsdp")
    got = spread(meta, keep, give, bins)
    down, down_t, up_t = choose(meta, got, slots, v)
    parts, down, down_t, up_t = lax.optimization_barrier((parts, down, down_t, up_t))

    sums = exchange(project(meta, parts, down_t, up_t, rows, slots, rank), "fsdp")
    low_all = exchange(total(sums), "fsdp")
    terms = term(meta, low_all, down, piece, slots, rank)
    terms, low_all = lax.optimization_barrier((terms, low_all))
    terms = exchange(terms, "fsdp")
    sent = spread(meta, *gradient(meta, parts, low_all, chips, slots, rank, v), bins)
    done = base(meta, cotangent, weight)
    sent, done = lax.optimization_barrier((sent, done))
    down_grad, up_grad = collect(meta, sent, own, v, slots, scale)
    terms, down_grad, up_grad = lax.optimization_barrier((terms, down_grad, up_grad))
    return join(done, terms), jnp.swapaxes(down_grad, 1, 2), up_grad


def solution(mesh):
    placed = (
        P(("dp", "fsdp"), None),
        P(("dp", "fsdp"), None),
        P("fsdp", None),
        P("dp", "fsdp", None),
        P("dp", None, "fsdp"),
        P(),
        P(),
        P(),
    )
    return jax.shard_map(
        local,
        mesh=mesh,
        in_specs=placed,
        out_specs=(P(("dp", "fsdp"), None), P("dp", "fsdp", None), P("dp", None, "fsdp")),
        check_vma=False,
    )
```
